512 devices in a mesh: theta: 16 (over x, y), rad: 32 (over z, core).
Axes of the slice: x: 4, y: 4, z: 16, core: 2. Of those that a mesh axis runs over, the one named last changes fastest.
Arguments:
- pressure_source: float32 [8, 1024, 4096], P(None, 'rad', 'theta'), may hold values from -15 to 15
- conductance: float32 [8, 1024, 4096], P(None, 'rad', 'theta'), may hold values from 0.3 to 3
- slide: int32 [1], replicated, may hold values from 2048 to 2303
- slide_fraction: float32 [1], replicated, may hold values from 0.1 to 0.9
- interface_gain: float32 [1], replicated, may hold values from 0.5 to 4
Outputs:
- pressure: float32 [8, 1024, 4096], P(None, 'rad', 'theta')
- residual: float32 [8, 1024, 4096], P(None, 'rad', 'theta')
The draws below stay inside these ranges and needn't reach their ends.
All inputs are finite; a program needn't handle non-finite values.
Results may differ from the reference program's by a relative error of at most 0.0003.
Values sent between devices are 32-bit elements; how exact they have to be, the bound alone decides.
A program may use at most 64 MiB of HBM per device.

```python
import math
import jax
import jax.numpy as jnp

NZ = 8
CT = 256
LEVELS = 5
COARSE_SWEEPS = 4
NR = 1024
NT = 4096


def block_scale(own_key, extent, pieces, low, top_value):
    gain = 1.0
    for dim, shards_of in pieces:
        steps = jax.random.uniform(jax.random.fold_in(jax.random.fold_in(own_key, 6), dim), (shards_of,), jnp.float32, low / len(pieces), top_value / len(pieces))
        gain = gain * jnp.repeat(jnp.exp(steps), extent[dim] // shards_of).reshape((-1,) + (1,) * (len(extent) - 1 - dim))
    return gain


def noise(own_key, dims, deviation, limit, split=(), held_as=jnp.bfloat16):
    array = jax.random.normal(own_key, dims, jnp.float32) * deviation
    if len(split) > 0:
        array = block_scale(own_key, dims, split, -0.22, 0.18) * array
    return jnp.clip(array, min=-limit, max=limit).astype(held_as)


def setup_inputs(seed: int = 0) -> dict:
    arg_keys = jax.random.split(jax.random.key(seed), 6)
    return {
        "pressure_source": noise(arg_keys[0], (NZ, NR, NT), 3.0, 15.0, ((1, 32), (2, 16)), jnp.float32),
        "conductance": jnp.clip(jnp.exp(math.log(3.0) - 2.3025851 * jax.random.uniform(arg_keys[1], (NZ, NR, NT), jnp.float32) ** block_scale(arg_keys[1], (NZ, NR, NT), ((1, 32), (2, 16)), -0.2, 0.2)), 0.3, 3.0),
        "slide": jax.random.randint(arg_keys[2], (1,), NT // 2, NT // 2 + CT).astype(jnp.int32),
        "slide_fraction": jnp.clip(jax.random.uniform(arg_keys[3], (1,), jnp.float32, 0.1, 0.9), 0.1, 0.9),
        "interface_gain": jnp.clip(jnp.exp(jax.random.uniform(arg_keys[4], (1,), jnp.float32, math.log(0.5), math.log(4.0))), 0.5, 4.0),
    }


relaxation = 0.8


def coarsen(values):
    shape = values.shape
    return values.reshape(shape[0], shape[1] // 2, 2, shape[2] // 2, 2).sum(axis=(2, 4))


def prolong(values):
    return jnp.repeat(jnp.repeat(values, 2, axis=1), 2, axis=2)


def wrap_pad(values):
    beside_all = jnp.concatenate([values[:, :, -1:], values, values[:, :, :1]], axis=2)
    return jnp.pad(beside_all, ((0, 0), (1, 1), (0, 0)))


def face_coefs(conduct_pad, row_index, rows_level, gain_value, upper_mask, lower_mask):
    conduct = conduct_pad[:, 1:-1, 1:-1]
    position = row_index.astype(jnp.float32)
    radius_cell = (1.0 + (position + 0.5) / rows_level)[None, :, None]
    radius_upper = (1.0 + (position + 1.0) / rows_level)[None, :, None]
    radius_lower = (1.0 + position / rows_level)[None, :, None]
    upper_plain = 0.5 * (conduct + conduct_pad[:, 2:, 1:-1]) * radius_upper
    lower_plain = 0.5 * (conduct + conduct_pad[:, :-2, 1:-1]) * radius_lower
    upper_coef = jnp.where(upper_mask[None, :, None], gain_value * upper_plain, upper_plain)
    lower_coef = jnp.where(lower_mask[None, :, None], gain_value * lower_plain, lower_plain)
    east_coef = 0.5 * (conduct + conduct_pad[:, 1:-1, 2:]) / radius_cell
    west_coef = 0.5 * (conduct + conduct_pad[:, 1:-1, :-2]) / radius_cell
    axial_coef = 0.5 * (conduct[1:] + conduct[:-1]) * radius_cell
    diagonal = upper_coef + lower_coef + east_coef + west_coef
    diagonal = diagonal + jnp.pad(axial_coef, ((0, 1), (0, 0), (0, 0))) + jnp.pad(axial_coef, ((1, 0), (0, 0), (0, 0)))
    return (upper_coef, lower_coef, east_coef, west_coef, axial_coef, diagonal)


def remap(stator_row, rotor_row, slide_cells, fraction):
    rotor_side = (1.0 - fraction) * jnp.roll(stator_row, -slide_cells, axis=1) + fraction * jnp.roll(stator_row, -slide_cells - 1, axis=1)
    stator_side = (1.0 - fraction) * jnp.roll(rotor_row, slide_cells, axis=1) + fraction * jnp.roll(rotor_row, slide_cells + 1, axis=1)
    return rotor_side, stator_side


def apply_operator(field_pad, coeffs, rotor_side, stator_side, upper_mask, lower_mask):
    upper_coef, lower_coef, east_coef, west_coef, axial_coef, diagonal = coeffs
    field = field_pad[:, 1:-1, 1:-1]
    upper_values = jnp.where(upper_mask[None, :, None], rotor_side[:, None, :], field_pad[:, 2:, 1:-1])
    lower_values = jnp.where(lower_mask[None, :, None], stator_side[:, None, :], field_pad[:, :-2, 1:-1])
    axial_flux = axial_coef * (field[1:] - field[:-1])
    axial_term = jnp.pad(axial_flux, ((1, 0), (0, 0), (0, 0))) - jnp.pad(axial_flux, ((0, 1), (0, 0), (0, 0)))
    result = upper_coef * (field - upper_values) + lower_coef * (field - lower_values)
    result = result + east_coef * (field - field_pad[:, 1:-1, 2:]) + west_coef * (field - field_pad[:, 1:-1, :-2])
    return result + axial_term


def global_operator(conduct, gain_value, cells):
    rows_level = conduct.shape[1]
    row_index = jnp.arange(rows_level, dtype=jnp.int32)
    upper_mask = row_index == rows_level // 2 - 1
    lower_mask = row_index == rows_level // 2
    coeffs = face_coefs(wrap_pad(conduct), row_index, rows_level, gain_value, upper_mask, lower_mask)
    return (coeffs, upper_mask, lower_mask, cells)


def global_apply(field, operator, fraction):
    coeffs, upper_mask, lower_mask, cells = operator
    middle = field.shape[1] // 2
    rotor_side, stator_side = remap(field[:, middle, :], field[:, middle - 1, :], cells, fraction)
    return apply_operator(wrap_pad(field), coeffs, rotor_side, stator_side, upper_mask, lower_mask)


def reference(pressure_source, conductance, slide, slide_fraction, interface_gain):
    slide_cells = slide[0]
    fraction = slide_fraction[0]
    gain_value = interface_gain[0]
    conducts = [conductance]
    for level_index in range(1, LEVELS):
        conducts.append(0.25 * coarsen(conducts[-1]))
    operators = [global_operator(conducts[level_index], gain_value, slide_cells // (2 ** level_index)) for level_index in range(LEVELS)]

    def vcycle(level_index, source):
        operator = operators[level_index]
        diagonal = operator[0][5]
        field = relaxation * source / diagonal
        if level_index == LEVELS - 1:
            for sweep_index in range(COARSE_SWEEPS - 1):
                field = field + relaxation * (source - global_apply(field, operator, fraction)) / diagonal
            return field
        remainder = source - global_apply(field, operator, fraction)
        field = field + prolong(vcycle(level_index + 1, coarsen(remainder)))
        return field + relaxation * (source - global_apply(field, operator, fraction)) / diagonal

    pressure = vcycle(0, pressure_source)
    residual = pressure_source - global_apply(pressure, operators[0], fraction)
    return pressure, residual
```

```python
import functools

import jax
import jax.numpy as jnp
from jax import lax
from jax.experimental import pallas as pl
from jax.experimental.pallas import tpu as pltpu
from jax.sharding import PartitionSpec as P

MESH = pl.DeviceIdType.MESH
F32 = jnp.float32
NT, NR = 16, 32
HALF = NR // 2
ROWS = 32
GLOBAL_ROWS = NR * ROWS
LANES = 384
LO, GLU, GOD, OWN, GOU, GHD, HI, PHYS = 0, 12, 16, 20, 52, 56, 60, 72
REACH = 3
SEGS = 2 * REACH + 1
SLOTS = 4
NORMAL = {0: 0, 1: 1, 3: -1}
FROM_STATOR = (8, 9, 10, 7)
FROM_ROTOR = (-8, -7, -10, -9)
PER_LEVEL = ("K", "B", "U", "CU", "CL", "CE", "CW", "CZ", "CD", "WD", "E")


def roll(x, shift, axis):
    size = x.shape[axis]
    shift = shift % size
    return x if shift == 0 else pltpu.roll(x, shift, axis)


def tile_row(j, half):
    return (j // 8) * 16 + half * 8 + j % 8


def to_tiles(x):
    nz, rows, columns = x.shape
    x = x.reshape(nz, rows // 8, 8, columns // 128, 128)
    return x.transpose(0, 1, 3, 2, 4).reshape(nz * rows * columns // 128, 128)


def from_tiles(x, shape):
    nz, rows, columns = shape
    x = x.reshape(nz, rows // 8, columns // 128, 8, 128)
    return x.transpose(0, 1, 3, 2, 4).reshape(shape)


def loop_rows(low, high, body, unroll):
    count = (high - low) // unroll

    def step(i, carry):
        for q in range(unroll):
            body(low + i * unroll + q)
        return carry

    if count:
        lax.fori_loop(0, count, step, 0)
    for j in range(low + count * unroll, high):
        body(j)


def kernel(*refs):
    slide_ref, frac_ref, gain_ref, b_ref, k_ref, p_ref, res_ref = refs[:7]
    at = 7
    levels = []
    for _ in range(3):
        levels.append(dict(zip(PER_LEVEL, refs[at : at + len(PER_LEVEL)])))
        at += len(PER_LEVEL)
    (DG, B3S, EP, RT, RC_HI, RC_LO, RG, RGH, WC1, WC2, PK, PB, RN, RX, RB, VP, E3S) = refs[at : at + 17]
    sem_s, sem_r = refs[at + 17 :]

    t = lax.axis_index("theta")
    r = lax.axis_index("rad")
    side = r // HALF
    is_rot = r == HALF - 1
    is_sta = r == HALF
    is_if = is_rot | is_sta
    near = (r >= HALF - REACH) & (r < HALF + REACH)
    slide = slide_ref[0]
    frac = frac_ref[0]
    gain = gain_ref[0]

    def theta(offset):
        return lax.rem(t + offset + 2 * NT, NT)

    lane = lax.broadcasted_iota(jnp.int32, (8, 128), 1)
    lane3 = lax.broadcasted_iota(jnp.int32, (8, LANES), 1)
    axial = lax.broadcasted_iota(jnp.int32, (8, 128), 0)
    K0, B0 = levels[0]["K"], levels[0]["B"]

    zeros3 = jnp.zeros((12, 8, LANES), F32)

    @pl.when(r == 0)
    def _():
        K0[pl.ds(LO, 12)] = zeros3
        B0[pl.ds(LO, 12)] = zeros3

    @pl.when(r == NR - 1)
    def _():
        K0[pl.ds(HI, 12)] = zeros3
        B0[pl.ds(HI, 12)] = zeros3

    RC_LO[...] = jnp.zeros_like(RC_LO)
    RC_HI[...] = jnp.zeros_like(RC_HI)
    RN[...] = jnp.ones_like(RN)
    RX[...] = jnp.ones_like(RX)
    RB[...] = jnp.zeros_like(RB)

    barrier = pltpu.get_barrier_semaphore()
    peers = []
    for dr in range(-REACH, REACH + 1):
        inside = (r + dr >= 0) & (r + dr < NR)
        for dt in (-1, 0, 1):
            if dr or dt:
                peers.append((inside, dt, dr))
        if dr:
            crossing = near & inside & ((r + dr) // HALF != side)
            for o in range(7, 11):
                peers.append((crossing, (1 - 2 * side) * o, dr))
        if dr in (1, 2):
            for o in range(7, 11):
                peers.append((r + dr == HALF - 1, o, dr))
                peers.append((r == HALF, o, dr))
        if dr in (-1, -2):
            for o in range(7, 11):
                peers.append((r == HALF - 1, -o, dr))
                peers.append((r + dr == HALF, -o, dr))
    for o in range(6, 11):
        peers.append((is_if, o, 0))
    for cond, dt, dr in peers:
        peer = (theta(dt), r + dr)

        @pl.when(cond)
        def _(peer=peer):
            pl.semaphore_signal(barrier, inc=1, device_id=peer, device_id_type=MESH)

    for src, dst in ((k_ref, K0), (b_ref, B0)):

        def move(j, src=src, dst=dst):
            for half in range(2):
                dst[OWN + j, :, pl.ds(128 * half, 128)] = src[pl.ds(tile_row(j, half), 8, stride=2 * ROWS), :]

        loop_rows(0, ROWS, move, 8)

    for m in range(4):
        for arr, ref in enumerate((K0, B0)):
            left = right = None
            for q in range(8):
                row = OWN + 8 * m + q
                low = roll(ref[row, :, pl.ds(0, 128)], 16 * q, 1)
                high = roll(ref[row, :, pl.ds(128, 128)], 16 * q + 16, 1)
                here = lane // 16 == q
                left = low if q == 0 else jnp.where(here, low, left)
                right = high if q == 0 else jnp.where(here, high, right)
            EP[0, m, arr] = left
            EP[1, m, arr] = right

    pl.semaphore_wait(barrier, sum(cond.astype(jnp.int32) for cond, _, _ in peers))

    messages = []

    def message(index, send, recv, src, dst, target, start=True):
        copy = pltpu.make_async_remote_copy(
            src_ref=src,
            dst_ref=dst,
            send_sem=sem_s.at[index],
            recv_sem=sem_r.at[index],
            device_id=target,
            device_id_type=MESH,
        )
        if start:
            pl.when(send)(copy.start)
        messages.append((send, copy))
        return lambda: pl.when(recv)(copy.wait_recv)

    always = r >= 0
    down_s, down_r = (r >= 1) & (r != HALF), (r < NR - 1) & (r != HALF - 1)
    up_s, up_r = down_r, down_s
    wide = pl.ds(0, 256)
    w_th = [
        message(0, always, always, EP.at[0], RT.at[0], (theta(-1), r)),
        message(1, always, always, EP.at[1], RT.at[1], (theta(1), r)),
    ]
    w_k = [
        message(2, down_s, down_r, K0.at[pl.ds(OWN, 12), :, wide], K0.at[pl.ds(HI, 12), :, wide], (t, r - 1)),
        message(3, up_s, up_r, K0.at[pl.ds(OWN + 20, 12), :, wide], K0.at[pl.ds(LO, 12), :, wide], (t, r + 1)),
        message(4, down_s, down_r, EP.at[0, pl.ds(0, 2)], RC_HI.at[0], (theta(-1), r - 1)),
        message(5, down_s, down_r, EP.at[1, pl.ds(0, 2)], RC_HI.at[1], (theta(1), r - 1)),
        message(6, up_s, up_r, EP.at[0, pl.ds(2, 2)], RC_LO.at[0], (theta(-1), r + 1)),
        message(7, up_s, up_r, EP.at[1, pl.ds(2, 2)], RC_LO.at[1], (theta(1), r + 1)),
    ]
    w_b = [
        message(8, down_s, down_r, B0.at[pl.ds(OWN, 12), :, wide], B0.at[pl.ds(HI, 12), :, wide], (t, r - 1)),
        message(9, up_s, up_r, B0.at[pl.ds(OWN + 20, 12), :, wide], B0.at[pl.ds(LO, 12), :, wide], (t, r + 1)),
    ]
    w_i = []

    sgn = 1 - 2 * side
    th = {o: theta(o) for o in (-1, 1, 8)}
    th_far = {"g2": theta(-9 * sgn), "ge": theta(-10 + 17 * side), "gw": theta(-7 + 17 * side), "c2": theta(9 * sgn)}

    facing = OWN + 20 * (1 - side)
    facing4 = OWN + 28 * (1 - side)
    group4 = 3 * (1 - side)
    other = NR - 1 - r
    ghost = GOD + (GOU - GOD) * side
    own4 = K0.at[pl.ds(facing4, 4), :, wide]
    items = [
        (own4, K0.at[pl.ds(ghost, 4), :, wide], (t, other)),
        (EP.at[0, group4, 0], RG.at[0], (th[-1], other)),
        (EP.at[1, group4, 0], RG.at[1], (th[1], other)),
        (own4, WC1.at[pl.ds(24, 4)], (th[8], r)),
        (own4, WC2.at[pl.ds(24, 4)], (th_far["g2"], r)),
        (EP.at[0, group4, 0], RGH.at[0], (th_far["ge"], r)),
        (EP.at[1, group4, 0], RGH.at[1], (th_far["gw"], r)),
        (K0.at[pl.ds(facing, 12), :, wide], WC1.at[pl.ds(0, 12)], (th[8], other)),
        (K0.at[pl.ds(facing, 12), :, wide], WC2.at[pl.ds(0, 12)], (th_far["c2"], other)),
        (B0.at[pl.ds(facing, 12), :, wide], WC1.at[pl.ds(12, 12)], (th[8], other)),
        (B0.at[pl.ds(facing, 12), :, wide], WC2.at[pl.ds(12, 12)], (th_far["c2"], other)),
    ]
    for n, (src, dst, target) in enumerate(items):
        w_i.append(message(10 + n, is_if, is_if, src, dst, target))

    cross_corners = []
    for part, (cond, dst, first) in enumerate(((is_sta, RC_HI, 0), (is_rot, RC_LO, 2))):
        other = r - 1 if part == 0 else r + 1
        offs = (-10, -7) if part == 0 else (7, 10)
        got = is_rot if part == 0 else is_sta
        for e in range(2):
            cross_corners.append(
                message(
                    (4 if part == 0 else 6) + e,
                    cond,
                    got,
                    EP.at[e, pl.ds(first, 2)],
                    dst.at[e],
                    (theta(offs[e]), other),
                )
            )

    def pairs(x, cell):
        width = x.shape[-1]
        pick = (lax.broadcasted_iota(jnp.int32, x.shape, x.ndim - 1) // cell) % 2 == 1
        return x + jnp.where(pick, roll(x, cell, x.ndim - 1), roll(x, width - cell, x.ndim - 1))

    gather_index = (lane % 16) * 8

    def pack(rows):
        out = None
        for q, x in enumerate(rows):
            for half in range(2):
                part = jnp.take_along_axis(x[:, 128 * half : 128 * half + 128], gather_index, axis=1)
                out = part if out is None else jnp.where(lane // 16 == 2 * q + half, part, out)
        return out

    own3 = []
    for j in range(4):
        k2 = []
        for i in range(2):
            k1 = []
            for h in range(2):
                row = OWN + 8 * j + 4 * i + 2 * h
                k1.append(0.25 * pairs(K0[row, :, wide] + K0[row + 1, :, wide], 1))
            k2.append(0.25 * pairs(k1[0] + k1[1], 2))
        own3.append(0.25 * pairs(k2[0] + k2[1], 4))
    PK[...] = pack(own3)

    base_n, base_x, base_b = 21, 21 + SEGS * SLOTS, 21 + 2 * SEGS * SLOTS
    w_n, w_x = [], []
    for dr in range(-REACH, REACH + 1):
        inside_s = (r + dr >= 0) & (r + dr < NR)
        inside_r = (r - dr >= 0) & (r - dr < NR)
        seg = REACH - dr
        for slot, off in NORMAL.items():
            if dr or off:
                w_n.append(
                    message(
                        base_n + seg * SLOTS + slot, inside_s, inside_r, PK, RN.at[seg, slot], (theta(-off), r + dr)
                    )
                )
        to, fro = r + dr, r - dr
        to_rot = (to < HALF) & (to >= HALF - REACH) & (r >= HALF - 1)
        to_sta = (to >= HALF) & (to < HALF + REACH) & (r <= HALF)
        got = ((r < HALF) & (r >= HALF - REACH) & (fro >= HALF - 1)) | (
            (r >= HALF) & (r < HALF + REACH) & (fro <= HALF)
        )
        to_side = (r + dr) // HALF
        for slot in range(SLOTS):
            off = -FROM_STATOR[slot] + to_side * (FROM_STATOR[slot] - FROM_ROTOR[slot])
            w_x.append(
                message(
                    base_x + seg * SLOTS + slot, to_rot | to_sta, got, PK, RX.at[seg, slot], (theta(off), r + dr)
                )
            )
    RN[REACH, 0] = PK[...]

    def third(left_pack, right_pack, q):
        return jnp.where(lane < 64, roll(left_pack, -16 * q, 1), roll(right_pack, 112 - 16 * q, 1))

    halo = pl.ds(256, 128)
    for w in w_th:
        w()
    for m in range(4):
        for arr, ref in enumerate((K0, B0)):
            for q in range(8):
                ref[OWN + 8 * m + q, :, halo] = third(RT[0, m, arr], RT[1, m, arr], q)
    for w in w_k:
        w()
    for w in cross_corners:
        w()
    for w in w_b:
        w()
    for j in range(12):
        for arr, ref in enumerate((K0, B0)):
            m, q = divmod(j, 8)
            ref[HI + j, :, halo] = third(RC_HI[0, m, arr], RC_HI[1, m, arr], q)
            m, q = divmod(4 + j, 8)
            ref[LO + j, :, halo] = third(RC_LO[0, m, arr], RC_LO[1, m, arr], q)

    fine = slide - NT * 256 // 2
    d4 = (fine // 4) * 4
    q4 = d4 % 128
    far = d4 >= 128
    back4 = lax.rem(128 - q4, 128)

    for w in w_i:
        w()

    def window(tiles, sign):
        if sign > 0:
            tiles = [jnp.where(far, tiles[(i + 1) % 5], tiles[i]) for i in range(5)]
            turned = [pltpu.roll(x, back4, 1) for x in tiles]
            keep = lane < 128 - q4
            out = [jnp.where(keep, turned[i], turned[(i + 1) % 5]) for i in (0, 1, 2, 4)]
        else:
            tiles = [jnp.where(far, tiles[(i + 4) % 5], tiles[i]) for i in range(5)]
            turned = [pltpu.roll(x, q4, 1) for x in tiles]
            keep = lane >= q4
            out = [jnp.where(keep, turned[i], turned[(i + 4) % 5]) for i in (0, 1, 2, 4)]
        return out[0], out[1], jnp.where(lane < 64, out[2], out[3])

    def fill(sign, dst_k, dst_ghost):
        for j in range(28):
            if j < 24:
                ref, row = ((K0, B0)[j // 12], dst_k + j % 12)
                edge = ref[row, :, halo]
            else:
                ref, row = (K0, dst_ghost + j - 24)
                edge = third(RGH[0], RGH[1], j - 24 + (4 if sign > 0 else 0))
            a = [WC1[j, :, pl.ds(0, 128)], WC1[j, :, pl.ds(128, 128)]]
            b = [WC2[j, :, pl.ds(0, 128)], WC2[j, :, pl.ds(128, 128)]]
            tiles = a + b + [edge] if sign > 0 else a + [edge] + b
            for i, x in enumerate(window(tiles, sign)):
                ref[row, :, pl.ds(128 * i, 128)] = x

    @pl.when(is_rot)
    def _():
        fill(1, HI, GHD)
        for j in range(4):
            K0[GOU + j, :, halo] = third(RG[0], RG[1], j)

    @pl.when(is_sta)
    def _():
        fill(-1, LO, GLU)
        for j in range(4):
            K0[GOD + j, :, halo] = third(RG[0], RG[1], 4 + j)

    @pl.when(jnp.logical_not(is_rot))
    def _():
        K0[pl.ds(GOU, 4)] = K0[pl.ds(HI, 4)]
        K0[pl.ds(GHD, 4)] = K0[pl.ds(OWN + 28, 4)]

    @pl.when(jnp.logical_not(is_sta))
    def _():
        K0[pl.ds(GLU, 4)] = K0[pl.ds(OWN, 4)]
        K0[pl.ds(GOD, 4)] = K0[pl.ds(LO + 8, 4)]

    for level in (1, 2):
        fine_k, coarse_k = levels[level - 1]["K"], levels[level]["K"]

        def down_k(j, fine_k=fine_k, coarse_k=coarse_k, cell=1 << (level - 1)):
            coarse_k[j] = 0.25 * pairs(fine_k[2 * j] + fine_k[2 * j + 1], cell)

        loop_rows(0, PHYS >> level, down_k, 4)

    top = axial < 7
    low_ok, high_ok = r > 0, r < NR - 1

    def coefficients(level, seg, low, high):
        A = levels[level]
        rows_level = GLOBAL_ROWS >> level
        inv = 1.0 / rows_level
        cell = 1 << level
        start = {"lo": LO + 12, "own": OWN, "hi": HI - 32}[seg] >> level
        ok = {"lo": low_ok, "own": None, "hi": high_ok}[seg]

        def body(j):
            pos = r * (ROWS >> level) + j - start
            posf = pos.astype(F32)
            hu = 0.5 * (1.0 + (posf + 1.0) * inv) * jnp.where(pos == rows_level // 2 - 1, gain, 1.0)
            hl = 0.5 * (1.0 + posf * inv) * jnp.where(pos == rows_level // 2, gain, 1.0)
            rc = 1.0 + (posf + 0.5) * inv
            hc1 = 0.5 / jnp.full((8, 128), rc, F32)
            hz1 = jnp.where(top, 0.5 * rc, 0.0)
            hc = jnp.concatenate([hc1] * 3, axis=1)
            hz = jnp.concatenate([hz1] * 3, axis=1)
            k = A["K"][j]
            ce = (k + roll(k, -cell, 1)) * hc
            cw = roll(ce, cell, 1)
            cu = (k + A["K"][j + 1]) * hu
            cl = (k + A["K"][j - 1]) * hl
            cz = (k + roll(k, -1, 0)) * hz
            cd = roll(cz, 1, 0)
            diag = cu + cl + ce + cw + cz + cd
            wd = 0.8 / diag
            if ok is not None:
                wd = jnp.where(ok, wd, 0.0)
            A["CU"][j], A["CL"][j], A["CE"][j], A["CW"][j], A["CZ"][j], A["CD"][j] = cu, cl, ce, cw, cz, cd
            A["WD"][j] = wd
            if level == 0:
                A["U"][j] = wd * A["B"][j]
                if seg == "own":
                    DG[j - OWN] = diag

        loop_rows(low, high, body, 2)

    def spans(level, halo_rows):
        lo, own, hi = LO + 12 >> level, OWN >> level, HI >> level
        out = [("own", own, own + (ROWS >> level))]
        if halo_rows:
            out = [("lo", lo - halo_rows, lo)] + out + [("hi", hi, hi + halo_rows)]
        return out

    for level, halo_rows in ((0, 11), (1, 5), (2, 2)):
        for seg, low, high in spans(level, halo_rows):
            coefficients(level, seg, low, high)

    def weights(active, shift, count):
        out = []
        for i in range(count):
            w = jnp.where(shift == i, 1.0 - frac, 0.0) + jnp.where(shift == i - 1, frac, 0.0)
            out.append(jnp.where(active, w, 1.0 if i == 0 else 0.0))
        return out

    shifts = (fine % 4, (fine // 2) % 2, 0 * fine)
    up_w = [weights(is_rot, shifts[level], (5, 3, 2)[level]) for level in range(3)]
    low_w = [weights(is_sta, shifts[level], (5, 3, 2)[level]) for level in range(3)]

    def mix(x, w, step):
        out = w[0] * x
        for i in range(1, len(w)):
            out = out + w[i] * roll(x, i * step, x.ndim - 1)
        return out

    def ghosts(field, level):
        cell = 1 << level
        lo_end, own, own_end, hi = LO + 12 >> level, OWN >> level, GOU >> level, HI >> level
        field[own_end] = mix(field[hi], up_w[level], -cell)
        field[hi - 1] = mix(field[own_end - 1], up_w[level], cell)
        field[lo_end] = mix(field[own], low_w[level], -cell)
        field[own - 1] = mix(field[lo_end - 1], low_w[level], cell)

    def neighbours(level, field, j):
        A = levels[level]
        cell = 1 << level
        v = field[j]
        return (
            A["CU"][j] * field[j + 1]
            + A["CL"][j] * field[j - 1]
            + A["CE"][j] * roll(v, -cell, 1)
            + A["CW"][j] * roll(v, cell, 1)
            + A["CZ"][j] * roll(v, -1, 0)
            + A["CD"][j] * roll(v, 1, 0)
        )

    for level in range(3):
        A = levels[level]
        if level:

            def first(j, A=A):
                A["U"][j] = A["WD"][j] * A["B"][j]

            for seg, low, high in spans(level, (11, 5, 2)[level]):
                loop_rows(low, high, first, 2)
        ghosts(A["U"], level)

        def restrict(j, A=A, level=level):
            x = 0.2 * (A["B"][2 * j] + A["B"][2 * j + 1])
            x = x + (neighbours(level, A["U"], 2 * j) + neighbours(level, A["U"], 2 * j + 1))
            x = pairs(x, 1 << level)
            if level < 2:
                levels[level + 1]["B"][j] = x
            else:
                B3S[j - (OWN >> 3 if OWN % 8 == 0 else 0)] = x

        if level < 2:
            for seg, low, high in spans(level + 1, (5, 2)[level]):
                loop_rows(low, high, restrict, 1)
        else:
            for j in range(4):
                x = None
                for i in range(2):
                    row = (OWN >> 2) + 2 * j + i
                    y = 0.2 * A["B"][row] + neighbours(2, A["U"], row)
                    x = y if x is None else x + y
                B3S[j] = pairs(x, 4)

    PB[...] = pack([B3S[j, :, wide] for j in range(4)])
    RB[REACH, 0] = PB[...]
    w_p = []
    for dr in range(-REACH, REACH + 1):
        inside_s = (r + dr >= 0) & (r + dr < NR)
        inside_r = (r - dr >= 0) & (r - dr < NR)
        seg = REACH - dr
        same_s = (r + dr) // HALF == side
        same_r = (r - dr) // HALF == side
        to_side = (r + dr) // HALF
        for slot in range(SLOTS):
            index = base_b + seg * SLOTS + slot
            if slot in NORMAL and (dr or slot):
                w_p.append(
                    message(
                        index, inside_s & same_s, inside_r & same_r, PB, RB.at[seg, slot], (theta(-NORMAL[slot]), r + dr)
                    )
                )
            if dr:
                off = -FROM_STATOR[slot] + to_side * (FROM_STATOR[slot] - FROM_ROTOR[slot])
                w_p.append(
                    message(
                        index,
                        inside_s & jnp.logical_not(same_s),
                        inside_r & jnp.logical_not(same_r),
                        PB,
                        RB.at[seg, slot],
                        (theta(off), r + dr),
                    )
                )

    count3 = 4 * SEGS
    d3 = (fine // 16) * 2
    sgn_x = jnp.where(side == 0, lax.rem(128 - d3, 128), d3)

    def unpack(ref):
        tiles = [ref[:, o] for o in range(SLOTS)]
        lane7 = lax.broadcasted_iota(jnp.int32, (SEGS, 8, 128), 2) // 32
        rows = []
        for q in range(4):
            out = roll(tiles[0], -32 * q, 2)
            for o in range(1, SLOTS):
                out = jnp.where(lane7 == o, roll(tiles[o], 32 * (o - q), 2), out)
            rows.append(out)
        return jnp.stack(rows, axis=1).reshape(count3, 8, 128)

    def turn(x):
        return pltpu.roll(x, sgn_x, 2)

    for w in w_n + w_x:
        w()
    kn = unpack(RN)
    kx = turn(unpack(RX))

    far_off = jnp.where(near, side, 1 << 20)

    def coefficients_patch(kn, kx, rows, level, cell):
        rows_level = GLOBAL_ROWS >> level
        inv = 1.0 / rows_level
        pos = (r - REACH) * (ROWS >> level) + lax.broadcasted_iota(jnp.int32, (rows, 8, 128), 0)
        ok = (pos >= 0) & (pos < rows_level)
        beyond = (pos - rows_level // 2) * (1 - 2 * side) >= far_off
        posf = pos.astype(F32)
        hu = 0.5 * (1.0 + (posf + 1.0) * inv) * jnp.where(pos == rows_level // 2 - 1, gain, 1.0)
        hl = 0.5 * (1.0 + posf * inv) * jnp.where(pos == rows_level // 2, gain, 1.0)
        rc = 1.0 + (posf + 0.5) * inv
        hc = 0.5 / rc
        hz = jnp.where(lax.broadcasted_iota(jnp.int32, (rows, 8, 128), 1) < 7, 0.5 * rc, 0.0)
        k = jnp.where(beyond, kx, kn)
        ku = jnp.where(beyond, jnp.concatenate([kx[1:], kx[:1]], 0), jnp.concatenate([kn[1:], kn[:1]], 0))
        kd = jnp.where(beyond, jnp.concatenate([kx[-1:], kx[:-1]], 0), jnp.concatenate([kn[-1:], kn[:-1]], 0))
        ku = jnp.where(pos == rows_level - 1, 0.0, ku)
        kd = jnp.where(pos == 0, 0.0, kd)
        ce = (k + roll(k, -cell, 2)) * hc
        cw = roll(ce, cell, 2)
        cu = (k + ku) * hu
        cl = (k + kd) * hl
        cz = (k + roll(k, -1, 1)) * hz
        cd = roll(cz, 1, 1)
        wd = jnp.where(ok, 0.8 / (cu + cl + ce + cw + cz + cd), 0.0)
        return (cu, cl, ce, cw, cz, cd, wd, beyond)

    def coarse_k(x):
        y = x.reshape(x.shape[0] // 2, 2, 8, 128)
        return 0.25 * pairs(y[:, 0] + y[:, 1], 1)

    C3 = coefficients_patch(kn, kx, count3, 3, 1)
    C4 = coefficients_patch(coarse_k(kn), coarse_k(kx), count3 // 2, 4, 2)

    odd = (fine // 8) % 2
    w3 = weights(r >= 0, odd, 3)
    w4 = weights(r >= 0, 0 * odd, 2)

    def neighbours_patch(C, v, step, w, cell):
        n = v.shape[0]
        edge = lax.rem(HALF - r + REACH + 4 * SEGS, SEGS) * step
        VP[pl.ds(0, n)] = v
        over = mix(VP[edge], w, -cell)
        under = mix(VP[lax.rem(edge + n - 1, n)], w, cell)
        row = lax.broadcasted_iota(jnp.int32, v.shape, 0)
        vu = jnp.concatenate([v[1:], v[:1]], 0)
        vd = jnp.concatenate([v[-1:], v[:-1]], 0)
        mark = jnp.where(near, edge, -8)
        vu = jnp.where(row == mark - 1, over[None], vu)
        vd = jnp.where(row == mark, under[None], vd)
        return (
            C[0] * vu
            + C[1] * vd
            + C[2] * roll(v, -cell, 2)
            + C[3] * roll(v, cell, 2)
            + C[4] * roll(v, -1, 1)
            + C[5] * roll(v, 1, 1)
        )

    for w in w_p:
        w()
    b3 = unpack(RB)
    b3 = jnp.where(C3[7], turn(b3), b3)
    u3 = C3[6] * b3
    x = 0.2 * b3 + neighbours_patch(C3, u3, 4, w3, 1)
    x = x.reshape(count3 // 2, 2, 8, 128)
    b4 = pairs(x[:, 0] + x[:, 1], 1)
    v4 = C4[6] * b4
    for _ in range(3):
        v4 = 0.2 * v4 + C4[6] * (b4 + neighbours_patch(C4, v4, 2, w4, 2))
    up4 = jnp.broadcast_to(v4[:, None], (count3 // 2, 2, 8, 128)).reshape(count3, 8, 128)
    v3 = u3 + up4
    e3 = 0.2 * v3 + C3[6] * (b3 + neighbours_patch(C3, v3, 4, w3, 1))

    delta = (fine // 4) % 4 * 4
    first_row = 4 * REACH - 1
    for j in range(6):
        if j == 0:
            shift = jnp.where(is_sta, -delta, 0)
        elif j == 5:
            shift = jnp.where(is_rot, delta, 0)
        else:
            shift = 0
        for i in range(3):
            signed = lane + 128 * i
            if i == 2:
                signed = jnp.where(lane < 64, signed, signed - LANES)
            index = ((signed + shift + 1024) // 8) % 128
            E3S[j, :, pl.ds(128 * i, 128)] = jnp.take_along_axis(e3[first_row + j], index, axis=1)

    for level in (2, 1, 0):
        A = levels[level]
        low, own, hi = LO + 12 >> level, OWN >> level, HI >> level
        rows = ROWS >> level
        if level == 2:
            A["U"][low - 2] = A["U"][low - 2] + E3S[0]
            A["U"][low - 1] = A["U"][low - 1] + E3S[0]
            for j in range(rows):
                A["U"][own + j] = A["U"][own + j] + E3S[1 + j // 2]
            A["U"][hi] = A["U"][hi] + E3S[5]
            A["U"][hi + 1] = A["U"][hi + 1] + E3S[5]
        else:
            E = levels[level + 1]["E"]

            def add(j, A=A, E=E):
                e = E[j]
                A["U"][2 * j] = A["U"][2 * j] + e
                A["U"][2 * j + 1] = A["U"][2 * j + 1] + e

            add((low >> 1) - 1)
            loop_rows(own >> 1, (own + rows) >> 1, add, 4)
            add(hi >> 1)
        ghosts(A["U"], level)

        def smooth(j, A=A, level=level):
            A["E"][j] = 0.2 * A["U"][j] + A["WD"][j] * (A["B"][j] + neighbours(level, A["U"], j))

        smooth(low - 1)
        loop_rows(own, own + rows, smooth, 2)
        smooth(hi)

    ghosts(levels[0]["E"], 0)

    def finish(j):
        E = levels[0]["E"]
        p = E[OWN + j]
        out = B0[OWN + j] - DG[j] * p + neighbours(0, E, OWN + j)
        for half in range(2):
            place = pl.ds(tile_row(j, half), 8, stride=2 * ROWS)
            p_ref[place, :] = p[:, 128 * half : 128 * half + 128]
            res_ref[place, :] = out[:, 128 * half : 128 * half + 128]

    loop_rows(0, ROWS, finish, 2)

    for send, copy in messages:
        pl.when(send)(copy.wait_send)


def on_device(source, conductance, slide, fraction, gain):
    nz, rows, columns = source.shape
    scratch = []
    for level in range(3):
        scratch += [pltpu.VMEM((PHYS >> level, nz, LANES), F32)] * len(PER_LEVEL)
    tile = (8, 128)
    scratch += [
        pltpu.VMEM((ROWS, nz, LANES), F32),
        pltpu.VMEM((4, nz, LANES), F32),
        pltpu.VMEM((2, 4, 2) + tile, F32),
        pltpu.VMEM((2, 4, 2) + tile, F32),
        pltpu.VMEM((2, 2, 2) + tile, F32),
        pltpu.VMEM((2, 2, 2) + tile, F32),
        pltpu.VMEM((2,) + tile, F32),
        pltpu.VMEM((2,) + tile, F32),
        pltpu.VMEM((28, nz, 256), F32),
        pltpu.VMEM((28, nz, 256), F32),
        pltpu.VMEM(tile, F32),
        pltpu.VMEM(tile, F32),
        pltpu.VMEM((SEGS, SLOTS) + tile, F32),
        pltpu.VMEM((SEGS, SLOTS) + tile, F32),
        pltpu.VMEM((SEGS, SLOTS) + tile, F32),
        pltpu.VMEM((4 * SEGS,) + tile, F32),
        pltpu.VMEM((6, nz, LANES), F32),
    ]
    sems = 21 + 3 * SEGS * SLOTS
    scratch += [pltpu.SemaphoreType.DMA((sems,)), pltpu.SemaphoreType.DMA((sems,))]
    smem = pl.BlockSpec(memory_space=pltpu.SMEM)
    vmem = pl.BlockSpec(memory_space=pltpu.VMEM)
    flat = jax.ShapeDtypeStruct((nz * rows * columns // 128, 128), F32)
    pressure, residual = pl.pallas_call(
        kernel,
        out_shape=(flat, flat),
        in_specs=[smem, smem, smem, vmem, vmem],
        out_specs=(vmem, vmem),
        scratch_shapes=scratch,
        compiler_params=pltpu.CompilerParams(
            collective_id=0, has_side_effects=True, vmem_limit_bytes=48 * 1024 * 1024
        ),
    )(slide, fraction, gain, to_tiles(source), to_tiles(conductance))
    return from_tiles(pressure, source.shape), from_tiles(residual, source.shape)


def solution(mesh):
    spec = P(None, "rad", "theta")
    return jax.shard_map(
        on_device, mesh=mesh, in_specs=(spec, spec, P(), P(), P()), out_specs=(spec, spec), check_vma=False
    )
```

```python
import functools

import jax
import jax.numpy as jnp
from jax import lax
from jax.experimental import pallas as pl
from jax.experimental.pallas import tpu as pltpu
from jax.sharding import PartitionSpec as P

MESH = pl.DeviceIdType.MESH
F32 = jnp.float32
NT, NR = 16, 32
HALF = NR // 2
ROWS = 32
GLOBAL_ROWS = NR * ROWS
LANES = 384
LO, GLU, GOD, OWN, GOU, GHD, HI, PHYS = 0, 12, 16, 20, 52, 56, 60, 72
REACH = 3
SEGS = 2 * REACH + 1
SLOTS = 4
NORMAL = {0: 0, 1: 1, 3: -1}
FROM_STATOR = (8, 9, 10, 7)
FROM_ROTOR = (-9, -8, -7, -10)
PER_LEVEL = ("K", "B", "U", "CU", "CL", "CE", "CW", "CZ", "CD", "WD", "E")


def roll(x, shift, axis):
    size = x.shape[axis]
    shift = shift % size
    return x if shift == 0 else pltpu.roll(x, shift, axis)


def tile_row(j, half):
    return (j // 8) * 16 + half * 8 + j % 8


def to_tiles(x):
    nz, rows, columns = x.shape
    x = x.reshape(nz, rows // 8, 8, columns // 128, 128)
    return x.transpose(0, 1, 3, 2, 4).reshape(nz * rows * columns // 128, 128)


def from_tiles(x, shape):
    nz, rows, columns = shape
    x = x.reshape(nz, rows // 8, columns // 128, 8, 128)
    return x.transpose(0, 1, 3, 2, 4).reshape(shape)


def loop_rows(low, high, body, unroll):
    count = (high - low) // unroll

    def step(i, carry):
        for q in range(unroll):
            body(low + i * unroll + q)
        return carry

    if count:
        lax.fori_loop(0, count, step, 0)
    for j in range(low + count * unroll, high):
        body(j)


def kernel(*refs):
    slide_ref, frac_ref, gain_ref, b_hbm, k_hbm, p_ref, res_ref = refs[:7]
    at = 7
    levels = []
    for _ in range(3):
        levels.append(dict(zip(PER_LEVEL, refs[at : at + len(PER_LEVEL)])))
        at += len(PER_LEVEL)
    (DG, B3S, EP, RT, RC_HI, RC_LO, RG, RGH, WC1, WC2, PK, PB, RN, RX, RB, VP, E3S) = refs[at : at + 17]
    k_ref, b_ref, sem_s, sem_r, sem_in = refs[at + 17 :]

    loads = [pltpu.make_async_copy(x, y, sem_in.at[i]) for i, (x, y) in enumerate(((k_hbm, k_ref), (b_hbm, b_ref)))]
    for load in loads:
        load.start()

    t = lax.axis_index("theta")
    r = lax.axis_index("rad")
    side = r // HALF
    is_rot = r == HALF - 1
    is_sta = r == HALF
    is_if = is_rot | is_sta
    near = (r >= HALF - REACH) & (r < HALF + REACH)
    slide = slide_ref[0]
    frac = frac_ref[0]
    gain = gain_ref[0]

    def theta(offset):
        return lax.rem(t + offset + 2 * NT, NT)

    lane = lax.broadcasted_iota(jnp.int32, (8, 128), 1)
    lane3 = lax.broadcasted_iota(jnp.int32, (8, LANES), 1)
    axial = lax.broadcasted_iota(jnp.int32, (8, 128), 0)
    K0, B0 = levels[0]["K"], levels[0]["B"]

    zeros3 = jnp.zeros((12, 8, LANES), F32)

    @pl.when(r == 0)
    def _():
        K0[pl.ds(LO, 12)] = zeros3
        B0[pl.ds(LO, 12)] = zeros3

    @pl.when(r == NR - 1)
    def _():
        K0[pl.ds(HI, 12)] = zeros3
        B0[pl.ds(HI, 12)] = zeros3

    RC_LO[...] = jnp.zeros_like(RC_LO)
    RC_HI[...] = jnp.zeros_like(RC_HI)
    RN[...] = jnp.ones_like(RN)
    RX[...] = jnp.ones_like(RX)
    RB[...] = jnp.zeros_like(RB)

    barrier = pltpu.get_barrier_semaphore()
    sgn = 1 - 2 * side
    inner = near & jnp.logical_not(is_if)
    greet, heard = [], []

    def meet(cond, dt, dr):
        greet.append((cond, dt, dr))
        heard.append(cond)

    for dr in (1, 2, 3):
        far_dr = dr * sgn
        to_inner = is_if & (dr > 1)
        from_if = inner & ((r + far_dr == HALF - 1) | (r + far_dr == HALF)) & ((r + far_dr) // HALF != side)
        for o in range(7, 11):
            if dr > 1:
                greet.append((to_inner, sgn * o, far_dr))
            heard.append(from_if)
    for o in range(7, 11):
        meet(is_if, sgn * o, sgn)
        meet((r == HALF - 2) | (r == HALF + 1), sgn * o, 3 * sgn)
    for o in range(6, 11):
        meet(is_if, o, 0)
    for dr in (-3, 3, -2, 2, -1, 1, 0):
        inside = (r + dr >= 0) & (r + dr < NR)
        for dt in (-1, 1, 0) if abs(dr) < 2 else (0,):
            if dr or dt:
                meet(inside, dt, dr)
    for o in (-2, 2):
        meet(near, o, 0)
    for cond, dt, dr in greet:
        peer = (theta(dt), r + dr)

        @pl.when(cond)
        def _(peer=peer):
            pl.semaphore_signal(barrier, inc=1, device_id=peer, device_id_type=MESH)

    for arr, (src, dst) in enumerate(((k_ref, K0), (b_ref, B0))):
        loads[arr].wait()

        def move(j, src=src, dst=dst):
            for half in range(2):
                dst[OWN + j, :, pl.ds(128 * half, 128)] = src[pl.ds(tile_row(j, half), 8, stride=2 * ROWS), :]

        loop_rows(0, ROWS, move, ROWS)
        for m in range(4):
            left = right = None
            for q in range(8):
                row = OWN + 8 * m + q
                low = roll(dst[row, :, pl.ds(0, 128)], 16 * q, 1)
                high = roll(dst[row, :, pl.ds(128, 128)], 16 * q + 16, 1)
                here = lane // 16 == q
                left = low if q == 0 else jnp.where(here, low, left)
                right = high if q == 0 else jnp.where(here, high, right)
            EP[0, m, arr] = left
            EP[1, m, arr] = right

    pl.semaphore_wait(barrier, sum(cond.astype(jnp.int32) for cond in heard))

    messages = []

    def message(index, send, recv, src, dst, target, start=True):
        copy = pltpu.make_async_remote_copy(
            src_ref=src,
            dst_ref=dst,
            send_sem=sem_s.at[index],
            recv_sem=sem_r.at[index],
            device_id=target,
            device_id_type=MESH,
        )
        if start:
            pl.when(send)(copy.start)
        messages.append((send, copy))
        return lambda: pl.when(recv)(copy.wait_recv)

    always = r >= 0
    down_s, down_r = (r >= 1) & (r != HALF), (r < NR - 1) & (r != HALF - 1)
    up_s, up_r = down_r, down_s
    wide = pl.ds(0, 256)
    w_th = [
        message(0, always, always, EP.at[0], RT.at[0], (theta(-1), r)),
        message(1, always, always, EP.at[1], RT.at[1], (theta(1), r)),
    ]
    w_k = [
        message(2, down_s, down_r, K0.at[pl.ds(OWN, 12), :, wide], K0.at[pl.ds(HI, 12), :, wide], (t, r - 1)),
        message(3, up_s, up_r, K0.at[pl.ds(OWN + 20, 12), :, wide], K0.at[pl.ds(LO, 12), :, wide], (t, r + 1)),
        message(4, down_s, down_r, EP.at[0, pl.ds(0, 2)], RC_HI.at[0], (theta(-1), r - 1)),
        message(5, down_s, down_r, EP.at[1, pl.ds(0, 2)], RC_HI.at[1], (theta(1), r - 1)),
        message(6, up_s, up_r, EP.at[0, pl.ds(2, 2)], RC_LO.at[0], (theta(-1), r + 1)),
        message(7, up_s, up_r, EP.at[1, pl.ds(2, 2)], RC_LO.at[1], (theta(1), r + 1)),
    ]
    w_b = [
        message(8, down_s, down_r, B0.at[pl.ds(OWN, 12), :, wide], B0.at[pl.ds(HI, 12), :, wide], (t, r - 1)),
        message(9, up_s, up_r, B0.at[pl.ds(OWN + 20, 12), :, wide], B0.at[pl.ds(LO, 12), :, wide], (t, r + 1)),
    ]
    w_i = []

    th = {o: theta(o) for o in (-1, 1, 8)}
    th_far = {"g2": theta(-9 * sgn), "ge": theta(-10 + 17 * side), "gw": theta(-7 + 17 * side), "c2": theta(9 * sgn)}

    facing = OWN + 20 * (1 - side)
    facing4 = OWN + 28 * (1 - side)
    group4 = 3 * (1 - side)
    other = NR - 1 - r
    ghost = GOD + (GOU - GOD) * side
    own4 = K0.at[pl.ds(facing4, 4), :, wide]
    items = [
        (own4, K0.at[pl.ds(ghost, 4), :, wide], (t, other)),
        (EP.at[0, group4, 0], RG.at[0], (th[-1], other)),
        (EP.at[1, group4, 0], RG.at[1], (th[1], other)),
        (own4, WC1.at[pl.ds(24, 4)], (th[8], r)),
        (own4, WC2.at[pl.ds(24, 4)], (th_far["g2"], r)),
        (EP.at[0, group4, 0], RGH.at[0], (th_far["ge"], r)),
        (EP.at[1, group4, 0], RGH.at[1], (th_far["gw"], r)),
        (K0.at[pl.ds(facing, 12), :, wide], WC1.at[pl.ds(0, 12)], (th[8], other)),
        (K0.at[pl.ds(facing, 12), :, wide], WC2.at[pl.ds(0, 12)], (th_far["c2"], other)),
        (B0.at[pl.ds(facing, 12), :, wide], WC1.at[pl.ds(12, 12)], (th[8], other)),
        (B0.at[pl.ds(facing, 12), :, wide], WC2.at[pl.ds(12, 12)], (th_far["c2"], other)),
    ]
    for n, (src, dst, target) in enumerate(items):
        w_i.append(message(10 + n, is_if, is_if, src, dst, target))

    cross_corners = []
    for part, (cond, dst, first) in enumerate(((is_sta, RC_HI, 0), (is_rot, RC_LO, 2))):
        other = r - 1 if part == 0 else r + 1
        offs = (-10, -7) if part == 0 else (7, 10)
        got = is_rot if part == 0 else is_sta
        for e in range(2):
            cross_corners.append(
                message(
                    (4 if part == 0 else 6) + e,
                    cond,
                    got,
                    EP.at[e, pl.ds(first, 2)],
                    dst.at[e],
                    (theta(offs[e]), other),
                )
            )

    def pairs(x, cell):
        width = x.shape[-1]
        pick = (lax.broadcasted_iota(jnp.int32, x.shape, x.ndim - 1) // cell) % 2 == 1
        return x + jnp.where(pick, roll(x, cell, x.ndim - 1), roll(x, width - cell, x.ndim - 1))

    gather_index = (lane % 16) * 8

    def pack(rows):
        out = None
        for q, x in enumerate(rows):
            for half in range(2):
                part = jnp.take_along_axis(x[:, 128 * half : 128 * half + 128], gather_index, axis=1)
                out = part if out is None else jnp.where(lane // 16 == 2 * q + half, part, out)
        return out

    own3 = []
    for j in range(4):
        k2 = []
        for i in range(2):
            k1 = []
            for h in range(2):
                row = OWN + 8 * j + 4 * i + 2 * h
                k1.append(0.25 * pairs(K0[row, :, wide] + K0[row + 1, :, wide], 1))
            k2.append(0.25 * pairs(k1[0] + k1[1], 2))
        own3.append(0.25 * pairs(k2[0] + k2[1], 4))
    PK[...] = pack(own3)

    RN[REACH, 0] = PK[...]
    base_t, base_n, base_x, base_b = 21, 24, 24 + SEGS, 24 + 2 * SEGS
    w_t = [
        message(base_t, always, always, PK, RN.at[REACH, 1], (theta(-1), r)),
        message(base_t + 1, always, always, PK, RN.at[REACH, 3], (theta(1), r)),
        message(base_t + 2, near, near, PK, RN.at[REACH, 2], (theta(-2), r)),
    ]

    w_n, w_x = {}, {}

    def send_plain():
        for dr in (-3, 3, -2, 2, -1, 1):
            inside_s = (r + dr >= 0) & (r + dr < NR)
            inside_r = (r - dr >= 0) & (r - dr < NR)
            seg = REACH - dr
            w_n[seg] = message(base_n + seg, inside_s, inside_r, RN.at[REACH], RN.at[seg], (t, r + dr))

    def send_across(which):
        for dr in range(-REACH, REACH + 1):
            seg = REACH - dr
            to, fro = r + dr, r - dr
            to_rot = (to < HALF) & (to >= HALF - REACH) & (r >= HALF - 1)
            to_sta = (to >= HALF) & (to < HALF + REACH) & (r <= HALF)
            got = ((r < HALF) & (r >= HALF - REACH) & (fro >= HALF - 1)) | (
                (r >= HALF) & (r < HALF + REACH) & (fro <= HALF)
            )
            off = -FROM_STATOR[0] + ((r + dr) // HALF) * (FROM_STATOR[0] - FROM_ROTOR[0])
            w_x[seg] = message(
                base_x + seg, (to_rot | to_sta) & which, got, RN.at[REACH], RX.at[seg], (theta(off), r + dr)
            )

    def third(left_pack, right_pack, q):
        return jnp.where(lane < 64, roll(left_pack, -16 * q, 1), roll(right_pack, 112 - 16 * q, 1))

    halo = pl.ds(256, 128)
    for w in w_th:
        w()
    for m in range(4):
        for arr, ref in enumerate((K0, B0)):
            for q in range(8):
                ref[OWN + 8 * m + q, :, halo] = third(RT[0, m, arr], RT[1, m, arr], q)
    for w in w_t:
        w()
    send_plain()
    send_across(inner)
    top = axial < 7
    low_ok, high_ok = r > 0, r < NR - 1

    def coefficients(level, seg, low, high):
        A = levels[level]
        rows_level = GLOBAL_ROWS >> level
        inv = 1.0 / rows_level
        cell = 1 << level
        start = {"lo": LO + 12, "own": OWN, "hi": HI - 32}[seg] >> level
        ok = {"lo": low_ok, "own": None, "hi": high_ok}[seg]

        def body(j):
            pos = r * (ROWS >> level) + j - start
            posf = pos.astype(F32)
            hu = 0.5 * (1.0 + (posf + 1.0) * inv) * jnp.where(pos == rows_level // 2 - 1, gain, 1.0)
            hl = 0.5 * (1.0 + posf * inv) * jnp.where(pos == rows_level // 2, gain, 1.0)
            rc = 1.0 + (posf + 0.5) * inv
            hc1 = 0.5 / jnp.full((8, 128), rc, F32)
            hz1 = jnp.where(top, 0.5 * rc, 0.0)
            hc = jnp.concatenate([hc1] * 3, axis=1)
            hz = jnp.concatenate([hz1] * 3, axis=1)
            k = A["K"][j]
            ce = (k + roll(k, -cell, 1)) * hc
            cw = roll(ce, cell, 1)
            cu = (k + A["K"][j + 1]) * hu
            cl = (k + A["K"][j - 1]) * hl
            cz = (k + roll(k, -1, 0)) * hz
            cd = roll(cz, 1, 0)
            diag = cu + cl + ce + cw + cz + cd
            wd = 0.8 / diag
            if ok is not None:
                wd = jnp.where(ok, wd, 0.0)
            A["CU"][j], A["CL"][j], A["CE"][j], A["CW"][j], A["CZ"][j], A["CD"][j] = cu, cl, ce, cw, cz, cd
            A["WD"][j] = wd
            if level == 0:
                A["U"][j] = wd * A["B"][j]
                if seg == "own":
                    DG[j - OWN] = diag

        loop_rows(low, high, body, 8)

    coefficients(0, "own", OWN + 1, OWN + ROWS - 1)

    for w in w_k:
        w()
    for w in cross_corners:
        w()
    for w in w_b:
        w()
    for j in range(12):
        for arr, ref in enumerate((K0, B0)):
            m, q = divmod(j, 8)
            ref[HI + j, :, halo] = third(RC_HI[0, m, arr], RC_HI[1, m, arr], q)
            m, q = divmod(4 + j, 8)
            ref[LO + j, :, halo] = third(RC_LO[0, m, arr], RC_LO[1, m, arr], q)

    fine = slide - NT * 256 // 2
    d4 = (fine // 4) * 4
    q4 = d4 % 128
    far = d4 >= 128
    back4 = lax.rem(128 - q4, 128)

    for w in w_i:
        w()
    send_across(is_if)

    def window(tiles, sign):
        if sign > 0:
            tiles = [jnp.where(far, tiles[(i + 1) % 5], tiles[i]) for i in range(5)]
            turned = [pltpu.roll(x, back4, 1) for x in tiles]
            keep = lane < 128 - q4
            out = [jnp.where(keep, turned[i], turned[(i + 1) % 5]) for i in (0, 1, 2, 4)]
        else:
            tiles = [jnp.where(far, tiles[(i + 4) % 5], tiles[i]) for i in range(5)]
            turned = [pltpu.roll(x, q4, 1) for x in tiles]
            keep = lane >= q4
            out = [jnp.where(keep, turned[i], turned[(i + 4) % 5]) for i in (0, 1, 2, 4)]
        return out[0], out[1], jnp.where(lane < 64, out[2], out[3])

    def fill(sign, dst_k, dst_ghost):
        for j in range(28):
            if j < 24:
                ref, row = ((K0, B0)[j // 12], dst_k + j % 12)
                edge = ref[row, :, halo]
            else:
                ref, row = (K0, dst_ghost + j - 24)
                edge = third(RGH[0], RGH[1], j - 24 + (4 if sign > 0 else 0))
            a = [WC1[j, :, pl.ds(0, 128)], WC1[j, :, pl.ds(128, 128)]]
            b = [WC2[j, :, pl.ds(0, 128)], WC2[j, :, pl.ds(128, 128)]]
            tiles = a + b + [edge] if sign > 0 else a + [edge] + b
            for i, x in enumerate(window(tiles, sign)):
                ref[row, :, pl.ds(128 * i, 128)] = x

    @pl.when(is_rot)
    def _():
        fill(1, HI, GHD)
        for j in range(4):
            K0[GOU + j, :, halo] = third(RG[0], RG[1], j)

    @pl.when(is_sta)
    def _():
        fill(-1, LO, GLU)
        for j in range(4):
            K0[GOD + j, :, halo] = third(RG[0], RG[1], 4 + j)

    @pl.when(jnp.logical_not(is_rot))
    def _():
        K0[pl.ds(GOU, 4)] = K0[pl.ds(HI, 4)]
        K0[pl.ds(GHD, 4)] = K0[pl.ds(OWN + 28, 4)]

    @pl.when(jnp.logical_not(is_sta))
    def _():
        K0[pl.ds(GLU, 4)] = K0[pl.ds(OWN, 4)]
        K0[pl.ds(GOD, 4)] = K0[pl.ds(LO + 8, 4)]

    for level in (1, 2):
        fine_k, coarse_k = levels[level - 1]["K"], levels[level]["K"]

        def down_k(j, fine_k=fine_k, coarse_k=coarse_k, cell=1 << (level - 1)):
            coarse_k[j] = 0.25 * pairs(fine_k[2 * j] + fine_k[2 * j + 1], cell)

        loop_rows(0, PHYS >> level, down_k, 4)

    def spans(level, halo_rows):
        lo, own, hi = LO + 12 >> level, OWN >> level, HI >> level
        out = [("own", own, own + (ROWS >> level))]
        if halo_rows:
            out = [("lo", lo - halo_rows, lo)] + out + [("hi", hi, hi + halo_rows)]
        return out

    for level, halo_rows in ((0, 11), (1, 5), (2, 2)):
        for seg, low, high in spans(level, halo_rows):
            if level == 0 and seg == "own":
                coefficients(level, seg, low, low + 1)
                coefficients(level, seg, high - 1, high)
            else:
                coefficients(level, seg, low, high)

    def weights(active, shift, count):
        out = []
        for i in range(count):
            w = jnp.where(shift == i, 1.0 - frac, 0.0) + jnp.where(shift == i - 1, frac, 0.0)
            out.append(jnp.where(active, w, 1.0 if i == 0 else 0.0))
        return out

    shifts = (fine % 4, (fine // 2) % 2, 0 * fine)
    up_w = [weights(is_rot, shifts[level], (5, 3, 2)[level]) for level in range(3)]
    low_w = [weights(is_sta, shifts[level], (5, 3, 2)[level]) for level in range(3)]

    def mix(x, w, step):
        out = w[0] * x
        for i in range(1, len(w)):
            out = out + w[i] * roll(x, i * step, x.ndim - 1)
        return out

    def ghosts(field, level):
        cell = 1 << level
        lo_end, own, own_end, hi = LO + 12 >> level, OWN >> level, GOU >> level, HI >> level
        field[own_end] = mix(field[hi], up_w[level], -cell)
        field[hi - 1] = mix(field[own_end - 1], up_w[level], cell)
        field[lo_end] = mix(field[own], low_w[level], -cell)
        field[own - 1] = mix(field[lo_end - 1], low_w[level], cell)

    def neighbours(level, field, j):
        A = levels[level]
        cell = 1 << level
        v = field[j]
        return (
            A["CU"][j] * field[j + 1]
            + A["CL"][j] * field[j - 1]
            + A["CE"][j] * roll(v, -cell, 1)
            + A["CW"][j] * roll(v, cell, 1)
            + A["CZ"][j] * roll(v, -1, 0)
            + A["CD"][j] * roll(v, 1, 0)
        )

    for level in range(3):
        A = levels[level]
        if level:

            def first(j, A=A):
                A["U"][j] = A["WD"][j] * A["B"][j]

            for seg, low, high in spans(level, (11, 5, 2)[level]):
                loop_rows(low, high, first, 8)
        ghosts(A["U"], level)

        def restrict(j, A=A, level=level):
            x = 0.2 * (A["B"][2 * j] + A["B"][2 * j + 1])
            x = x + (neighbours(level, A["U"], 2 * j) + neighbours(level, A["U"], 2 * j + 1))
            x = pairs(x, 1 << level)
            if level < 2:
                levels[level + 1]["B"][j] = x
            else:
                B3S[j - (OWN >> 3 if OWN % 8 == 0 else 0)] = x

        if level < 2:
            for seg, low, high in spans(level + 1, (5, 2)[level]):
                loop_rows(low, high, restrict, 4)
        else:
            for j in range(4):
                x = None
                for i in range(2):
                    row = (OWN >> 2) + 2 * j + i
                    y = 0.2 * A["B"][row] + neighbours(2, A["U"], row)
                    x = y if x is None else x + y
                B3S[j] = pairs(x, 4)

    for w in w_n.values():
        w()
    PB[...] = pack([B3S[j, :, wide] for j in range(4)])
    RB[REACH, 0] = PB[...]
    w_p = []
    for dr in range(-REACH, REACH + 1):
        inside_s = (r + dr >= 0) & (r + dr < NR)
        inside_r = (r - dr >= 0) & (r - dr < NR)
        seg = REACH - dr
        same_s = (r + dr) // HALF == side
        same_r = (r - dr) // HALF == side
        to_side = (r + dr) // HALF
        for slot in range(SLOTS):
            index = base_b + seg * SLOTS + slot
            if slot in NORMAL and (dr or slot):
                w_p.append(
                    message(
                        index, inside_s & same_s, inside_r & same_r, PB, RB.at[seg, slot], (theta(-NORMAL[slot]), r + dr)
                    )
                )
            if dr:
                off = -FROM_STATOR[slot] + to_side * (FROM_STATOR[slot] - FROM_ROTOR[slot])
                w_p.append(
                    message(
                        index,
                        inside_s & jnp.logical_not(same_s),
                        inside_r & jnp.logical_not(same_r),
                        PB,
                        RB.at[seg, slot],
                        (theta(off), r + dr),
                    )
                )

    count3 = 4 * SEGS
    d3 = (fine // 16) * 2
    sgn_x = jnp.where(side == 0, lax.rem(128 - d3, 128), lax.rem(d3 + 96, 128))

    def unpack(ref):
        tiles = [ref[:, o] for o in range(SLOTS)]
        lane7 = lax.broadcasted_iota(jnp.int32, (SEGS, 8, 128), 2) // 32
        rows = []
        for q in range(4):
            out = roll(tiles[0], -32 * q, 2)
            for o in range(1, SLOTS):
                out = jnp.where(lane7 == o, roll(tiles[o], 32 * (o - q), 2), out)
            rows.append(out)
        return jnp.stack(rows, axis=1).reshape(count3, 8, 128)

    def turn(x):
        return pltpu.roll(x, sgn_x, 2)

    for w in w_x.values():
        w()
    kn = unpack(RN)
    kx = turn(unpack(RX))

    far_off = jnp.where(near, side, 1 << 20)

    def coefficients_patch(kn, kx, rows, level, cell):
        rows_level = GLOBAL_ROWS >> level
        inv = 1.0 / rows_level
        pos = (r - REACH) * (ROWS >> level) + lax.broadcasted_iota(jnp.int32, (rows, 8, 128), 0)
        ok = (pos >= 0) & (pos < rows_level)
        beyond = (pos - rows_level // 2) * (1 - 2 * side) >= far_off
        posf = pos.astype(F32)
        hu = 0.5 * (1.0 + (posf + 1.0) * inv) * jnp.where(pos == rows_level // 2 - 1, gain, 1.0)
        hl = 0.5 * (1.0 + posf * inv) * jnp.where(pos == rows_level // 2, gain, 1.0)
        rc = 1.0 + (posf + 0.5) * inv
        hc = 0.5 / rc
        hz = jnp.where(lax.broadcasted_iota(jnp.int32, (rows, 8, 128), 1) < 7, 0.5 * rc, 0.0)
        k = jnp.where(beyond, kx, kn)
        ku = jnp.where(beyond, jnp.concatenate([kx[1:], kx[:1]], 0), jnp.concatenate([kn[1:], kn[:1]], 0))
        kd = jnp.where(beyond, jnp.concatenate([kx[-1:], kx[:-1]], 0), jnp.concatenate([kn[-1:], kn[:-1]], 0))
        ku = jnp.where(pos == rows_level - 1, 0.0, ku)
        kd = jnp.where(pos == 0, 0.0, kd)
        ce = (k + roll(k, -cell, 2)) * hc
        cw = roll(ce, cell, 2)
        cu = (k + ku) * hu
        cl = (k + kd) * hl
        cz = (k + roll(k, -1, 1)) * hz
        cd = roll(cz, 1, 1)
        wd = jnp.where(ok, 0.8 / (cu + cl + ce + cw + cz + cd), 0.0)
        return (cu, cl, ce, cw, cz, cd, wd, beyond)

    def coarse_k(x):
        y = x.reshape(x.shape[0] // 2, 2, 8, 128)
        return 0.25 * pairs(y[:, 0] + y[:, 1], 1)

    C3 = coefficients_patch(kn, kx, count3, 3, 1)
    C4 = coefficients_patch(coarse_k(kn), coarse_k(kx), count3 // 2, 4, 2)

    odd = (fine // 8) % 2
    w3 = weights(r >= 0, odd, 3)
    w4 = weights(r >= 0, 0 * odd, 2)

    def neighbours_patch(C, v, step, w, cell):
        n = v.shape[0]
        edge = lax.rem(HALF - r + REACH + 4 * SEGS, SEGS) * step
        VP[pl.ds(0, n)] = v
        over = mix(VP[edge], w, -cell)
        under = mix(VP[lax.rem(edge + n - 1, n)], w, cell)
        row = lax.broadcasted_iota(jnp.int32, v.shape, 0)
        vu = jnp.concatenate([v[1:], v[:1]], 0)
        vd = jnp.concatenate([v[-1:], v[:-1]], 0)
        mark = jnp.where(near, edge, -8)
        vu = jnp.where(row == mark - 1, over[None], vu)
        vd = jnp.where(row == mark, under[None], vd)
        return (
            C[0] * vu
            + C[1] * vd
            + C[2] * roll(v, -cell, 2)
            + C[3] * roll(v, cell, 2)
            + C[4] * roll(v, -1, 1)
            + C[5] * roll(v, 1, 1)
        )

    for w in w_p:
        w()
    b3 = unpack(RB)
    b3 = jnp.where(C3[7], turn(b3), b3)
    u3 = C3[6] * b3
    x = 0.2 * b3 + neighbours_patch(C3, u3, 4, w3, 1)
    x = x.reshape(count3 // 2, 2, 8, 128)
    b4 = pairs(x[:, 0] + x[:, 1], 1)
    v4 = C4[6] * b4
    for _ in range(3):
        v4 = 0.2 * v4 + C4[6] * (b4 + neighbours_patch(C4, v4, 2, w4, 2))
    up4 = jnp.broadcast_to(v4[:, None], (count3 // 2, 2, 8, 128)).reshape(count3, 8, 128)
    v3 = u3 + up4
    e3 = 0.2 * v3 + C3[6] * (b3 + neighbours_patch(C3, v3, 4, w3, 1))

    delta = (fine // 4) % 4 * 4
    first_row = 4 * REACH - 1
    for j in range(6):
        if j == 0:
            shift = jnp.where(is_sta, -delta, 0)
        elif j == 5:
            shift = jnp.where(is_rot, delta, 0)
        else:
            shift = 0
        for i in range(3):
            signed = lane + 128 * i
            if i == 2:
                signed = jnp.where(lane < 64, signed, signed - LANES)
            index = ((signed + shift + 1024) // 8) % 128
            E3S[j, :, pl.ds(128 * i, 128)] = jnp.take_along_axis(e3[first_row + j], index, axis=1)

    for level in (2, 1, 0):
        A = levels[level]
        low, own, hi = LO + 12 >> level, OWN >> level, HI >> level
        rows = ROWS >> level
        if level == 2:
            A["U"][low - 2] = A["U"][low - 2] + E3S[0]
            A["U"][low - 1] = A["U"][low - 1] + E3S[0]
            for j in range(rows):
                A["U"][own + j] = A["U"][own + j] + E3S[1 + j // 2]
            A["U"][hi] = A["U"][hi] + E3S[5]
            A["U"][hi + 1] = A["U"][hi + 1] + E3S[5]
        else:
            E = levels[level + 1]["E"]

            def add(j, A=A, E=E):
                e = E[j]
                A["U"][2 * j] = A["U"][2 * j] + e
                A["U"][2 * j + 1] = A["U"][2 * j + 1] + e

            add((low >> 1) - 1)
            loop_rows(own >> 1, (own + rows) >> 1, add, 4)
            add(hi >> 1)
        ghosts(A["U"], level)

        def smooth(j, A=A, level=level):
            A["E"][j] = 0.2 * A["U"][j] + A["WD"][j] * (A["B"][j] + neighbours(level, A["U"], j))

        smooth(low - 1)
        loop_rows(own, own + rows, smooth, 8)
        smooth(hi)

    ghosts(levels[0]["E"], 0)

    def finish(j):
        E = levels[0]["E"]
        p = E[OWN + j]
        out = B0[OWN + j] - DG[j] * p + neighbours(0, E, OWN + j)
        for half in range(2):
            place = pl.ds(tile_row(j, half), 8, stride=2 * ROWS)
            p_ref[place, :] = p[:, 128 * half : 128 * half + 128]
            res_ref[place, :] = out[:, 128 * half : 128 * half + 128]

    loop_rows(0, ROWS, finish, 8)

    for send, copy in messages:
        pl.when(send)(copy.wait_send)


def on_device(source, conductance, slide, fraction, gain):
    nz, rows, columns = source.shape
    scratch = []
    for level in range(3):
        scratch += [pltpu.VMEM((PHYS >> level, nz, LANES), F32)] * len(PER_LEVEL)
    tile = (8, 128)
    scratch += [
        pltpu.VMEM((ROWS, nz, LANES), F32),
        pltpu.VMEM((4, nz, LANES), F32),
        pltpu.VMEM((2, 4, 2) + tile, F32),
        pltpu.VMEM((2, 4, 2) + tile, F32),
        pltpu.VMEM((2, 2, 2) + tile, F32),
        pltpu.VMEM((2, 2, 2) + tile, F32),
        pltpu.VMEM((2,) + tile, F32),
        pltpu.VMEM((2,) + tile, F32),
        pltpu.VMEM((28, nz, 256), F32),
        pltpu.VMEM((28, nz, 256), F32),
        pltpu.VMEM(tile, F32),
        pltpu.VMEM(tile, F32),
        pltpu.VMEM((SEGS, SLOTS) + tile, F32),
        pltpu.VMEM((SEGS, SLOTS) + tile, F32),
        pltpu.VMEM((SEGS, SLOTS) + tile, F32),
        pltpu.VMEM((4 * SEGS,) + tile, F32),
        pltpu.VMEM((6, nz, LANES), F32),
        pltpu.VMEM((nz * rows * columns // 128, 128), F32),
        pltpu.VMEM((nz * rows * columns // 128, 128), F32),
    ]
    sems = 24 + 2 * SEGS + SEGS * SLOTS
    scratch += [pltpu.SemaphoreType.DMA((n,)) for n in (sems, sems, 2)]
    smem = pl.BlockSpec(memory_space=pltpu.SMEM)
    vmem = pl.BlockSpec(memory_space=pltpu.VMEM)
    hbm = pl.BlockSpec(memory_space=pl.ANY)
    flat = jax.ShapeDtypeStruct((nz * rows * columns // 128, 128), F32)
    pressure, residual = pl.pallas_call(
        kernel,
        out_shape=(flat, flat),
        in_specs=[smem, smem, smem, hbm, hbm],
        out_specs=(vmem, vmem),
        scratch_shapes=scratch,
        compiler_params=pltpu.CompilerParams(
            collective_id=0, has_side_effects=True, vmem_limit_bytes=48 * 1024 * 1024
        ),
    )(slide, fraction, gain, to_tiles(source), to_tiles(conductance))
    return from_tiles(pressure, source.shape), from_tiles(residual, source.shape)


def solution(mesh):
    spec = P(None, "rad", "theta")
    return jax.shard_map(
        on_device, mesh=mesh, in_specs=(spec, spec, P(), P(), P()), out_specs=(spec, spec), check_vma=False
    )
```

```python
import functools

import jax
import jax.numpy as jnp
from jax import lax
from jax.experimental import pallas as pl
from jax.experimental.pallas import tpu as pltpu
from jax.sharding import PartitionSpec as P

MESH = pl.DeviceIdType.MESH
F32 = jnp.float32
NT, NR = 16, 32
HALF = NR // 2
ROWS = 32
GLOBAL_ROWS = NR * ROWS
LANES = 384
LO, GLU, GOD, OWN, GOU, GHD, HI, PHYS = 0, 12, 16, 20, 52, 56, 60, 72
REACH = 3
SEGS = 2 * REACH + 1
SLOTS = 4
NORMAL = {0: 0, 1: 1, 3: -1}
FROM_STATOR = (8, 9, 10, 7)
FROM_ROTOR = (-9, -8, -7, -10)
PER_LEVEL = ("K", "B", "U", "CU", "CL", "CE", "CW", "CZ", "CD", "WD", "E")


def roll(x, shift, axis):
    size = x.shape[axis]
    shift = shift % size
    return x if shift == 0 else pltpu.roll(x, shift, axis)


def tile_row(j, half):
    return (j // 8) * 16 + half * 8 + j % 8


def to_tiles(x):
    nz, rows, columns = x.shape
    x = x.reshape(nz, rows // 8, 8, columns // 128, 128)
    return x.transpose(0, 1, 3, 2, 4).reshape(nz * rows * columns // 128, 128)


def from_tiles(x, shape):
    nz, rows, columns = shape
    x = x.reshape(nz, rows // 8, columns // 128, 8, 128)
    return x.transpose(0, 1, 3, 2, 4).reshape(shape)


def loop_rows(low, high, body, unroll):
    count = (high - low) // unroll

    def step(i, carry):
        for q in range(unroll):
            body(low + i * unroll + q)
        return carry

    if count:
        lax.fori_loop(0, count, step, 0)
    for j in range(low + count * unroll, high):
        body(j)


def kernel(*refs):
    slide_ref, frac_ref, gain_ref, b_hbm, k_hbm, p_ref, res_ref = refs[:7]
    at = 7
    levels = []
    for _ in range(3):
        levels.append(dict(zip(PER_LEVEL, refs[at : at + len(PER_LEVEL)])))
        at += len(PER_LEVEL)
    (DG, B3S, EP, RT, RC_HI, RC_LO, RG, RGH, WC1, WC2, PK, PB, RN, RX, RB, VP, E3S) = refs[at : at + 17]
    k_ref, b_ref, sem_s, sem_r, sem_in = refs[at + 17 :]

    moves = ((k_hbm, k_ref), (b_hbm, b_ref))
    loads = [pltpu.make_async_copy(x, y, sem_in.at[i]) for i, (x, y) in enumerate(moves)]
    for load in loads:
        load.start()

    t = lax.axis_index("theta")
    r = lax.axis_index("rad")
    side = r // HALF
    is_rot = r == HALF - 1
    is_sta = r == HALF
    is_if = is_rot | is_sta
    near = (r >= HALF - REACH) & (r < HALF + REACH)

    def theta(offset):
        return lax.rem(t + offset + 2 * NT, NT)

    lane = lax.broadcasted_iota(jnp.int32, (8, 128), 1)
    lane3 = lax.broadcasted_iota(jnp.int32, (8, LANES), 1)
    axial = lax.broadcasted_iota(jnp.int32, (8, 128), 0)
    K0, B0 = levels[0]["K"], levels[0]["B"]

    zeros3 = jnp.zeros((12, 8, LANES), F32)

    @pl.when(r == 0)
    def _():
        K0[pl.ds(LO, 12)] = zeros3
        B0[pl.ds(LO, 12)] = zeros3

    @pl.when(r == NR - 1)
    def _():
        K0[pl.ds(HI, 12)] = zeros3
        B0[pl.ds(HI, 12)] = zeros3

    RC_LO[...] = jnp.zeros_like(RC_LO)
    RC_HI[...] = jnp.zeros_like(RC_HI)
    RN[...] = jnp.ones_like(RN)
    RX[...] = jnp.ones_like(RX)
    RB[...] = jnp.zeros_like(RB)

    barrier = pltpu.get_barrier_semaphore()
    sgn = 1 - 2 * side
    inner = near & jnp.logical_not(is_if)
    greet, heard = [], []

    def meet(cond, dt, dr):
        greet.append((cond, dt, dr))
        heard.append(cond)

    for dr in (1, 2, 3):
        far_dr = dr * sgn
        to_inner = is_if & (dr > 1)
        from_if = inner & ((r + far_dr == HALF - 1) | (r + far_dr == HALF)) & ((r + far_dr) // HALF != side)
        for o in range(7, 11):
            if dr > 1:
                greet.append((to_inner, sgn * o, far_dr))
            heard.append(from_if)
    for o in range(7, 11):
        meet(is_if, sgn * o, sgn)
        meet((r == HALF - 2) | (r == HALF + 1), sgn * o, 3 * sgn)
    for o in range(6, 11):
        meet(is_if, o, 0)
    for dr in (-3, 3, -2, 2, -1, 1, 0):
        inside = (r + dr >= 0) & (r + dr < NR)
        for dt in (-1, 1, 0) if abs(dr) < 2 else (0,):
            if dr or dt:
                meet(inside, dt, dr)
    for o in (-2, 2):
        meet(near, o, 0)
    for cond, dt, dr in greet:
        peer = (theta(dt), r + dr)

        @pl.when(cond)
        def _(peer=peer):
            pl.semaphore_signal(barrier, inc=1, device_id=peer, device_id_type=MESH)

    for arr, (src, dst) in enumerate(((k_ref, K0), (b_ref, B0))):
        loads[arr].wait()

        def move(j, src=src, dst=dst):
            for half in range(2):
                dst[OWN + j, :, pl.ds(128 * half, 128)] = src[pl.ds(tile_row(j, half), 8, stride=2 * ROWS), :]

        loop_rows(0, ROWS, move, ROWS)
        for m in range(4):
            left = right = None
            for q in range(8):
                row = OWN + 8 * m + q
                low = roll(dst[row, :, pl.ds(0, 128)], 16 * q, 1)
                high = roll(dst[row, :, pl.ds(128, 128)], 16 * q + 16, 1)
                here = lane // 16 == q
                left = low if q == 0 else jnp.where(here, low, left)
                right = high if q == 0 else jnp.where(here, high, right)
            EP[0, m, arr] = left
            EP[1, m, arr] = right

    pl.semaphore_wait(barrier, sum(cond.astype(jnp.int32) for cond in heard))

    messages = []

    def message(index, send, recv, src, dst, target, start=True):
        copy = pltpu.make_async_remote_copy(
            src_ref=src,
            dst_ref=dst,
            send_sem=sem_s.at[index],
            recv_sem=sem_r.at[index],
            device_id=target,
            device_id_type=MESH,
        )
        if start:
            pl.when(send)(copy.start)
        messages.append((send, copy))
        return lambda: pl.when(recv)(copy.wait_recv)

    always = r >= 0
    down_s, down_r = (r >= 1) & (r != HALF), (r < NR - 1) & (r != HALF - 1)
    up_s, up_r = down_r, down_s
    wide = pl.ds(0, 256)
    w_th = [
        message(0, always, always, EP.at[0], RT.at[0], (theta(-1), r)),
        message(1, always, always, EP.at[1], RT.at[1], (theta(1), r)),
    ]
    w_k = [
        message(2, down_s, down_r, K0.at[pl.ds(OWN, 12), :, wide], K0.at[pl.ds(HI, 12), :, wide], (t, r - 1)),
        message(3, up_s, up_r, K0.at[pl.ds(OWN + 20, 12), :, wide], K0.at[pl.ds(LO, 12), :, wide], (t, r + 1)),
        message(4, down_s, down_r, EP.at[0, pl.ds(0, 2)], RC_HI.at[0], (theta(-1), r - 1)),
        message(5, down_s, down_r, EP.at[1, pl.ds(0, 2)], RC_HI.at[1], (theta(1), r - 1)),
        message(6, up_s, up_r, EP.at[0, pl.ds(2, 2)], RC_LO.at[0], (theta(-1), r + 1)),
        message(7, up_s, up_r, EP.at[1, pl.ds(2, 2)], RC_LO.at[1], (theta(1), r + 1)),
    ]
    w_b = [
        message(8, down_s, down_r, B0.at[pl.ds(OWN, 12), :, wide], B0.at[pl.ds(HI, 12), :, wide], (t, r - 1)),
        message(9, up_s, up_r, B0.at[pl.ds(OWN + 20, 12), :, wide], B0.at[pl.ds(LO, 12), :, wide], (t, r + 1)),
    ]
    w_i = []

    th = {o: theta(o) for o in (-1, 1, 8)}
    th_far = {"g2": theta(-9 * sgn), "ge": theta(-10 + 17 * side), "gw": theta(-7 + 17 * side), "c2": theta(9 * sgn)}

    facing = OWN + 20 * (1 - side)
    facing4 = OWN + 28 * (1 - side)
    group4 = 3 * (1 - side)
    other = NR - 1 - r
    ghost = GOD + (GOU - GOD) * side
    own4 = K0.at[pl.ds(facing4, 4), :, wide]
    items = [
        (own4, K0.at[pl.ds(ghost, 4), :, wide], (t, other)),
        (EP.at[0, group4, 0], RG.at[0], (th[-1], other)),
        (EP.at[1, group4, 0], RG.at[1], (th[1], other)),
        (own4, WC1.at[pl.ds(24, 4)], (th[8], r)),
        (own4, WC2.at[pl.ds(24, 4)], (th_far["g2"], r)),
        (EP.at[0, group4, 0], RGH.at[0], (th_far["ge"], r)),
        (EP.at[1, group4, 0], RGH.at[1], (th_far["gw"], r)),
        (K0.at[pl.ds(facing, 12), :, wide], WC1.at[pl.ds(0, 12)], (th[8], other)),
        (K0.at[pl.ds(facing, 12), :, wide], WC2.at[pl.ds(0, 12)], (th_far["c2"], other)),
        (B0.at[pl.ds(facing, 12), :, wide], WC1.at[pl.ds(12, 12)], (th[8], other)),
        (B0.at[pl.ds(facing, 12), :, wide], WC2.at[pl.ds(12, 12)], (th_far["c2"], other)),
    ]
    for n, (src, dst, target) in enumerate(items):
        w_i.append(message(10 + n, is_if, is_if, src, dst, target))

    cross_corners = []
    for part, (cond, dst, first) in enumerate(((is_sta, RC_HI, 0), (is_rot, RC_LO, 2))):
        other = r - 1 if part == 0 else r + 1
        offs = (-10, -7) if part == 0 else (7, 10)
        got = is_rot if part == 0 else is_sta
        for e in range(2):
            cross_corners.append(
                message(
                    (4 if part == 0 else 6) + e,
                    cond,
                    got,
                    EP.at[e, pl.ds(first, 2)],
                    dst.at[e],
                    (theta(offs[e]), other),
                )
            )

    slide = slide_ref[0]
    frac = frac_ref[0]
    gain = gain_ref[0]

    def pairs(x, cell):
        width = x.shape[-1]
        pick = (lax.broadcasted_iota(jnp.int32, x.shape, x.ndim - 1) // cell) % 2 == 1
        return x + jnp.where(pick, roll(x, cell, x.ndim - 1), roll(x, width - cell, x.ndim - 1))

    gather_index = (lane % 16) * 8

    def pack(rows):
        out = None
        for q, x in enumerate(rows):
            for half in range(2):
                part = jnp.take_along_axis(x[:, 128 * half : 128 * half + 128], gather_index, axis=1)
                out = part if out is None else jnp.where(lane // 16 == 2 * q + half, part, out)
        return out

    own3 = []
    for j in range(4):
        k2 = []
        for i in range(2):
            k1 = []
            for h in range(2):
                row = OWN + 8 * j + 4 * i + 2 * h
                k1.append(0.25 * pairs(K0[row, :, wide] + K0[row + 1, :, wide], 1))
            k2.append(0.25 * pairs(k1[0] + k1[1], 2))
        own3.append(0.25 * pairs(k2[0] + k2[1], 4))
    PK[...] = pack(own3)

    RN[REACH, 0] = PK[...]
    base_t, base_n, base_x, base_b = 21, 24, 24 + SEGS, 24 + 2 * SEGS
    w_t = [
        message(base_t, always, always, PK, RN.at[REACH, 1], (theta(-1), r)),
        message(base_t + 1, always, always, PK, RN.at[REACH, 3], (theta(1), r)),
        message(base_t + 2, near, near, PK, RN.at[REACH, 2], (theta(-2), r)),
    ]

    w_n, w_x = {}, {}

    def send_plain():
        for dr in (-3, 3, -2, 2, -1, 1):
            inside_s = (r + dr >= 0) & (r + dr < NR)
            inside_r = (r - dr >= 0) & (r - dr < NR)
            seg = REACH - dr
            w_n[seg] = message(base_n + seg, inside_s, inside_r, RN.at[REACH], RN.at[seg], (t, r + dr))

    def send_across(which):
        for dr in range(-REACH, REACH + 1):
            seg = REACH - dr
            to, fro = r + dr, r - dr
            to_rot = (to < HALF) & (to >= HALF - REACH) & (r >= HALF - 1)
            to_sta = (to >= HALF) & (to < HALF + REACH) & (r <= HALF)
            got = ((r < HALF) & (r >= HALF - REACH) & (fro >= HALF - 1)) | (
                (r >= HALF) & (r < HALF + REACH) & (fro <= HALF)
            )
            off = -FROM_STATOR[0] + ((r + dr) // HALF) * (FROM_STATOR[0] - FROM_ROTOR[0])
            w_x[seg] = message(
                base_x + seg, (to_rot | to_sta) & which, got, RN.at[REACH], RX.at[seg], (theta(off), r + dr)
            )

    def third(left_pack, right_pack, q):
        return jnp.where(lane < 64, roll(left_pack, -16 * q, 1), roll(right_pack, 112 - 16 * q, 1))

    halo = pl.ds(256, 128)
    for w in w_th:
        w()
    for m in range(4):
        for arr, ref in enumerate((K0, B0)):
            for q in range(8):
                ref[OWN + 8 * m + q, :, halo] = third(RT[0, m, arr], RT[1, m, arr], q)
    for w in w_t:
        w()
    send_plain()
    send_across(inner)
    def down_k(level, low, high):
        fine_k, coarse_k = levels[level - 1]["K"], levels[level]["K"]

        def body(j):
            coarse_k[j] = 0.25 * pairs(fine_k[2 * j] + fine_k[2 * j + 1], 1 << (level - 1))

        loop_rows(low, high, body, 8)

    top = axial < 7
    low_ok, high_ok = r > 0, r < NR - 1

    def coefficients(level, seg, low, high):
        A = levels[level]
        rows_level = GLOBAL_ROWS >> level
        inv = 1.0 / rows_level
        cell = 1 << level
        start = {"lo": LO + 12, "own": OWN, "hi": HI - 32}[seg] >> level
        ok = {"lo": low_ok, "own": None, "hi": high_ok}[seg]

        def body(j):
            pos = r * (ROWS >> level) + j - start
            posf = pos.astype(F32)
            hu = 0.5 * (1.0 + (posf + 1.0) * inv) * jnp.where(pos == rows_level // 2 - 1, gain, 1.0)
            hl = 0.5 * (1.0 + posf * inv) * jnp.where(pos == rows_level // 2, gain, 1.0)
            rc = 1.0 + (posf + 0.5) * inv
            hc1 = 0.5 / jnp.full((8, 128), rc, F32)
            hz1 = jnp.where(top, 0.5 * rc, 0.0)
            hc = jnp.concatenate([hc1] * 3, axis=1)
            hz = jnp.concatenate([hz1] * 3, axis=1)
            k = A["K"][j]
            ce = (k + roll(k, -cell, 1)) * hc
            cw = roll(ce, cell, 1)
            cu = (k + A["K"][j + 1]) * hu
            cl = (k + A["K"][j - 1]) * hl
            cz = (k + roll(k, -1, 0)) * hz
            cd = roll(cz, 1, 0)
            diag = cu + cl + ce + cw + cz + cd
            wd = 0.8 / diag
            if ok is not None:
                wd = jnp.where(ok, wd, 0.0)
            A["CU"][j], A["CL"][j], A["CE"][j], A["CW"][j], A["CZ"][j], A["CD"][j] = cu, cl, ce, cw, cz, cd
            A["WD"][j] = wd
            if level == 0:
                A["U"][j] = wd * A["B"][j]
                if seg == "own":
                    DG[j - OWN] = diag

        loop_rows(low, high, body, 8)

    fine = slide - NT * 256 // 2

    def weights(active, shift, count):
        out = []
        for i in range(count):
            w = jnp.where(shift == i, 1.0 - frac, 0.0) + jnp.where(shift == i - 1, frac, 0.0)
            out.append(jnp.where(active, w, 1.0 if i == 0 else 0.0))
        return out

    shifts = (fine % 4, (fine // 2) % 2, 0 * fine)
    up_w = [weights(is_rot, shifts[level], (5, 3, 2)[level]) for level in range(3)]
    low_w = [weights(is_sta, shifts[level], (5, 3, 2)[level]) for level in range(3)]

    def mix(x, w, step):
        out = w[0] * x
        for i in range(1, len(w)):
            out = out + w[i] * roll(x, i * step, x.ndim - 1)
        return out

    def ghosts(field, level):
        cell = 1 << level
        lo_end, own, own_end, hi = LO + 12 >> level, OWN >> level, GOU >> level, HI >> level
        field[own_end] = mix(field[hi], up_w[level], -cell)
        field[hi - 1] = mix(field[own_end - 1], up_w[level], cell)
        field[lo_end] = mix(field[own], low_w[level], -cell)
        field[own - 1] = mix(field[lo_end - 1], low_w[level], cell)

    def neighbours(level, field, j):
        A = levels[level]
        cell = 1 << level
        v = field[j]
        return (
            A["CU"][j] * field[j + 1]
            + A["CL"][j] * field[j - 1]
            + A["CE"][j] * roll(v, -cell, 1)
            + A["CW"][j] * roll(v, cell, 1)
            + A["CZ"][j] * roll(v, -1, 0)
            + A["CD"][j] * roll(v, 1, 0)
        )

    def first(level, low, high):
        A = levels[level]

        def body(j):
            A["U"][j] = A["WD"][j] * A["B"][j]

        loop_rows(low, high, body, 8)

    def restrict(level, low, high):
        A = levels[level]

        def body(j):
            x = 0.2 * (A["B"][2 * j] + A["B"][2 * j + 1])
            x = x + (neighbours(level, A["U"], 2 * j) + neighbours(level, A["U"], 2 * j + 1))
            levels[level + 1]["B"][j] = pairs(x, 1 << level)

        loop_rows(low, high, body, 4)

    def restrict3(rows):
        A = levels[2]
        for j in rows:
            x = None
            for i in range(2):
                row = (OWN >> 2) + 2 * j + i
                y = 0.2 * A["B"][row] + neighbours(2, A["U"], row)
                x = y if x is None else x + y
            B3S[j] = pairs(x, 4)

    own0, own1, own2 = OWN, OWN >> 1, OWN >> 2
    lo0, lo1, lo2 = LO + 12, LO + 12 >> 1, LO + 12 >> 2
    hi0, hi1, hi2 = HI, HI >> 1, HI >> 2

    down_k(1, own1, own1 + 16)
    down_k(2, own2, own2 + 8)
    coefficients(0, "own", own0 + 1, own0 + 31)
    coefficients(1, "own", own1 + 1, own1 + 15)
    coefficients(2, "own", own2 + 1, own2 + 7)
    restrict(0, own1 + 1, own1 + 15)
    first(1, own1 + 1, own1 + 15)
    restrict(1, own2 + 1, own2 + 7)
    first(2, own2 + 1, own2 + 7)
    restrict3((1, 2))

    for w in w_k:
        w()
    for w in cross_corners:
        w()
    for w in w_b:
        w()
    for j in range(12):
        for arr, ref in enumerate((K0, B0)):
            m, q = divmod(j, 8)
            ref[HI + j, :, halo] = third(RC_HI[0, m, arr], RC_HI[1, m, arr], q)
            m, q = divmod(4 + j, 8)
            ref[LO + j, :, halo] = third(RC_LO[0, m, arr], RC_LO[1, m, arr], q)

    d4 = (fine // 4) * 4
    q4 = d4 % 128
    far = d4 >= 128
    back4 = lax.rem(128 - q4, 128)

    for w in w_i:
        w()
    send_across(is_if)

    def window(tiles, sign):
        if sign > 0:
            tiles = [jnp.where(far, tiles[(i + 1) % 5], tiles[i]) for i in range(5)]
            turned = [pltpu.roll(x, back4, 1) for x in tiles]
            keep = lane < 128 - q4
            out = [jnp.where(keep, turned[i], turned[(i + 1) % 5]) for i in (0, 1, 2, 4)]
        else:
            tiles = [jnp.where(far, tiles[(i + 4) % 5], tiles[i]) for i in range(5)]
            turned = [pltpu.roll(x, q4, 1) for x in tiles]
            keep = lane >= q4
            out = [jnp.where(keep, turned[i], turned[(i + 4) % 5]) for i in (0, 1, 2, 4)]
        return out[0], out[1], jnp.where(lane < 64, out[2], out[3])

    def fill(sign, dst_k, dst_ghost):
        for j in range(28):
            if j < 24:
                ref, row = ((K0, B0)[j // 12], dst_k + j % 12)
                edge = ref[row, :, halo]
            else:
                ref, row = (K0, dst_ghost + j - 24)
                edge = third(RGH[0], RGH[1], j - 24 + (4 if sign > 0 else 0))
            a = [WC1[j, :, pl.ds(0, 128)], WC1[j, :, pl.ds(128, 128)]]
            b = [WC2[j, :, pl.ds(0, 128)], WC2[j, :, pl.ds(128, 128)]]
            tiles = a + b + [edge] if sign > 0 else a + [edge] + b
            for i, x in enumerate(window(tiles, sign)):
                ref[row, :, pl.ds(128 * i, 128)] = x

    @pl.when(is_rot)
    def _():
        fill(1, HI, GHD)
        for j in range(4):
            K0[GOU + j, :, halo] = third(RG[0], RG[1], j)

    @pl.when(is_sta)
    def _():
        fill(-1, LO, GLU)
        for j in range(4):
            K0[GOD + j, :, halo] = third(RG[0], RG[1], 4 + j)

    @pl.when(jnp.logical_not(is_rot))
    def _():
        K0[pl.ds(GOU, 4)] = K0[pl.ds(HI, 4)]
        K0[pl.ds(GHD, 4)] = K0[pl.ds(OWN + 28, 4)]

    @pl.when(jnp.logical_not(is_sta))
    def _():
        K0[pl.ds(GLU, 4)] = K0[pl.ds(OWN, 4)]
        K0[pl.ds(GOD, 4)] = K0[pl.ds(LO + 8, 4)]

    for level, low, high, end in ((1, own1, own1 + 16, PHYS >> 1), (2, own2, own2 + 8, PHYS >> 2)):
        down_k(level, 0, low)
        down_k(level, high, end)
    coefficients(0, "own", own0, own0 + 1)
    coefficients(0, "own", own0 + 31, own0 + 32)
    coefficients(0, "lo", lo0 - 11, lo0)
    coefficients(0, "hi", hi0, hi0 + 11)
    coefficients(1, "own", own1, own1 + 1)
    coefficients(1, "own", own1 + 15, own1 + 16)
    coefficients(1, "lo", lo1 - 5, lo1)
    coefficients(1, "hi", hi1, hi1 + 5)
    coefficients(2, "own", own2, own2 + 1)
    coefficients(2, "own", own2 + 7, own2 + 8)
    coefficients(2, "lo", lo2 - 2, lo2)
    coefficients(2, "hi", hi2, hi2 + 2)
    ghosts(levels[0]["U"], 0)
    for low, high in ((lo1 - 5, lo1), (own1, own1 + 1), (own1 + 15, own1 + 16), (hi1, hi1 + 5)):
        restrict(0, low, high)
    for low, high in ((lo1 - 5, lo1), (own1, own1 + 1), (own1 + 15, own1 + 16), (hi1, hi1 + 5)):
        first(1, low, high)
    ghosts(levels[1]["U"], 1)
    for low, high in ((lo2 - 2, lo2), (own2, own2 + 1), (own2 + 7, own2 + 8), (hi2, hi2 + 2)):
        restrict(1, low, high)
    for low, high in ((lo2 - 2, lo2), (own2, own2 + 1), (own2 + 7, own2 + 8), (hi2, hi2 + 2)):
        first(2, low, high)
    ghosts(levels[2]["U"], 2)
    restrict3((0, 3))

    for w in w_n.values():
        w()
    PB[...] = pack([B3S[j, :, wide] for j in range(4)])
    RB[REACH, 0] = PB[...]
    w_p = []
    for dr in (-3, 3, -2, 2, -1, 1, 0):
        inside_s = (r + dr >= 0) & (r + dr < NR)
        inside_r = (r - dr >= 0) & (r - dr < NR)
        seg = REACH - dr
        same_s = (r + dr) // HALF == side
        same_r = (r - dr) // HALF == side
        to_side = (r + dr) // HALF
        for slot in range(SLOTS):
            index = base_b + seg * SLOTS + slot
            if slot in NORMAL and (dr or slot):
                w_p.append(
                    message(
                        index, inside_s & same_s, inside_r & same_r, PB, RB.at[seg, slot], (theta(-NORMAL[slot]), r + dr)
                    )
                )
            if dr:
                off = -FROM_STATOR[slot] + to_side * (FROM_STATOR[slot] - FROM_ROTOR[slot])
                w_p.append(
                    message(
                        index,
                        inside_s & jnp.logical_not(same_s),
                        inside_r & jnp.logical_not(same_r),
                        PB,
                        RB.at[seg, slot],
                        (theta(off), r + dr),
                    )
                )

    count3 = 4 * SEGS
    d3 = (fine // 16) * 2
    sgn_x = jnp.where(side == 0, lax.rem(128 - d3, 128), lax.rem(d3 + 96, 128))

    def unpack(ref):
        tiles = [ref[:, o] for o in range(SLOTS)]
        lane7 = lax.broadcasted_iota(jnp.int32, (SEGS, 8, 128), 2) // 32
        rows = []
        for q in range(4):
            out = roll(tiles[0], -32 * q, 2)
            for o in range(1, SLOTS):
                out = jnp.where(lane7 == o, roll(tiles[o], 32 * (o - q), 2), out)
            rows.append(out)
        return jnp.stack(rows, axis=1).reshape(count3, 8, 128)

    def turn(x):
        return pltpu.roll(x, sgn_x, 2)

    for w in w_x.values():
        w()
    kn = unpack(RN)
    kx = turn(unpack(RX))

    far_off = jnp.where(near, side, 1 << 20)

    def coefficients_patch(kn, kx, rows, level, cell):
        rows_level = GLOBAL_ROWS >> level
        inv = 1.0 / rows_level
        pos = (r - REACH) * (ROWS >> level) + lax.broadcasted_iota(jnp.int32, (rows, 8, 128), 0)
        ok = (pos >= 0) & (pos < rows_level)
        beyond = (pos - rows_level // 2) * (1 - 2 * side) >= far_off
        posf = pos.astype(F32)
        hu = 0.5 * (1.0 + (posf + 1.0) * inv) * jnp.where(pos == rows_level // 2 - 1, gain, 1.0)
        hl = 0.5 * (1.0 + posf * inv) * jnp.where(pos == rows_level // 2, gain, 1.0)
        rc = 1.0 + (posf + 0.5) * inv
        hc = 0.5 / rc
        hz = jnp.where(lax.broadcasted_iota(jnp.int32, (rows, 8, 128), 1) < 7, 0.5 * rc, 0.0)
        k = jnp.where(beyond, kx, kn)
        ku = jnp.where(beyond, jnp.concatenate([kx[1:], kx[:1]], 0), jnp.concatenate([kn[1:], kn[:1]], 0))
        kd = jnp.where(beyond, jnp.concatenate([kx[-1:], kx[:-1]], 0), jnp.concatenate([kn[-1:], kn[:-1]], 0))
        ku = jnp.where(pos == rows_level - 1, 0.0, ku)
        kd = jnp.where(pos == 0, 0.0, kd)
        ce = (k + roll(k, -cell, 2)) * hc
        cw = roll(ce, cell, 2)
        cu = (k + ku) * hu
        cl = (k + kd) * hl
        cz = (k + roll(k, -1, 1)) * hz
        cd = roll(cz, 1, 1)
        wd = jnp.where(ok, 0.8 / (cu + cl + ce + cw + cz + cd), 0.0)
        return (cu, cl, ce, cw, cz, cd, wd, beyond)

    def coarse_k(x):
        y = x.reshape(x.shape[0] // 2, 2, 8, 128)
        return 0.25 * pairs(y[:, 0] + y[:, 1], 1)

    C3 = coefficients_patch(kn, kx, count3, 3, 1)
    C4 = coefficients_patch(coarse_k(kn), coarse_k(kx), count3 // 2, 4, 2)

    odd = (fine // 8) % 2
    w3 = weights(r >= 0, odd, 3)
    w4 = weights(r >= 0, 0 * odd, 2)

    def neighbours_patch(C, v, step, w, cell):
        n = v.shape[0]
        edge = lax.rem(HALF - r + REACH + 4 * SEGS, SEGS) * step
        VP[pl.ds(0, n)] = v
        over = mix(VP[edge], w, -cell)
        under = mix(VP[lax.rem(edge + n - 1, n)], w, cell)
        row = lax.broadcasted_iota(jnp.int32, v.shape, 0)
        vu = jnp.concatenate([v[1:], v[:1]], 0)
        vd = jnp.concatenate([v[-1:], v[:-1]], 0)
        mark = jnp.where(near, edge, -8)
        vu = jnp.where(row == mark - 1, over[None], vu)
        vd = jnp.where(row == mark, under[None], vd)
        return (
            C[0] * vu
            + C[1] * vd
            + C[2] * roll(v, -cell, 2)
            + C[3] * roll(v, cell, 2)
            + C[4] * roll(v, -1, 1)
            + C[5] * roll(v, 1, 1)
        )

    for w in w_p:
        w()
    b3 = unpack(RB)
    b3 = jnp.where(C3[7], turn(b3), b3)
    u3 = C3[6] * b3
    x = 0.2 * b3 + neighbours_patch(C3, u3, 4, w3, 1)
    x = x.reshape(count3 // 2, 2, 8, 128)
    b4 = pairs(x[:, 0] + x[:, 1], 1)
    v4 = C4[6] * b4
    for _ in range(3):
        v4 = 0.2 * v4 + C4[6] * (b4 + neighbours_patch(C4, v4, 2, w4, 2))
    up4 = jnp.broadcast_to(v4[:, None], (count3 // 2, 2, 8, 128)).reshape(count3, 8, 128)
    v3 = u3 + up4
    e3 = 0.2 * v3 + C3[6] * (b3 + neighbours_patch(C3, v3, 4, w3, 1))

    delta = (fine // 4) % 4 * 4
    first_row = 4 * REACH - 1
    for j in range(6):
        if j == 0:
            shift = jnp.where(is_sta, -delta, 0)
        elif j == 5:
            shift = jnp.where(is_rot, delta, 0)
        else:
            shift = 0
        for i in range(3):
            signed = lane + 128 * i
            if i == 2:
                signed = jnp.where(lane < 64, signed, signed - LANES)
            index = ((signed + shift + 1024) // 8) % 128
            E3S[j, :, pl.ds(128 * i, 128)] = jnp.take_along_axis(e3[first_row + j], index, axis=1)

    for level in (2, 1, 0):
        A = levels[level]
        low, own, hi = LO + 12 >> level, OWN >> level, HI >> level
        rows = ROWS >> level
        if level == 2:
            A["U"][low - 2] = A["U"][low - 2] + E3S[0]
            A["U"][low - 1] = A["U"][low - 1] + E3S[0]
            for j in range(rows):
                A["U"][own + j] = A["U"][own + j] + E3S[1 + j // 2]
            A["U"][hi] = A["U"][hi] + E3S[5]
            A["U"][hi + 1] = A["U"][hi + 1] + E3S[5]
        else:
            E = levels[level + 1]["E"]

            def add(j, A=A, E=E):
                e = E[j]
                A["U"][2 * j] = A["U"][2 * j] + e
                A["U"][2 * j + 1] = A["U"][2 * j + 1] + e

            add((low >> 1) - 1)
            loop_rows(own >> 1, (own + rows) >> 1, add, 4)
            add(hi >> 1)
        ghosts(A["U"], level)

        def smooth(j, A=A, level=level):
            A["E"][j] = 0.2 * A["U"][j] + A["WD"][j] * (A["B"][j] + neighbours(level, A["U"], j))

        smooth(low - 1)
        loop_rows(own, own + rows, smooth, 8)
        smooth(hi)

    ghosts(levels[0]["E"], 0)

    def finish(j):
        E = levels[0]["E"]
        p = E[OWN + j]
        out = B0[OWN + j] - DG[j] * p + neighbours(0, E, OWN + j)
        for half in range(2):
            place = pl.ds(tile_row(j, half), 8, stride=2 * ROWS)
            p_ref[place, :] = p[:, 128 * half : 128 * half + 128]
            res_ref[place, :] = out[:, 128 * half : 128 * half + 128]

    loop_rows(0, ROWS, finish, 8)

    for send, copy in messages:
        pl.when(send)(copy.wait_send)


def on_device(source, conductance, slide, fraction, gain):
    nz, rows, columns = source.shape
    scratch = []
    for level in range(3):
        scratch += [pltpu.VMEM((PHYS >> level, nz, LANES), F32)] * len(PER_LEVEL)
    tile = (8, 128)
    scratch += [
        pltpu.VMEM((ROWS, nz, LANES), F32),
        pltpu.VMEM((4, nz, LANES), F32),
        pltpu.VMEM((2, 4, 2) + tile, F32),
        pltpu.VMEM((2, 4, 2) + tile, F32),
        pltpu.VMEM((2, 2, 2) + tile, F32),
        pltpu.VMEM((2, 2, 2) + tile, F32),
        pltpu.VMEM((2,) + tile, F32),
        pltpu.VMEM((2,) + tile, F32),
        pltpu.VMEM((28, nz, 256), F32),
        pltpu.VMEM((28, nz, 256), F32),
        pltpu.VMEM(tile, F32),
        pltpu.VMEM(tile, F32),
        pltpu.VMEM((SEGS, SLOTS) + tile, F32),
        pltpu.VMEM((SEGS, SLOTS) + tile, F32),
        pltpu.VMEM((SEGS, SLOTS) + tile, F32),
        pltpu.VMEM((4 * SEGS,) + tile, F32),
        pltpu.VMEM((6, nz, LANES), F32),
        pltpu.VMEM((nz * rows * columns // 128, 128), F32),
        pltpu.VMEM((nz * rows * columns // 128, 128), F32),
    ]
    sems = 24 + 2 * SEGS + SEGS * SLOTS
    scratch += [pltpu.SemaphoreType.DMA((n,)) for n in (sems, sems, 2)]
    vmem = pl.BlockSpec(memory_space=pltpu.VMEM)
    smem = pl.BlockSpec(memory_space=pltpu.SMEM)
    hbm = pl.BlockSpec(memory_space=pltpu.HBM)
    flat = jax.ShapeDtypeStruct((nz * rows * columns // 128, 128), F32)
    large = [pltpu.with_memory_space_constraint(to_tiles(x), pltpu.HBM) for x in (source, conductance)]
    operands = (slide, fraction, gain, *large)
    pressure, residual = pl.pallas_call(
        kernel,
        out_shape=(flat, flat),
        in_specs=[smem] * 3 + [hbm] * 2,
        out_specs=(vmem, vmem),
        scratch_shapes=scratch,
        compiler_params=pltpu.CompilerParams(
            collective_id=0, has_side_effects=True, vmem_limit_bytes=48 * 1024 * 1024
        ),
    )(*operands)
    return from_tiles(pressure, source.shape), from_tiles(residual, source.shape)


def solution(mesh):
    spec = P(None, "rad", "theta")
    return jax.shard_map(
        on_device, mesh=mesh, in_specs=(spec, spec, P(), P(), P()), out_specs=(spec, spec), check_vma=False
    )
```

```python
import functools

import jax
import jax.numpy as jnp
from jax import lax
from jax.experimental import pallas as pl
from jax.experimental.pallas import tpu as pltpu
from jax.sharding import PartitionSpec as P

MESH = pl.DeviceIdType.MESH
F32 = jnp.float32
NT, NR = 16, 32
HALF = NR // 2
ROWS = 32
GLOBAL_ROWS = NR * ROWS
LANES = 384
LO, GLU, GOD, OWN, GOU, GHD, HI, PHYS = 0, 12, 16, 20, 52, 56, 60, 72
REACH = 3
SEGS = 2 * REACH + 1
SLOTS = 4
NORMAL = {0: 0, 1: 1, 3: -1}
FROM_STATOR = (8, 9, 10, 7)
FROM_ROTOR = (-9, -8, -7, -10)
PER_LEVEL = ("K", "B", "U", "CU", "CL", "CE", "CW", "CZ", "CD", "WD", "E")


def roll(x, shift, axis):
    size = x.shape[axis]
    shift = shift % size
    return x if shift == 0 else pltpu.roll(x, shift, axis)


def tile_row(j, half):
    return (j // 8) * 16 + half * 8 + j % 8


def to_tiles(x):
    nz, rows, columns = x.shape
    x = x.reshape(nz, rows // 8, 8, columns // 128, 128)
    return x.transpose(0, 1, 3, 2, 4).reshape(nz * rows * columns // 128, 128)


def from_tiles(x, shape):
    nz, rows, columns = shape
    x = x.reshape(nz, rows // 8, columns // 128, 8, 128)
    return x.transpose(0, 1, 3, 2, 4).reshape(shape)


def loop_rows(low, high, body, unroll):
    count = (high - low) // unroll

    def step(i, carry):
        for q in range(unroll):
            body(low + i * unroll + q)
        return carry

    if count:
        lax.fori_loop(0, count, step, 0)
    for j in range(low + count * unroll, high):
        body(j)


def kernel(*refs):
    slide_ref, frac_ref, gain_ref, b_hbm, k_hbm, p_ref, res_ref = refs[:7]
    at = 7
    levels = []
    for _ in range(3):
        levels.append(dict(zip(PER_LEVEL, refs[at : at + len(PER_LEVEL)])))
        at += len(PER_LEVEL)
    (DG, B3S, EP, RT, RC_HI, RC_LO, RG, RGH, WC1, WC2, PK, PB, RN, RX, RB, VP, E3S) = refs[at : at + 17]
    k_ref, b_ref, sem_s, sem_r, sem_in = refs[at + 17 :]

    moves = ((k_hbm, k_ref), (b_hbm, b_ref))
    loads = [pltpu.make_async_copy(x, y, sem_in.at[i]) for i, (x, y) in enumerate(moves)]
    for load in loads:
        load.start()

    t = lax.axis_index("theta")
    r = lax.axis_index("rad")
    side = r // HALF
    is_rot = r == HALF - 1
    is_sta = r == HALF
    is_if = is_rot | is_sta
    near = (r >= HALF - REACH) & (r < HALF + REACH)

    def theta(offset):
        return lax.rem(t + offset + 2 * NT, NT)

    lane = lax.broadcasted_iota(jnp.int32, (8, 128), 1)
    lane3 = lax.broadcasted_iota(jnp.int32, (8, LANES), 1)
    axial = lax.broadcasted_iota(jnp.int32, (8, 128), 0)
    K0, B0 = levels[0]["K"], levels[0]["B"]

    zeros3 = jnp.zeros((12, 8, LANES), F32)

    @pl.when(r == 0)
    def _():
        K0[pl.ds(LO, 12)] = zeros3
        B0[pl.ds(LO, 12)] = zeros3

    @pl.when(r == NR - 1)
    def _():
        K0[pl.ds(HI, 12)] = zeros3
        B0[pl.ds(HI, 12)] = zeros3

    RC_LO[...] = jnp.zeros_like(RC_LO)
    RC_HI[...] = jnp.zeros_like(RC_HI)
    RN[...] = jnp.ones_like(RN)
    RX[...] = jnp.ones_like(RX)
    RB[...] = jnp.zeros_like(RB)

    barrier = pltpu.get_barrier_semaphore()
    sgn = 1 - 2 * side
    inner = near & jnp.logical_not(is_if)
    greet, heard = [], []

    def meet(cond, dt, dr):
        greet.append((cond, dt, dr))
        heard.append(cond)

    for dr in (1, 2, 3):
        far_dr = dr * sgn
        to_inner = is_if & (dr > 1)
        from_if = inner & ((r + far_dr == HALF - 1) | (r + far_dr == HALF)) & ((r + far_dr) // HALF != side)
        for o in range(7, 11):
            if dr > 1:
                greet.append((to_inner, sgn * o, far_dr))
            heard.append(from_if)
    for o in range(7, 11):
        meet(is_if, sgn * o, sgn)
        meet((r == HALF - 2) | (r == HALF + 1), sgn * o, 3 * sgn)
    for o in range(6, 11):
        meet(is_if, o, 0)
    for dr in (-3, 3, -2, 2, -1, 1, 0):
        inside = (r + dr >= 0) & (r + dr < NR)
        for dt in (-1, 1, 0) if abs(dr) < 2 else (0,):
            if dr or dt:
                meet(inside, dt, dr)
    for o in (-2, 2):
        meet(near, o, 0)
    for cond, dt, dr in greet:
        peer = (theta(dt), r + dr)

        @pl.when(cond)
        def _(peer=peer):
            pl.semaphore_signal(barrier, inc=1, device_id=peer, device_id_type=MESH)

    for arr, (src, dst) in enumerate(((k_ref, K0), (b_ref, B0))):
        loads[arr].wait()

        def move(j, src=src, dst=dst):
            for half in range(2):
                dst[OWN + j, :, pl.ds(128 * half, 128)] = src[pl.ds(tile_row(j, half), 8, stride=2 * ROWS), :]

        loop_rows(0, ROWS, move, ROWS)
        for m in range(4):
            left = right = None
            for q in range(8):
                row = OWN + 8 * m + q
                low = roll(dst[row, :, pl.ds(0, 128)], 16 * q, 1)
                high = roll(dst[row, :, pl.ds(128, 128)], 16 * q + 16, 1)
                here = lane // 16 == q
                left = low if q == 0 else jnp.where(here, low, left)
                right = high if q == 0 else jnp.where(here, high, right)
            EP[0, m, arr] = left
            EP[1, m, arr] = right

    pl.semaphore_wait(barrier, sum(cond.astype(jnp.int32) for cond in heard))

    messages = []

    def message(index, send, recv, src, dst, target, start=True):
        copy = pltpu.make_async_remote_copy(
            src_ref=src,
            dst_ref=dst,
            send_sem=sem_s.at[index],
            recv_sem=sem_r.at[index],
            device_id=target,
            device_id_type=MESH,
        )
        if start:
            pl.when(send)(copy.start)
        messages.append((send, copy))
        return lambda: pl.when(recv)(copy.wait_recv)

    always = r >= 0
    down_s, down_r = (r >= 1) & (r != HALF), (r < NR - 1) & (r != HALF - 1)
    up_s, up_r = down_r, down_s
    wide = pl.ds(0, 256)
    w_th = [
        message(0, always, always, EP.at[0], RT.at[0], (theta(-1), r)),
        message(1, always, always, EP.at[1], RT.at[1], (theta(1), r)),
    ]
    w_k = [
        message(2, down_s, down_r, K0.at[pl.ds(OWN, 12), :, wide], K0.at[pl.ds(HI, 12), :, wide], (t, r - 1)),
        message(3, up_s, up_r, K0.at[pl.ds(OWN + 20, 12), :, wide], K0.at[pl.ds(LO, 12), :, wide], (t, r + 1)),
        message(4, down_s, down_r, EP.at[0, pl.ds(0, 2)], RC_HI.at[0], (theta(-1), r - 1)),
        message(5, down_s, down_r, EP.at[1, pl.ds(0, 2)], RC_HI.at[1], (theta(1), r - 1)),
        message(6, up_s, up_r, EP.at[0, pl.ds(2, 2)], RC_LO.at[0], (theta(-1), r + 1)),
        message(7, up_s, up_r, EP.at[1, pl.ds(2, 2)], RC_LO.at[1], (theta(1), r + 1)),
    ]
    w_b = [
        message(8, down_s, down_r, B0.at[pl.ds(OWN, 12), :, wide], B0.at[pl.ds(HI, 12), :, wide], (t, r - 1)),
        message(9, up_s, up_r, B0.at[pl.ds(OWN + 20, 12), :, wide], B0.at[pl.ds(LO, 12), :, wide], (t, r + 1)),
    ]
    w_i = []

    th = {o: theta(o) for o in (-1, 1, 8)}
    th_far = {"g2": theta(-9 * sgn), "ge": theta(-10 + 17 * side), "gw": theta(-7 + 17 * side), "c2": theta(9 * sgn)}

    facing = OWN + 20 * (1 - side)
    facing4 = OWN + 28 * (1 - side)
    group4 = 3 * (1 - side)
    other = NR - 1 - r
    ghost = GOD + (GOU - GOD) * side
    own4 = K0.at[pl.ds(facing4, 4), :, wide]
    items = [
        (own4, K0.at[pl.ds(ghost, 4), :, wide], (t, other)),
        (EP.at[0, group4, 0], RG.at[0], (th[-1], other)),
        (EP.at[1, group4, 0], RG.at[1], (th[1], other)),
        (own4, WC1.at[pl.ds(24, 4)], (th[8], r)),
        (own4, WC2.at[pl.ds(24, 4)], (th_far["g2"], r)),
        (EP.at[0, group4, 0], RGH.at[0], (th_far["ge"], r)),
        (EP.at[1, group4, 0], RGH.at[1], (th_far["gw"], r)),
        (K0.at[pl.ds(facing, 12), :, wide], WC1.at[pl.ds(0, 12)], (th[8], other)),
        (K0.at[pl.ds(facing, 12), :, wide], WC2.at[pl.ds(0, 12)], (th_far["c2"], other)),
        (B0.at[pl.ds(facing, 12), :, wide], WC1.at[pl.ds(12, 12)], (th[8], other)),
        (B0.at[pl.ds(facing, 12), :, wide], WC2.at[pl.ds(12, 12)], (th_far["c2"], other)),
    ]
    for n, (src, dst, target) in enumerate(items):
        w_i.append(message(10 + n, is_if, is_if, src, dst, target))

    cross_corners = []
    for part, (cond, dst, first) in enumerate(((is_sta, RC_HI, 0), (is_rot, RC_LO, 2))):
        other = r - 1 if part == 0 else r + 1
        offs = (-10, -7) if part == 0 else (7, 10)
        got = is_rot if part == 0 else is_sta
        for e in range(2):
            cross_corners.append(
                message(
                    (4 if part == 0 else 6) + e,
                    cond,
                    got,
                    EP.at[e, pl.ds(first, 2)],
                    dst.at[e],
                    (theta(offs[e]), other),
                )
            )

    slide = slide_ref[0]
    frac = frac_ref[0]
    gain = gain_ref[0]

    def pairs(x, cell):
        width = x.shape[-1]
        pick = (lax.broadcasted_iota(jnp.int32, x.shape, x.ndim - 1) // cell) % 2 == 1
        return x + jnp.where(pick, roll(x, cell, x.ndim - 1), roll(x, width - cell, x.ndim - 1))

    gather_index = (lane % 16) * 8

    def pack(rows):
        out = None
        for q, x in enumerate(rows):
            for half in range(2):
                part = jnp.take_along_axis(x[:, 128 * half : 128 * half + 128], gather_index, axis=1)
                out = part if out is None else jnp.where(lane // 16 == 2 * q + half, part, out)
        return out

    own3 = []
    for j in range(4):
        k2 = []
        for i in range(2):
            k1 = []
            for h in range(2):
                row = OWN + 8 * j + 4 * i + 2 * h
                k1.append(0.25 * pairs(K0[row, :, wide] + K0[row + 1, :, wide], 1))
            k2.append(0.25 * pairs(k1[0] + k1[1], 2))
        own3.append(0.25 * pairs(k2[0] + k2[1], 4))
    PK[...] = pack(own3)

    RN[REACH, 0] = PK[...]
    base_t, base_n, base_x, base_b = 21, 24, 24 + SEGS, 24 + 2 * SEGS
    w_t = [
        message(base_t, always, always, PK, RN.at[REACH, 1], (theta(-1), r)),
        message(base_t + 1, always, always, PK, RN.at[REACH, 3], (theta(1), r)),
        message(base_t + 2, near, near, PK, RN.at[REACH, 2], (theta(-2), r)),
    ]

    w_n, w_x = {}, {}

    def send_plain():
        for dr in (-3, 3, -2, 2, -1, 1):
            inside_s = (r + dr >= 0) & (r + dr < NR)
            inside_r = (r - dr >= 0) & (r - dr < NR)
            seg = REACH - dr
            w_n[seg] = message(base_n + seg, inside_s, inside_r, RN.at[REACH], RN.at[seg], (t, r + dr))

    def send_across(which):
        for dr in range(-REACH, REACH + 1):
            seg = REACH - dr
            to, fro = r + dr, r - dr
            to_rot = (to < HALF) & (to >= HALF - REACH) & (r >= HALF - 1)
            to_sta = (to >= HALF) & (to < HALF + REACH) & (r <= HALF)
            got = ((r < HALF) & (r >= HALF - REACH) & (fro >= HALF - 1)) | (
                (r >= HALF) & (r < HALF + REACH) & (fro <= HALF)
            )
            off = -FROM_STATOR[0] + ((r + dr) // HALF) * (FROM_STATOR[0] - FROM_ROTOR[0])
            w_x[seg] = message(
                base_x + seg, (to_rot | to_sta) & which, got, RN.at[REACH], RX.at[seg], (theta(off), r + dr)
            )

    def third(left_pack, right_pack, q):
        return jnp.where(lane < 64, roll(left_pack, -16 * q, 1), roll(right_pack, 112 - 16 * q, 1))

    halo = pl.ds(256, 128)
    for w in w_th:
        w()
    for m in range(4):
        for arr, ref in enumerate((K0, B0)):
            for q in range(8):
                ref[OWN + 8 * m + q, :, halo] = third(RT[0, m, arr], RT[1, m, arr], q)
    for w in w_t:
        w()
    send_plain()
    send_across(inner)
    def down_k(level, low, high):
        fine_k, coarse_k = levels[level - 1]["K"], levels[level]["K"]

        def body(j):
            coarse_k[j] = 0.25 * pairs(fine_k[2 * j] + fine_k[2 * j + 1], 1 << (level - 1))

        loop_rows(low, high, body, 8)

    top = axial < 7
    low_ok, high_ok = r > 0, r < NR - 1

    def coefficients(level, seg, low, high, unroll=8):
        A = levels[level]
        rows_level = GLOBAL_ROWS >> level
        inv = 1.0 / rows_level
        cell = 1 << level
        start = {"lo": LO + 12, "own": OWN, "hi": HI - 32}[seg] >> level
        ok = {"lo": low_ok, "own": None, "hi": high_ok}[seg]

        def body(j):
            pos = r * (ROWS >> level) + j - start
            posf = pos.astype(F32)
            hu = 0.5 * (1.0 + (posf + 1.0) * inv) * jnp.where(pos == rows_level // 2 - 1, gain, 1.0)
            hl = 0.5 * (1.0 + posf * inv) * jnp.where(pos == rows_level // 2, gain, 1.0)
            rc = 1.0 + (posf + 0.5) * inv
            hc1 = 0.5 / jnp.full((8, 128), rc, F32)
            hz1 = jnp.where(top, 0.5 * rc, 0.0)
            hc = jnp.concatenate([hc1] * 3, axis=1)
            hz = jnp.concatenate([hz1] * 3, axis=1)
            k = A["K"][j]
            ce = (k + roll(k, -cell, 1)) * hc
            cw = roll(ce, cell, 1)
            cu = (k + A["K"][j + 1]) * hu
            cl = (k + A["K"][j - 1]) * hl
            cz = (k + roll(k, -1, 0)) * hz
            cd = roll(cz, 1, 0)
            diag = cu + cl + ce + cw + cz + cd
            wd = 0.8 / diag
            if ok is not None:
                wd = jnp.where(ok, wd, 0.0)
            A["CU"][j], A["CL"][j], A["CE"][j], A["CW"][j], A["CZ"][j], A["CD"][j] = cu, cl, ce, cw, cz, cd
            A["WD"][j] = wd
            if level == 0:
                A["U"][j] = wd * A["B"][j]
                if seg == "own":
                    DG[j - OWN] = diag

        loop_rows(low, high, body, unroll)

    fine = slide - NT * 256 // 2

    def weights(active, shift, count):
        out = []
        for i in range(count):
            w = jnp.where(shift == i, 1.0 - frac, 0.0) + jnp.where(shift == i - 1, frac, 0.0)
            out.append(jnp.where(active, w, 1.0 if i == 0 else 0.0))
        return out

    shifts = (fine % 4, (fine // 2) % 2, 0 * fine)
    up_w = [weights(is_rot, shifts[level], (5, 3, 2)[level]) for level in range(3)]
    low_w = [weights(is_sta, shifts[level], (5, 3, 2)[level]) for level in range(3)]

    def mix(x, w, step):
        out = w[0] * x
        for i in range(1, len(w)):
            out = out + w[i] * roll(x, i * step, x.ndim - 1)
        return out

    def ghosts(field, level):
        cell = 1 << level
        lo_end, own, own_end, hi = LO + 12 >> level, OWN >> level, GOU >> level, HI >> level
        field[own_end] = mix(field[hi], up_w[level], -cell)
        field[hi - 1] = mix(field[own_end - 1], up_w[level], cell)
        field[lo_end] = mix(field[own], low_w[level], -cell)
        field[own - 1] = mix(field[lo_end - 1], low_w[level], cell)

    def neighbours(level, field, j):
        A = levels[level]
        cell = 1 << level
        v = field[j]
        return (
            A["CU"][j] * field[j + 1]
            + A["CL"][j] * field[j - 1]
            + A["CE"][j] * roll(v, -cell, 1)
            + A["CW"][j] * roll(v, cell, 1)
            + A["CZ"][j] * roll(v, -1, 0)
            + A["CD"][j] * roll(v, 1, 0)
        )

    def first(level, low, high):
        A = levels[level]

        def body(j):
            A["U"][j] = A["WD"][j] * A["B"][j]

        loop_rows(low, high, body, 8)

    def restrict(level, low, high):
        A = levels[level]

        def body(j):
            x = 0.2 * (A["B"][2 * j] + A["B"][2 * j + 1])
            x = x + (neighbours(level, A["U"], 2 * j) + neighbours(level, A["U"], 2 * j + 1))
            levels[level + 1]["B"][j] = pairs(x, 1 << level)

        loop_rows(low, high, body, 4)

    def restrict3(rows):
        A = levels[2]
        for j in rows:
            x = None
            for i in range(2):
                row = (OWN >> 2) + 2 * j + i
                y = 0.2 * A["B"][row] + neighbours(2, A["U"], row)
                x = y if x is None else x + y
            B3S[j] = pairs(x, 4)

    own0, own1, own2 = OWN, OWN >> 1, OWN >> 2
    lo0, lo1, lo2 = LO + 12, LO + 12 >> 1, LO + 12 >> 2
    hi0, hi1, hi2 = HI, HI >> 1, HI >> 2

    down_k(1, own1, own1 + 16)
    down_k(2, own2, own2 + 8)
    coefficients(0, "own", own0 + 1, own0 + 31)
    coefficients(1, "own", own1 + 1, own1 + 15)
    coefficients(2, "own", own2 + 1, own2 + 7)
    restrict(0, own1 + 1, own1 + 15)
    first(1, own1 + 1, own1 + 15)
    restrict(1, own2 + 1, own2 + 7)
    first(2, own2 + 1, own2 + 7)
    restrict3((1, 2))

    for w in w_k:
        w()
    for w in cross_corners:
        w()
    for w in w_b:
        w()
    for j in range(12):
        for arr, ref in enumerate((K0, B0)):
            m, q = divmod(j, 8)
            ref[HI + j, :, halo] = third(RC_HI[0, m, arr], RC_HI[1, m, arr], q)
            m, q = divmod(4 + j, 8)
            ref[LO + j, :, halo] = third(RC_LO[0, m, arr], RC_LO[1, m, arr], q)

    d4 = (fine // 4) * 4
    q4 = d4 % 128
    far = d4 >= 128
    back4 = lax.rem(128 - q4, 128)

    for w in w_i:
        w()
    send_across(is_if)

    def window(tiles, sign):
        if sign > 0:
            tiles = [jnp.where(far, tiles[(i + 1) % 5], tiles[i]) for i in range(5)]
            turned = [pltpu.roll(x, back4, 1) for x in tiles]
            keep = lane < 128 - q4
            out = [jnp.where(keep, turned[i], turned[(i + 1) % 5]) for i in (0, 1, 2, 4)]
        else:
            tiles = [jnp.where(far, tiles[(i + 4) % 5], tiles[i]) for i in range(5)]
            turned = [pltpu.roll(x, q4, 1) for x in tiles]
            keep = lane >= q4
            out = [jnp.where(keep, turned[i], turned[(i + 4) % 5]) for i in (0, 1, 2, 4)]
        return out[0], out[1], jnp.where(lane < 64, out[2], out[3])

    def fill(sign, dst_k, dst_ghost):
        for j in range(28):
            if j < 24:
                ref, row = ((K0, B0)[j // 12], dst_k + j % 12)
                edge = ref[row, :, halo]
            else:
                ref, row = (K0, dst_ghost + j - 24)
                edge = third(RGH[0], RGH[1], j - 24 + (4 if sign > 0 else 0))
            a = [WC1[j, :, pl.ds(0, 128)], WC1[j, :, pl.ds(128, 128)]]
            b = [WC2[j, :, pl.ds(0, 128)], WC2[j, :, pl.ds(128, 128)]]
            tiles = a + b + [edge] if sign > 0 else a + [edge] + b
            for i, x in enumerate(window(tiles, sign)):
                ref[row, :, pl.ds(128 * i, 128)] = x

    @pl.when(is_rot)
    def _():
        fill(1, HI, GHD)
        for j in range(4):
            K0[GOU + j, :, halo] = third(RG[0], RG[1], j)

    @pl.when(is_sta)
    def _():
        fill(-1, LO, GLU)
        for j in range(4):
            K0[GOD + j, :, halo] = third(RG[0], RG[1], 4 + j)

    @pl.when(jnp.logical_not(is_rot))
    def _():
        K0[pl.ds(GOU, 4)] = K0[pl.ds(HI, 4)]
        K0[pl.ds(GHD, 4)] = K0[pl.ds(OWN + 28, 4)]

    @pl.when(jnp.logical_not(is_sta))
    def _():
        K0[pl.ds(GLU, 4)] = K0[pl.ds(OWN, 4)]
        K0[pl.ds(GOD, 4)] = K0[pl.ds(LO + 8, 4)]

    for level, low, high, end in ((1, own1, own1 + 16, PHYS >> 1), (2, own2, own2 + 8, PHYS >> 2)):
        down_k(level, 0, low)
        down_k(level, high, end)
    coefficients(0, "own", own0, own0 + 1)
    coefficients(0, "own", own0 + 31, own0 + 32)
    coefficients(0, "lo", lo0 - 11, lo0)
    coefficients(0, "hi", hi0, hi0 + 11)
    coefficients(1, "own", own1, own1 + 1)
    coefficients(1, "own", own1 + 15, own1 + 16)
    coefficients(1, "lo", lo1 - 5, lo1)
    coefficients(1, "hi", hi1, hi1 + 5)
    coefficients(2, "own", own2, own2 + 1)
    coefficients(2, "own", own2 + 7, own2 + 8)
    coefficients(2, "lo", lo2 - 2, lo2)
    coefficients(2, "hi", hi2, hi2 + 2)
    ghosts(levels[0]["U"], 0)
    for low, high in ((lo1 - 5, lo1), (own1, own1 + 1), (own1 + 15, own1 + 16), (hi1, hi1 + 5)):
        restrict(0, low, high)
    for low, high in ((lo1 - 5, lo1), (own1, own1 + 1), (own1 + 15, own1 + 16), (hi1, hi1 + 5)):
        first(1, low, high)
    ghosts(levels[1]["U"], 1)
    for low, high in ((lo2 - 2, lo2), (own2, own2 + 1), (own2 + 7, own2 + 8), (hi2, hi2 + 2)):
        restrict(1, low, high)
    for low, high in ((lo2 - 2, lo2), (own2, own2 + 1), (own2 + 7, own2 + 8), (hi2, hi2 + 2)):
        first(2, low, high)
    ghosts(levels[2]["U"], 2)
    restrict3((0, 3))

    PB[...] = pack([B3S[j, :, wide] for j in range(4)])
    RB[REACH, 0] = PB[...]
    w_p = []
    for dr in (-3, 3, -2, 2, -1, 1, 0):
        inside_s = (r + dr >= 0) & (r + dr < NR)
        inside_r = (r - dr >= 0) & (r - dr < NR)
        seg = REACH - dr
        same_s = (r + dr) // HALF == side
        same_r = (r - dr) // HALF == side
        to_side = (r + dr) // HALF
        for slot in range(SLOTS):
            index = base_b + seg * SLOTS + slot
            if slot in NORMAL and (dr or slot):
                w_p.append(
                    message(
                        index, inside_s & same_s, inside_r & same_r, PB, RB.at[seg, slot], (theta(-NORMAL[slot]), r + dr)
                    )
                )
            if dr:
                off = -FROM_STATOR[slot] + to_side * (FROM_STATOR[slot] - FROM_ROTOR[slot])
                w_p.append(
                    message(
                        index,
                        inside_s & jnp.logical_not(same_s),
                        inside_r & jnp.logical_not(same_r),
                        PB,
                        RB.at[seg, slot],
                        (theta(off), r + dr),
                    )
                )

    count3 = 4 * SEGS
    d3 = (fine // 16) * 2
    sgn_x = jnp.where(side == 0, lax.rem(128 - d3, 128), lax.rem(d3 + 96, 128))

    def unpack(ref):
        tiles = [ref[:, o] for o in range(SLOTS)]
        lane7 = lax.broadcasted_iota(jnp.int32, (SEGS, 8, 128), 2) // 32
        rows = []
        for q in range(4):
            out = roll(tiles[0], -32 * q, 2)
            for o in range(1, SLOTS):
                out = jnp.where(lane7 == o, roll(tiles[o], 32 * (o - q), 2), out)
            rows.append(out)
        return jnp.stack(rows, axis=1).reshape(count3, 8, 128)

    def turn(x):
        return pltpu.roll(x, sgn_x, 2)

    for w in list(w_x.values()) + list(w_n.values()):
        w()
    kn = unpack(RN)
    kx = turn(unpack(RX))

    far_off = jnp.where(near, side, 1 << 20)

    def coefficients_patch(kn, kx, rows, level, cell):
        rows_level = GLOBAL_ROWS >> level
        inv = 1.0 / rows_level
        pos = (r - REACH) * (ROWS >> level) + lax.broadcasted_iota(jnp.int32, (rows, 8, 128), 0)
        ok = (pos >= 0) & (pos < rows_level)
        beyond = (pos - rows_level // 2) * (1 - 2 * side) >= far_off
        posf = pos.astype(F32)
        hu = 0.5 * (1.0 + (posf + 1.0) * inv) * jnp.where(pos == rows_level // 2 - 1, gain, 1.0)
        hl = 0.5 * (1.0 + posf * inv) * jnp.where(pos == rows_level // 2, gain, 1.0)
        rc = 1.0 + (posf + 0.5) * inv
        hc = 0.5 / rc
        hz = jnp.where(lax.broadcasted_iota(jnp.int32, (rows, 8, 128), 1) < 7, 0.5 * rc, 0.0)
        k = jnp.where(beyond, kx, kn)
        ku = jnp.where(beyond, jnp.concatenate([kx[1:], kx[:1]], 0), jnp.concatenate([kn[1:], kn[:1]], 0))
        kd = jnp.where(beyond, jnp.concatenate([kx[-1:], kx[:-1]], 0), jnp.concatenate([kn[-1:], kn[:-1]], 0))
        ku = jnp.where(pos == rows_level - 1, 0.0, ku)
        kd = jnp.where(pos == 0, 0.0, kd)
        ce = (k + roll(k, -cell, 2)) * hc
        cw = roll(ce, cell, 2)
        cu = (k + ku) * hu
        cl = (k + kd) * hl
        cz = (k + roll(k, -1, 1)) * hz
        cd = roll(cz, 1, 1)
        wd = jnp.where(ok, 0.8 / (cu + cl + ce + cw + cz + cd), 0.0)
        return (cu, cl, ce, cw, cz, cd, wd, beyond)

    def coarse_k(x):
        y = x.reshape(x.shape[0] // 2, 2, 8, 128)
        return 0.25 * pairs(y[:, 0] + y[:, 1], 1)

    C3 = coefficients_patch(kn, kx, count3, 3, 1)
    C4 = coefficients_patch(coarse_k(kn), coarse_k(kx), count3 // 2, 4, 2)

    odd = (fine // 8) % 2
    w3 = weights(r >= 0, odd, 3)
    w4 = weights(r >= 0, 0 * odd, 2)

    def neighbours_patch(C, v, step, w, cell):
        n = v.shape[0]
        edge = lax.rem(HALF - r + REACH + 4 * SEGS, SEGS) * step
        VP[pl.ds(0, n)] = v
        over = mix(VP[edge], w, -cell)
        under = mix(VP[lax.rem(edge + n - 1, n)], w, cell)
        row = lax.broadcasted_iota(jnp.int32, v.shape, 0)
        vu = jnp.concatenate([v[1:], v[:1]], 0)
        vd = jnp.concatenate([v[-1:], v[:-1]], 0)
        mark = jnp.where(near, edge, -8)
        vu = jnp.where(row == mark - 1, over[None], vu)
        vd = jnp.where(row == mark, under[None], vd)
        return (
            C[0] * vu
            + C[1] * vd
            + C[2] * roll(v, -cell, 2)
            + C[3] * roll(v, cell, 2)
            + C[4] * roll(v, -1, 1)
            + C[5] * roll(v, 1, 1)
        )

    for w in w_p:
        w()
    b3 = unpack(RB)
    b3 = jnp.where(C3[7], turn(b3), b3)
    u3 = C3[6] * b3
    x = 0.2 * b3 + neighbours_patch(C3, u3, 4, w3, 1)
    x = x.reshape(count3 // 2, 2, 8, 128)
    b4 = pairs(x[:, 0] + x[:, 1], 1)
    v4 = C4[6] * b4
    for _ in range(3):
        v4 = 0.2 * v4 + C4[6] * (b4 + neighbours_patch(C4, v4, 2, w4, 2))
    up4 = jnp.broadcast_to(v4[:, None], (count3 // 2, 2, 8, 128)).reshape(count3, 8, 128)
    v3 = u3 + up4
    e3 = 0.2 * v3 + C3[6] * (b3 + neighbours_patch(C3, v3, 4, w3, 1))

    delta = (fine // 4) % 4 * 4
    first_row = 4 * REACH - 1
    for j in range(6):
        if j == 0:
            shift = jnp.where(is_sta, -delta, 0)
        elif j == 5:
            shift = jnp.where(is_rot, delta, 0)
        else:
            shift = 0
        for i in range(3):
            signed = lane + 128 * i
            if i == 2:
                signed = jnp.where(lane < 64, signed, signed - LANES)
            index = ((signed + shift + 1024) // 8) % 128
            E3S[j, :, pl.ds(128 * i, 128)] = jnp.take_along_axis(e3[first_row + j], index, axis=1)

    for level in (2, 1, 0):
        A = levels[level]
        low, own, hi = LO + 12 >> level, OWN >> level, HI >> level
        rows = ROWS >> level
        if level == 2:
            A["U"][low - 2] = A["U"][low - 2] + E3S[0]
            A["U"][low - 1] = A["U"][low - 1] + E3S[0]
            for j in range(rows):
                A["U"][own + j] = A["U"][own + j] + E3S[1 + j // 2]
            A["U"][hi] = A["U"][hi] + E3S[5]
            A["U"][hi + 1] = A["U"][hi + 1] + E3S[5]
        else:
            E = levels[level + 1]["E"]

            def add(j, A=A, E=E):
                e = E[j]
                A["U"][2 * j] = A["U"][2 * j] + e
                A["U"][2 * j + 1] = A["U"][2 * j + 1] + e

            add((low >> 1) - 1)
            loop_rows(own >> 1, (own + rows) >> 1, add, 4)
            add(hi >> 1)
        ghosts(A["U"], level)

        def smooth(j, A=A, level=level):
            A["E"][j] = 0.2 * A["U"][j] + A["WD"][j] * (A["B"][j] + neighbours(level, A["U"], j))

        smooth(low - 1)
        loop_rows(own, own + rows, smooth, 8)
        smooth(hi)

    ghosts(levels[0]["E"], 0)

    def finish(j):
        E = levels[0]["E"]
        p = E[OWN + j]
        out = B0[OWN + j] - DG[j] * p + neighbours(0, E, OWN + j)
        for half in range(2):
            place = pl.ds(tile_row(j, half), 8, stride=2 * ROWS)
            p_ref[place, :] = p[:, 128 * half : 128 * half + 128]
            res_ref[place, :] = out[:, 128 * half : 128 * half + 128]

    loop_rows(0, ROWS, finish, 8)

    for send, copy in messages:
        pl.when(send)(copy.wait_send)


def on_device(source, conductance, slide, fraction, gain):
    nz, rows, columns = source.shape
    scratch = []
    for level in range(3):
        scratch += [pltpu.VMEM((PHYS >> level, nz, LANES), F32)] * len(PER_LEVEL)
    tile = (8, 128)
    scratch += [
        pltpu.VMEM((ROWS, nz, LANES), F32),
        pltpu.VMEM((4, nz, LANES), F32),
        pltpu.VMEM((2, 4, 2) + tile, F32),
        pltpu.VMEM((2, 4, 2) + tile, F32),
        pltpu.VMEM((2, 2, 2) + tile, F32),
        pltpu.VMEM((2, 2, 2) + tile, F32),
        pltpu.VMEM((2,) + tile, F32),
        pltpu.VMEM((2,) + tile, F32),
        pltpu.VMEM((28, nz, 256), F32),
        pltpu.VMEM((28, nz, 256), F32),
        pltpu.VMEM(tile, F32),
        pltpu.VMEM(tile, F32),
        pltpu.VMEM((SEGS, SLOTS) + tile, F32),
        pltpu.VMEM((SEGS, SLOTS) + tile, F32),
        pltpu.VMEM((SEGS, SLOTS) + tile, F32),
        pltpu.VMEM((4 * SEGS,) + tile, F32),
        pltpu.VMEM((6, nz, LANES), F32),
        pltpu.VMEM((nz * rows * columns // 128, 128), F32),
        pltpu.VMEM((nz * rows * columns // 128, 128), F32),
    ]
    sems = 24 + 2 * SEGS + SEGS * SLOTS
    scratch += [pltpu.SemaphoreType.DMA((n,)) for n in (sems, sems, 2)]
    vmem = pl.BlockSpec(memory_space=pltpu.VMEM)
    smem = pl.BlockSpec(memory_space=pltpu.SMEM)
    hbm = pl.BlockSpec(memory_space=pltpu.HBM)
    flat = jax.ShapeDtypeStruct((nz * rows * columns // 128, 128), F32)
    large = [pltpu.with_memory_space_constraint(to_tiles(x), pltpu.HBM) for x in (source, conductance)]
    operands = (slide, fraction, gain, *large)
    pressure, residual = pl.pallas_call(
        kernel,
        out_shape=(flat, flat),
        in_specs=[smem] * 3 + [hbm] * 2,
        out_specs=(vmem, vmem),
        scratch_shapes=scratch,
        compiler_params=pltpu.CompilerParams(
            collective_id=0, has_side_effects=True, vmem_limit_bytes=48 * 1024 * 1024
        ),
    )(*operands)
    return from_tiles(pressure, source.shape), from_tiles(residual, source.shape)


def solution(mesh):
    spec = P(None, "rad", "theta")
    return jax.shard_map(
        on_device, mesh=mesh, in_specs=(spec, spec, P(), P(), P()), out_specs=(spec, spec), check_vma=False
    )
```

```python
import functools

import jax
import jax.numpy as jnp
from jax import lax
from jax.experimental import pallas as pl
from jax.experimental.pallas import tpu as pltpu
from jax.sharding import PartitionSpec as P

MESH = pl.DeviceIdType.MESH
F32 = jnp.float32
NT, NR = 16, 32
HALF = NR // 2
ROWS = 32
GLOBAL_ROWS = NR * ROWS
LANES = 384
LO, GLU, GOD, OWN, GOU, GHD, HI, PHYS = 0, 12, 16, 20, 52, 56, 60, 72
REACH = 3
SEGS = 2 * REACH + 1
SLOTS = 4
NORMAL = {0: 0, 1: 1, 3: -1}
FROM_STATOR = (8, 9, 10, 7)
FROM_ROTOR = (-9, -8, -7, -10)
PER_LEVEL = ("K", "B", "U", "CU", "CL", "CE", "CW", "CZ", "CD", "WD", "E")


def roll(x, shift, axis):
    size = x.shape[axis]
    shift = shift % size
    return x if shift == 0 else pltpu.roll(x, shift, axis)


def tile_row(j, half):
    return (j // 8) * 16 + half * 8 + j % 8


def to_tiles(x):
    nz, rows, columns = x.shape
    x = x.reshape(nz, rows // 8, 8, columns // 128, 128)
    return x.transpose(0, 1, 3, 2, 4).reshape(nz * rows * columns // 128, 128)


def from_tiles(x, shape):
    nz, rows, columns = shape
    x = x.reshape(nz, rows // 8, columns // 128, 8, 128)
    return x.transpose(0, 1, 3, 2, 4).reshape(shape)


def loop_rows(low, high, body, unroll):
    count = (high - low) // unroll

    def step(i, carry):
        for q in range(unroll):
            body(low + i * unroll + q)
        return carry

    if count:
        lax.fori_loop(0, count, step, 0)
    for j in range(low + count * unroll, high):
        body(j)


def kernel(*refs):
    slide_ref, frac_ref, gain_ref, b_hbm, k_hbm, p_ref, res_ref = refs[:7]
    at = 7
    levels = []
    for _ in range(3):
        levels.append(dict(zip(PER_LEVEL, refs[at : at + len(PER_LEVEL)])))
        at += len(PER_LEVEL)
    (DG, B3S, EP, RT, RC_HI, RC_LO, RG, RGH, WC1, WC2, PK, PB, RN, RX, RB, VP, E3S) = refs[at : at + 17]
    k_ref, b_ref, sem_s, sem_r, sem_in = refs[at + 17 :]

    moves = ((k_hbm, k_ref), (b_hbm, b_ref))
    loads = [pltpu.make_async_copy(x, y, sem_in.at[i]) for i, (x, y) in enumerate(moves)]
    for load in loads:
        load.start()

    t = lax.axis_index("theta")
    r = lax.axis_index("rad")
    side = r // HALF
    is_rot = r == HALF - 1
    is_sta = r == HALF
    is_if = is_rot | is_sta
    near = (r >= HALF - REACH) & (r < HALF + REACH)

    def theta(offset):
        return lax.rem(t + offset + 2 * NT, NT)

    lane = lax.broadcasted_iota(jnp.int32, (8, 128), 1)
    lane3 = lax.broadcasted_iota(jnp.int32, (8, LANES), 1)
    axial = lax.broadcasted_iota(jnp.int32, (8, 128), 0)
    K0, B0 = levels[0]["K"], levels[0]["B"]

    zeros3 = jnp.zeros((12, 8, LANES), F32)

    @pl.when(r == 0)
    def _():
        K0[pl.ds(LO, 12)] = zeros3
        B0[pl.ds(LO, 12)] = zeros3

    @pl.when(r == NR - 1)
    def _():
        K0[pl.ds(HI, 12)] = zeros3
        B0[pl.ds(HI, 12)] = zeros3

    RC_LO[...] = jnp.zeros_like(RC_LO)
    RC_HI[...] = jnp.zeros_like(RC_HI)
    RN[...] = jnp.ones_like(RN)
    RX[...] = jnp.ones_like(RX)
    RB[...] = jnp.zeros_like(RB)

    barrier = pltpu.get_barrier_semaphore()
    sgn = 1 - 2 * side
    inner = near & jnp.logical_not(is_if)
    greet, heard = [], []

    def meet(cond, dt, dr):
        greet.append((cond, dt, dr))
        heard.append(cond)

    for dr in (1, 2, 3):
        far_dr = dr * sgn
        to_inner = is_if & (dr > 1)
        from_if = inner & ((r + far_dr == HALF - 1) | (r + far_dr == HALF)) & ((r + far_dr) // HALF != side)
        for o in range(7, 11):
            if dr > 1:
                greet.append((to_inner, sgn * o, far_dr))
            heard.append(from_if)
    for o in range(7, 11):
        meet(is_if, sgn * o, sgn)
        meet((r == HALF - 2) | (r == HALF + 1), sgn * o, 3 * sgn)
    for o in range(6, 11):
        meet(is_if, o, 0)
    for dr in (-3, 3, -2, 2, -1, 1, 0):
        inside = (r + dr >= 0) & (r + dr < NR)
        for dt in (-1, 1, 0) if abs(dr) < 2 else (0,):
            if dr or dt:
                meet(inside, dt, dr)
    for o in (-2, 2):
        meet(near, o, 0)
    for cond, dt, dr in greet:
        peer = (theta(dt), r + dr)

        @pl.when(cond)
        def _(peer=peer):
            pl.semaphore_signal(barrier, inc=1, device_id=peer, device_id_type=MESH)

    for arr, (src, dst) in enumerate(((k_ref, K0), (b_ref, B0))):
        loads[arr].wait()

        def move(j, src=src, dst=dst):
            for half in range(2):
                dst[OWN + j, :, pl.ds(128 * half, 128)] = src[pl.ds(tile_row(j, half), 8, stride=2 * ROWS), :]

        loop_rows(0, ROWS, move, ROWS)
        for m in range(4):
            left = right = None
            for q in range(8):
                row = OWN + 8 * m + q
                low = roll(dst[row, :, pl.ds(0, 128)], 16 * q, 1)
                high = roll(dst[row, :, pl.ds(128, 128)], 16 * q + 16, 1)
                here = lane // 16 == q
                left = low if q == 0 else jnp.where(here, low, left)
                right = high if q == 0 else jnp.where(here, high, right)
            EP[0, m, arr] = left
            EP[1, m, arr] = right

    pl.semaphore_wait(barrier, sum(cond.astype(jnp.int32) for cond in heard))

    messages = []

    def message(index, send, recv, src, dst, target, start=True):
        copy = pltpu.make_async_remote_copy(
            src_ref=src,
            dst_ref=dst,
            send_sem=sem_s.at[index],
            recv_sem=sem_r.at[index],
            device_id=target,
            device_id_type=MESH,
        )
        if start:
            pl.when(send)(copy.start)
        messages.append((send, copy))
        return lambda: pl.when(recv)(copy.wait_recv)

    always = r >= 0
    down_s, down_r = (r >= 1) & (r != HALF), (r < NR - 1) & (r != HALF - 1)
    up_s, up_r = down_r, down_s
    wide = pl.ds(0, 256)
    w_th = [
        message(0, always, always, EP.at[0], RT.at[0], (theta(-1), r)),
        message(1, always, always, EP.at[1], RT.at[1], (theta(1), r)),
    ]
    w_k = [
        message(2, down_s, down_r, K0.at[pl.ds(OWN, 12), :, wide], K0.at[pl.ds(HI, 12), :, wide], (t, r - 1)),
        message(3, up_s, up_r, K0.at[pl.ds(OWN + 20, 12), :, wide], K0.at[pl.ds(LO, 12), :, wide], (t, r + 1)),
        message(4, down_s, down_r, EP.at[0, pl.ds(0, 2)], RC_HI.at[0], (theta(-1), r - 1)),
        message(5, down_s, down_r, EP.at[1, pl.ds(0, 2)], RC_HI.at[1], (theta(1), r - 1)),
        message(6, up_s, up_r, EP.at[0, pl.ds(2, 2)], RC_LO.at[0], (theta(-1), r + 1)),
        message(7, up_s, up_r, EP.at[1, pl.ds(2, 2)], RC_LO.at[1], (theta(1), r + 1)),
    ]
    w_b = [
        message(8, down_s, down_r, B0.at[pl.ds(OWN, 12), :, wide], B0.at[pl.ds(HI, 12), :, wide], (t, r - 1)),
        message(9, up_s, up_r, B0.at[pl.ds(OWN + 20, 12), :, wide], B0.at[pl.ds(LO, 12), :, wide], (t, r + 1)),
    ]
    w_i = []

    th = {o: theta(o) for o in (-1, 1, 8)}
    th_far = {"g2": theta(-9 * sgn), "ge": theta(-10 + 17 * side), "gw": theta(-7 + 17 * side), "c2": theta(9 * sgn)}

    facing = OWN + 20 * (1 - side)
    facing4 = OWN + 28 * (1 - side)
    group4 = 3 * (1 - side)
    other = NR - 1 - r
    ghost = GOD + (GOU - GOD) * side
    own4 = K0.at[pl.ds(facing4, 4), :, wide]
    items = [
        (own4, K0.at[pl.ds(ghost, 4), :, wide], (t, other)),
        (EP.at[0, group4, 0], RG.at[0], (th[-1], other)),
        (EP.at[1, group4, 0], RG.at[1], (th[1], other)),
        (own4, WC1.at[pl.ds(24, 4)], (th[8], r)),
        (own4, WC2.at[pl.ds(24, 4)], (th_far["g2"], r)),
        (EP.at[0, group4, 0], RGH.at[0], (th_far["ge"], r)),
        (EP.at[1, group4, 0], RGH.at[1], (th_far["gw"], r)),
        (K0.at[pl.ds(facing, 12), :, wide], WC1.at[pl.ds(0, 12)], (th[8], other)),
        (K0.at[pl.ds(facing, 12), :, wide], WC2.at[pl.ds(0, 12)], (th_far["c2"], other)),
        (B0.at[pl.ds(facing, 12), :, wide], WC1.at[pl.ds(12, 12)], (th[8], other)),
        (B0.at[pl.ds(facing, 12), :, wide], WC2.at[pl.ds(12, 12)], (th_far["c2"], other)),
    ]
    for n, (src, dst, target) in enumerate(items):
        w_i.append(message(10 + n, is_if, is_if, src, dst, target))

    cross_corners = []
    for part, (cond, dst, first) in enumerate(((is_sta, RC_HI, 0), (is_rot, RC_LO, 2))):
        other = r - 1 if part == 0 else r + 1
        offs = (-10, -7) if part == 0 else (7, 10)
        got = is_rot if part == 0 else is_sta
        for e in range(2):
            cross_corners.append(
                message(
                    (4 if part == 0 else 6) + e,
                    cond,
                    got,
                    EP.at[e, pl.ds(first, 2)],
                    dst.at[e],
                    (theta(offs[e]), other),
                )
            )

    slide = slide_ref[0]
    frac = frac_ref[0]
    gain = gain_ref[0]

    def pairs(x, cell):
        width = x.shape[-1]
        pick = (lax.broadcasted_iota(jnp.int32, x.shape, x.ndim - 1) // cell) % 2 == 1
        return x + jnp.where(pick, roll(x, cell, x.ndim - 1), roll(x, width - cell, x.ndim - 1))

    gather_index = (lane % 16) * 8

    def pack(rows):
        out = None
        for q, x in enumerate(rows):
            for half in range(2):
                part = jnp.take_along_axis(x[:, 128 * half : 128 * half + 128], gather_index, axis=1)
                out = part if out is None else jnp.where(lane // 16 == 2 * q + half, part, out)
        return out

    own3 = []
    for j in range(4):
        k2 = []
        for i in range(2):
            k1 = []
            for h in range(2):
                row = OWN + 8 * j + 4 * i + 2 * h
                k1.append(0.25 * pairs(K0[row, :, wide] + K0[row + 1, :, wide], 1))
            k2.append(0.25 * pairs(k1[0] + k1[1], 2))
        own3.append(0.25 * pairs(k2[0] + k2[1], 4))
    PK[...] = pack(own3)

    RN[REACH, 0] = PK[...]
    base_t, base_n, base_x, base_b = 21, 24, 24 + SEGS, 24 + 2 * SEGS
    w_t = [
        message(base_t, always, always, PK, RN.at[REACH, 1], (theta(-1), r)),
        message(base_t + 1, always, always, PK, RN.at[REACH, 3], (theta(1), r)),
        message(base_t + 2, near, near, PK, RN.at[REACH, 2], (theta(-2), r)),
    ]

    w_n, w_x = {}, {}

    def send_plain():
        for dr in (-3, 3, -2, 2, -1, 1):
            inside_s = (r + dr >= 0) & (r + dr < NR)
            inside_r = (r - dr >= 0) & (r - dr < NR)
            seg = REACH - dr
            w_n[seg] = message(base_n + seg, inside_s, inside_r, RN.at[REACH], RN.at[seg], (t, r + dr))

    def send_across(which):
        for dr in range(-REACH, REACH + 1):
            seg = REACH - dr
            to, fro = r + dr, r - dr
            to_rot = (to < HALF) & (to >= HALF - REACH) & (r >= HALF - 1)
            to_sta = (to >= HALF) & (to < HALF + REACH) & (r <= HALF)
            got = ((r < HALF) & (r >= HALF - REACH) & (fro >= HALF - 1)) | (
                (r >= HALF) & (r < HALF + REACH) & (fro <= HALF)
            )
            off = -FROM_STATOR[0] + ((r + dr) // HALF) * (FROM_STATOR[0] - FROM_ROTOR[0])
            w_x[seg] = message(
                base_x + seg, (to_rot | to_sta) & which, got, RN.at[REACH], RX.at[seg], (theta(off), r + dr)
            )

    def third(left_pack, right_pack, q):
        return jnp.where(lane < 64, roll(left_pack, -16 * q, 1), roll(right_pack, 112 - 16 * q, 1))

    halo = pl.ds(256, 128)
    for w in w_th:
        w()
    for m in range(4):
        for arr, ref in enumerate((K0, B0)):
            for q in range(8):
                ref[OWN + 8 * m + q, :, halo] = third(RT[0, m, arr], RT[1, m, arr], q)
    for w in w_t:
        w()
    send_plain()
    send_across(inner)
    def down_k(level, low, high):
        fine_k, coarse_k = levels[level - 1]["K"], levels[level]["K"]

        def body(j):
            coarse_k[j] = 0.25 * pairs(fine_k[2 * j] + fine_k[2 * j + 1], 1 << (level - 1))

        loop_rows(low, high, body, 8)

    top = axial < 7
    low_ok, high_ok = r > 0, r < NR - 1

    def coefficients(level, seg, low, high, unroll=8):
        A = levels[level]
        rows_level = GLOBAL_ROWS >> level
        inv = 1.0 / rows_level
        cell = 1 << level
        start = {"lo": LO + 12, "own": OWN, "hi": HI - 32}[seg] >> level
        ok = {"lo": low_ok, "own": None, "hi": high_ok}[seg]

        def body(j):
            pos = r * (ROWS >> level) + j - start
            posf = pos.astype(F32)
            hu = 0.5 * (1.0 + (posf + 1.0) * inv) * jnp.where(pos == rows_level // 2 - 1, gain, 1.0)
            hl = 0.5 * (1.0 + posf * inv) * jnp.where(pos == rows_level // 2, gain, 1.0)
            rc = 1.0 + (posf + 0.5) * inv
            hc1 = 0.5 / jnp.full((8, 128), rc, F32)
            hz1 = jnp.where(top, 0.5 * rc, 0.0)
            hc = jnp.concatenate([hc1] * 3, axis=1)
            hz = jnp.concatenate([hz1] * 3, axis=1)
            k = A["K"][j]
            ce = (k + roll(k, -cell, 1)) * hc
            cw = roll(ce, cell, 1)
            cu = (k + A["K"][j + 1]) * hu
            cl = (k + A["K"][j - 1]) * hl
            cz = (k + roll(k, -1, 0)) * hz
            cd = roll(cz, 1, 0)
            diag = cu + cl + ce + cw + cz + cd
            wd = 0.8 / diag
            if ok is not None:
                wd = jnp.where(ok, wd, 0.0)
            A["CU"][j], A["CL"][j], A["CE"][j], A["CW"][j], A["CZ"][j], A["CD"][j] = cu, cl, ce, cw, cz, cd
            A["WD"][j] = wd
            if level == 0:
                A["U"][j] = wd * A["B"][j]
                if seg == "own":
                    DG[j - OWN] = diag

        loop_rows(low, high, body, unroll)

    fine = slide - NT * 256 // 2

    def weights(active, shift, count):
        out = []
        for i in range(count):
            w = jnp.where(shift == i, 1.0 - frac, 0.0) + jnp.where(shift == i - 1, frac, 0.0)
            out.append(jnp.where(active, w, 1.0 if i == 0 else 0.0))
        return out

    shifts = (fine % 4, (fine // 2) % 2, 0 * fine)
    up_w = [weights(is_rot, shifts[level], (5, 3, 2)[level]) for level in range(3)]
    low_w = [weights(is_sta, shifts[level], (5, 3, 2)[level]) for level in range(3)]

    def mix(x, w, step):
        out = w[0] * x
        for i in range(1, len(w)):
            out = out + w[i] * roll(x, i * step, x.ndim - 1)
        return out

    def ghosts(field, level):
        cell = 1 << level
        lo_end, own, own_end, hi = LO + 12 >> level, OWN >> level, GOU >> level, HI >> level
        field[own_end] = mix(field[hi], up_w[level], -cell)
        field[hi - 1] = mix(field[own_end - 1], up_w[level], cell)
        field[lo_end] = mix(field[own], low_w[level], -cell)
        field[own - 1] = mix(field[lo_end - 1], low_w[level], cell)

    def neighbours(level, field, j):
        A = levels[level]
        cell = 1 << level
        v = field[j]
        return (
            A["CU"][j] * field[j + 1]
            + A["CL"][j] * field[j - 1]
            + A["CE"][j] * roll(v, -cell, 1)
            + A["CW"][j] * roll(v, cell, 1)
            + A["CZ"][j] * roll(v, -1, 0)
            + A["CD"][j] * roll(v, 1, 0)
        )

    def first(level, low, high):
        A = levels[level]

        def body(j):
            A["U"][j] = A["WD"][j] * A["B"][j]

        loop_rows(low, high, body, 8)

    def restrict(level, low, high):
        A = levels[level]

        def body(j):
            x = 0.2 * (A["B"][2 * j] + A["B"][2 * j + 1])
            x = x + (neighbours(level, A["U"], 2 * j) + neighbours(level, A["U"], 2 * j + 1))
            levels[level + 1]["B"][j] = pairs(x, 1 << level)

        loop_rows(low, high, body, 4)

    def restrict3(rows):
        A = levels[2]
        for j in rows:
            x = None
            for i in range(2):
                row = (OWN >> 2) + 2 * j + i
                y = 0.2 * A["B"][row] + neighbours(2, A["U"], row)
                x = y if x is None else x + y
            B3S[j] = pairs(x, 4)

    own0, own1, own2 = OWN, OWN >> 1, OWN >> 2
    lo0, lo1, lo2 = LO + 12, LO + 12 >> 1, LO + 12 >> 2
    hi0, hi1, hi2 = HI, HI >> 1, HI >> 2

    down_k(1, own1, own1 + 16)
    down_k(2, own2, own2 + 8)
    coefficients(0, "own", own0 + 1, own0 + 31)
    coefficients(1, "own", own1 + 1, own1 + 15)
    coefficients(2, "own", own2 + 1, own2 + 7)
    restrict(0, own1 + 1, own1 + 15)
    first(1, own1 + 1, own1 + 15)
    restrict(1, own2 + 1, own2 + 7)
    first(2, own2 + 1, own2 + 7)
    restrict3((1, 2))

    for w in w_k:
        w()
    for w in cross_corners:
        w()
    for w in w_b:
        w()
    for j in range(12):
        for arr, ref in enumerate((K0, B0)):
            m, q = divmod(j, 8)
            ref[HI + j, :, halo] = third(RC_HI[0, m, arr], RC_HI[1, m, arr], q)
            m, q = divmod(4 + j, 8)
            ref[LO + j, :, halo] = third(RC_LO[0, m, arr], RC_LO[1, m, arr], q)

    d4 = (fine // 4) * 4
    q4 = d4 % 128
    far = d4 >= 128
    back4 = lax.rem(128 - q4, 128)

    for w in w_i:
        w()
    send_across(is_if)

    def window(tiles, sign):
        if sign > 0:
            tiles = [jnp.where(far, tiles[(i + 1) % 5], tiles[i]) for i in range(5)]
            turned = [pltpu.roll(x, back4, 1) for x in tiles]
            keep = lane < 128 - q4
            out = [jnp.where(keep, turned[i], turned[(i + 1) % 5]) for i in (0, 1, 2, 4)]
        else:
            tiles = [jnp.where(far, tiles[(i + 4) % 5], tiles[i]) for i in range(5)]
            turned = [pltpu.roll(x, q4, 1) for x in tiles]
            keep = lane >= q4
            out = [jnp.where(keep, turned[i], turned[(i + 4) % 5]) for i in (0, 1, 2, 4)]
        return out[0], out[1], jnp.where(lane < 64, out[2], out[3])

    def fill(sign, dst_k, dst_ghost):
        for j in range(28):
            if j < 24:
                ref, row = ((K0, B0)[j // 12], dst_k + j % 12)
                edge = ref[row, :, halo]
            else:
                ref, row = (K0, dst_ghost + j - 24)
                edge = third(RGH[0], RGH[1], j - 24 + (4 if sign > 0 else 0))
            a = [WC1[j, :, pl.ds(0, 128)], WC1[j, :, pl.ds(128, 128)]]
            b = [WC2[j, :, pl.ds(0, 128)], WC2[j, :, pl.ds(128, 128)]]
            tiles = a + b + [edge] if sign > 0 else a + [edge] + b
            for i, x in enumerate(window(tiles, sign)):
                ref[row, :, pl.ds(128 * i, 128)] = x

    @pl.when(is_rot)
    def _():
        fill(1, HI, GHD)
        for j in range(4):
            K0[GOU + j, :, halo] = third(RG[0], RG[1], j)

    @pl.when(is_sta)
    def _():
        fill(-1, LO, GLU)
        for j in range(4):
            K0[GOD + j, :, halo] = third(RG[0], RG[1], 4 + j)

    @pl.when(jnp.logical_not(is_rot))
    def _():
        K0[pl.ds(GOU, 4)] = K0[pl.ds(HI, 4)]
        K0[pl.ds(GHD, 4)] = K0[pl.ds(OWN + 28, 4)]

    @pl.when(jnp.logical_not(is_sta))
    def _():
        K0[pl.ds(GLU, 4)] = K0[pl.ds(OWN, 4)]
        K0[pl.ds(GOD, 4)] = K0[pl.ds(LO + 8, 4)]

    for level, low, high, end in ((1, own1, own1 + 16, PHYS >> 1), (2, own2, own2 + 8, PHYS >> 2)):
        down_k(level, 0, low)
        down_k(level, high, end)
    coefficients(0, "own", own0, own0 + 1)
    coefficients(0, "own", own0 + 31, own0 + 32)
    coefficients(0, "lo", lo0 - 11, lo0)
    coefficients(0, "hi", hi0, hi0 + 11)
    coefficients(1, "own", own1, own1 + 1)
    coefficients(1, "own", own1 + 15, own1 + 16)
    coefficients(1, "lo", lo1 - 5, lo1)
    coefficients(1, "hi", hi1, hi1 + 5)
    coefficients(2, "own", own2, own2 + 1)
    coefficients(2, "own", own2 + 7, own2 + 8)
    coefficients(2, "lo", lo2 - 2, lo2)
    coefficients(2, "hi", hi2, hi2 + 2)
    ghosts(levels[0]["U"], 0)
    for low, high in ((lo1 - 5, lo1), (own1, own1 + 1), (own1 + 15, own1 + 16), (hi1, hi1 + 5)):
        restrict(0, low, high)
    for low, high in ((lo1 - 5, lo1), (own1, own1 + 1), (own1 + 15, own1 + 16), (hi1, hi1 + 5)):
        first(1, low, high)
    ghosts(levels[1]["U"], 1)
    for low, high in ((lo2 - 2, lo2), (own2, own2 + 1), (own2 + 7, own2 + 8), (hi2, hi2 + 2)):
        restrict(1, low, high)
    for low, high in ((lo2 - 2, lo2), (own2, own2 + 1), (own2 + 7, own2 + 8), (hi2, hi2 + 2)):
        first(2, low, high)
    ghosts(levels[2]["U"], 2)
    restrict3((0, 3))

    PB[...] = pack([B3S[j, :, wide] for j in range(4)])
    RB[REACH, 0] = PB[...]
    w_p, sent = [], []
    for dr in (-3, 3, -2, 2, -1, 1, 0):
        inside_s = (r + dr >= 0) & (r + dr < NR)
        inside_r = (r - dr >= 0) & (r - dr < NR)
        seg = REACH - dr
        same_s = (r + dr) // HALF == side
        same_r = (r - dr) // HALF == side
        to_side = (r + dr) // HALF
        near_ways = [(slot, off) for slot, off in NORMAL.items() if dr or off]
        ways = [(inside_s & same_s, inside_r & same_r, [(slot, theta(-off)) for slot, off in near_ways])]
        if dr:
            across = [
                (slot, theta(-FROM_STATOR[slot] + to_side * (FROM_STATOR[slot] - FROM_ROTOR[slot])))
                for slot in range(SLOTS)
            ]
            ways.append((inside_s & jnp.logical_not(same_s), inside_r & jnp.logical_not(same_r), across))
        for send, recv, targets in ways:

            def copy_of(src, dst, target, seg=seg, dr=dr):
                return pltpu.make_async_remote_copy(
                    src_ref=src,
                    dst_ref=dst,
                    send_sem=sem_s.at[base_b + seg],
                    recv_sem=sem_r.at[base_b + seg],
                    device_id=(target, r + dr),
                    device_id_type=MESH,
                )

            copies = [copy_of(PB, RB.at[seg, slot], target) for slot, target in targets]

            @pl.when(send)
            def _(copies=copies):
                for copy in copies:
                    copy.start()

            whole = RB.at[seg, pl.ds(0, len(targets))]
            both = copy_of(whole, whole, targets[0][1])
            w_p.append((recv, both))
            sent.append((send, both))
    for send, copy in messages:
        pl.when(send)(copy.wait_send)

    count3 = 4 * SEGS
    d3 = (fine // 16) * 2
    sgn_x = jnp.where(side == 0, lax.rem(128 - d3, 128), lax.rem(d3 + 96, 128))

    def unpack(ref):
        tiles = [ref[:, o] for o in range(SLOTS)]
        lane7 = lax.broadcasted_iota(jnp.int32, (SEGS, 8, 128), 2) // 32
        rows = []
        for q in range(4):
            out = roll(tiles[0], -32 * q, 2)
            for o in range(1, SLOTS):
                out = jnp.where(lane7 == o, roll(tiles[o], 32 * (o - q), 2), out)
            rows.append(out)
        return jnp.stack(rows, axis=1).reshape(count3, 8, 128)

    def turn(x):
        return pltpu.roll(x, sgn_x, 2)

    for w in list(w_x.values()) + list(w_n.values()):
        w()
    kn = unpack(RN)
    kx = turn(unpack(RX))

    far_off = jnp.where(near, side, 1 << 20)

    def coefficients_patch(kn, kx, rows, level, cell):
        rows_level = GLOBAL_ROWS >> level
        inv = 1.0 / rows_level
        pos = (r - REACH) * (ROWS >> level) + lax.broadcasted_iota(jnp.int32, (rows, 8, 128), 0)
        ok = (pos >= 0) & (pos < rows_level)
        beyond = (pos - rows_level // 2) * (1 - 2 * side) >= far_off
        posf = pos.astype(F32)
        hu = 0.5 * (1.0 + (posf + 1.0) * inv) * jnp.where(pos == rows_level // 2 - 1, gain, 1.0)
        hl = 0.5 * (1.0 + posf * inv) * jnp.where(pos == rows_level // 2, gain, 1.0)
        rc = 1.0 + (posf + 0.5) * inv
        hc = 0.5 / rc
        hz = jnp.where(lax.broadcasted_iota(jnp.int32, (rows, 8, 128), 1) < 7, 0.5 * rc, 0.0)
        k = jnp.where(beyond, kx, kn)
        ku = jnp.where(beyond, jnp.concatenate([kx[1:], kx[:1]], 0), jnp.concatenate([kn[1:], kn[:1]], 0))
        kd = jnp.where(beyond, jnp.concatenate([kx[-1:], kx[:-1]], 0), jnp.concatenate([kn[-1:], kn[:-1]], 0))
        ku = jnp.where(pos == rows_level - 1, 0.0, ku)
        kd = jnp.where(pos == 0, 0.0, kd)
        ce = (k + roll(k, -cell, 2)) * hc
        cw = roll(ce, cell, 2)
        cu = (k + ku) * hu
        cl = (k + kd) * hl
        cz = (k + roll(k, -1, 1)) * hz
        cd = roll(cz, 1, 1)
        wd = jnp.where(ok, 0.8 / (cu + cl + ce + cw + cz + cd), 0.0)
        return (cu, cl, ce, cw, cz, cd, wd, beyond)

    def coarse_k(x):
        y = x.reshape(x.shape[0] // 2, 2, 8, 128)
        return 0.25 * pairs(y[:, 0] + y[:, 1], 1)

    C3 = coefficients_patch(kn, kx, count3, 3, 1)
    C4 = coefficients_patch(coarse_k(kn), coarse_k(kx), count3 // 2, 4, 2)

    odd = (fine // 8) % 2
    w3 = weights(r >= 0, odd, 3)
    w4 = weights(r >= 0, 0 * odd, 2)

    def neighbours_patch(C, v, step, w, cell):
        n = v.shape[0]
        edge = lax.rem(HALF - r + REACH + 4 * SEGS, SEGS) * step
        VP[pl.ds(0, n)] = v
        over = mix(VP[edge], w, -cell)
        under = mix(VP[lax.rem(edge + n - 1, n)], w, cell)
        row = lax.broadcasted_iota(jnp.int32, v.shape, 0)
        vu = jnp.concatenate([v[1:], v[:1]], 0)
        vd = jnp.concatenate([v[-1:], v[:-1]], 0)
        mark = jnp.where(near, edge, -8)
        vu = jnp.where(row == mark - 1, over[None], vu)
        vd = jnp.where(row == mark, under[None], vd)
        return (
            C[0] * vu
            + C[1] * vd
            + C[2] * roll(v, -cell, 2)
            + C[3] * roll(v, cell, 2)
            + C[4] * roll(v, -1, 1)
            + C[5] * roll(v, 1, 1)
        )

    for recv, both in w_p:
        pl.when(recv)(both.wait_recv)
    b3 = unpack(RB)
    b3 = jnp.where(C3[7], turn(b3), b3)
    u3 = C3[6] * b3
    x = 0.2 * b3 + neighbours_patch(C3, u3, 4, w3, 1)
    x = x.reshape(count3 // 2, 2, 8, 128)
    b4 = pairs(x[:, 0] + x[:, 1], 1)
    v4 = C4[6] * b4
    for _ in range(3):
        v4 = 0.2 * v4 + C4[6] * (b4 + neighbours_patch(C4, v4, 2, w4, 2))
    up4 = jnp.broadcast_to(v4[:, None], (count3 // 2, 2, 8, 128)).reshape(count3, 8, 128)
    v3 = u3 + up4
    e3 = 0.2 * v3 + C3[6] * (b3 + neighbours_patch(C3, v3, 4, w3, 1))

    delta = (fine // 4) % 4 * 4
    first_row = 4 * REACH - 1
    for j in range(6):
        if j == 0:
            shift = jnp.where(is_sta, -delta, 0)
        elif j == 5:
            shift = jnp.where(is_rot, delta, 0)
        else:
            shift = 0
        for i in range(3):
            signed = lane + 128 * i
            if i == 2:
                signed = jnp.where(lane < 64, signed, signed - LANES)
            index = ((signed + shift + 1024) // 8) % 128
            E3S[j, :, pl.ds(128 * i, 128)] = jnp.take_along_axis(e3[first_row + j], index, axis=1)

    for level in (2, 1, 0):
        A = levels[level]
        low, own, hi = LO + 12 >> level, OWN >> level, HI >> level
        rows = ROWS >> level
        if level == 2:
            A["U"][low - 2] = A["U"][low - 2] + E3S[0]
            A["U"][low - 1] = A["U"][low - 1] + E3S[0]
            for j in range(rows):
                A["U"][own + j] = A["U"][own + j] + E3S[1 + j // 2]
            A["U"][hi] = A["U"][hi] + E3S[5]
            A["U"][hi + 1] = A["U"][hi + 1] + E3S[5]
        else:
            E = levels[level + 1]["E"]

            def add(j, A=A, E=E):
                e = E[j]
                A["U"][2 * j] = A["U"][2 * j] + e
                A["U"][2 * j + 1] = A["U"][2 * j + 1] + e

            add((low >> 1) - 1)
            loop_rows(own >> 1, (own + rows) >> 1, add, 4)
            add(hi >> 1)
        ghosts(A["U"], level)

        def smooth(j, A=A, level=level):
            A["E"][j] = 0.2 * A["U"][j] + A["WD"][j] * (A["B"][j] + neighbours(level, A["U"], j))

        smooth(low - 1)
        loop_rows(own, own + rows, smooth, 8)
        smooth(hi)

    ghosts(levels[0]["E"], 0)

    def finish(j):
        E = levels[0]["E"]
        p = E[OWN + j]
        A = levels[0]
        o = OWN + j
        east, west = roll(p, -1, 1)[:, :256], roll(p, 1, 1)[:, :256]
        v = p[:, :256]
        out = (
            B0[o, :, wide]
            - DG[j, :, wide] * v
            + A["CU"][o, :, wide] * E[o + 1, :, wide]
            + A["CL"][o, :, wide] * E[o - 1, :, wide]
            + A["CE"][o, :, wide] * east
            + A["CW"][o, :, wide] * west
            + A["CZ"][o, :, wide] * roll(v, -1, 0)
            + A["CD"][o, :, wide] * roll(v, 1, 0)
        )
        for half in range(2):
            place = pl.ds(tile_row(j, half), 8, stride=2 * ROWS)
            p_ref[place, :] = p[:, 128 * half : 128 * half + 128]
            res_ref[place, :] = out[:, 128 * half : 128 * half + 128]

    loop_rows(0, ROWS, finish, 8)

    for send, both in sent:
        pl.when(send)(both.wait_send)


def on_device(source, conductance, slide, fraction, gain):
    nz, rows, columns = source.shape
    scratch = []
    for level in range(3):
        scratch += [pltpu.VMEM((PHYS >> level, nz, LANES), F32)] * len(PER_LEVEL)
    tile = (8, 128)
    scratch += [
        pltpu.VMEM((ROWS, nz, LANES), F32),
        pltpu.VMEM((4, nz, LANES), F32),
        pltpu.VMEM((2, 4, 2) + tile, F32),
        pltpu.VMEM((2, 4, 2) + tile, F32),
        pltpu.VMEM((2, 2, 2) + tile, F32),
        pltpu.VMEM((2, 2, 2) + tile, F32),
        pltpu.VMEM((2,) + tile, F32),
        pltpu.VMEM((2,) + tile, F32),
        pltpu.VMEM((28, nz, 256), F32),
        pltpu.VMEM((28, nz, 256), F32),
        pltpu.VMEM(tile, F32),
        pltpu.VMEM(tile, F32),
        pltpu.VMEM((SEGS, SLOTS) + tile, F32),
        pltpu.VMEM((SEGS, SLOTS) + tile, F32),
        pltpu.VMEM((SEGS, SLOTS) + tile, F32),
        pltpu.VMEM((4 * SEGS,) + tile, F32),
        pltpu.VMEM((6, nz, LANES), F32),
        pltpu.VMEM((nz * rows * columns // 128, 128), F32),
        pltpu.VMEM((nz * rows * columns // 128, 128), F32),
    ]
    sems = 24 + 3 * SEGS
    scratch += [pltpu.SemaphoreType.DMA((n,)) for n in (sems, sems, 2)]
    vmem = pl.BlockSpec(memory_space=pltpu.VMEM)
    smem = pl.BlockSpec(memory_space=pltpu.SMEM)
    hbm = pl.BlockSpec(memory_space=pltpu.HBM)
    flat = jax.ShapeDtypeStruct((nz * rows * columns // 128, 128), F32)
    large = [pltpu.with_memory_space_constraint(to_tiles(x), pltpu.HBM) for x in (source, conductance)]
    operands = (slide, fraction, gain, *large)
    pressure, residual = pl.pallas_call(
        kernel,
        out_shape=(flat, flat),
        in_specs=[smem] * 3 + [hbm] * 2,
        out_specs=(vmem, vmem),
        scratch_shapes=scratch,
        compiler_params=pltpu.CompilerParams(
            collective_id=0, has_side_effects=True, vmem_limit_bytes=48 * 1024 * 1024
        ),
    )(*operands)
    return from_tiles(pressure, source.shape), from_tiles(residual, source.shape)


def solution(mesh):
    spec = P(None, "rad", "theta")
    return jax.shard_map(
        on_device, mesh=mesh, in_specs=(spec, spec, P(), P(), P()), out_specs=(spec, spec), check_vma=False
    )
```

```python
import functools

import jax
import jax.numpy as jnp
from jax import lax
from jax.experimental import pallas as pl
from jax.experimental.pallas import tpu as pltpu
from jax.sharding import PartitionSpec as P

MESH = pl.DeviceIdType.MESH
F32 = jnp.float32
NT, NR = 16, 32
HALF = NR // 2
ROWS = 32
GLOBAL_ROWS = NR * ROWS
LANES = 384
LO, GLU, GOD, OWN, GOU, GHD, HI, PHYS = 0, 12, 16, 20, 52, 56, 60, 72
REACH = 3
SEGS = 2 * REACH + 1
SLOTS = 4
NORMAL = {0: 0, 1: 1, 3: -1}
FROM_STATOR = (8, 9, 10, 7)
FROM_ROTOR = (-9, -8, -7, -10)
PER_LEVEL = ("K", "B", "U", "CU", "CL", "CE", "CW", "CZ", "CD", "WD", "E")


def roll(x, shift, axis):
    size = x.shape[axis]
    shift = shift % size
    return x if shift == 0 else pltpu.roll(x, shift, axis)


def tile_row(j, half):
    return (j // 8) * 16 + half * 8 + j % 8


def to_tiles(x):
    nz, rows, columns = x.shape
    x = x.reshape(nz, rows // 8, 8, columns // 128, 128)
    return x.transpose(0, 1, 3, 2, 4).reshape(nz * rows * columns // 128, 128)


def from_tiles(x, shape):
    nz, rows, columns = shape
    x = x.reshape(nz, rows // 8, columns // 128, 8, 128)
    return x.transpose(0, 1, 3, 2, 4).reshape(shape)


def loop_rows(low, high, body, unroll):
    count = (high - low) // unroll

    def step(i, carry):
        for q in range(unroll):
            body(low + i * unroll + q)
        return carry

    if count:
        lax.fori_loop(0, count, step, 0)
    for j in range(low + count * unroll, high):
        body(j)


def kernel(*refs):
    slide_ref, frac_ref, gain_ref, b_hbm, k_hbm, p_ref, res_ref = refs[:7]
    at = 7
    levels = []
    for _ in range(3):
        levels.append(dict(zip(PER_LEVEL, refs[at : at + len(PER_LEVEL)])))
        at += len(PER_LEVEL)
    (DG, B3S, EP, RT, RC_HI, RC_LO, RG, RGH, WC1, WC2, PK, PB, RN, RX, RB, VP, E3S) = refs[at : at + 17]
    k_ref, b_ref, sem_s, sem_r, sem_in = refs[at + 17 :]

    moves = ((k_hbm, k_ref), (b_hbm, b_ref))
    loads = [pltpu.make_async_copy(x, y, sem_in.at[i]) for i, (x, y) in enumerate(moves)]
    for load in loads:
        load.start()

    t = lax.axis_index("theta")
    r = lax.axis_index("rad")
    side = r // HALF
    is_rot = r == HALF - 1
    is_sta = r == HALF
    is_if = is_rot | is_sta
    near = (r >= HALF - REACH) & (r < HALF + REACH)

    def theta(offset):
        return lax.rem(t + offset + 2 * NT, NT)

    lane = lax.broadcasted_iota(jnp.int32, (8, 128), 1)
    lane3 = lax.broadcasted_iota(jnp.int32, (8, LANES), 1)
    axial = lax.broadcasted_iota(jnp.int32, (8, 128), 0)
    K0, B0 = levels[0]["K"], levels[0]["B"]

    zeros3 = jnp.zeros((12, 8, LANES), F32)

    @pl.when(r == 0)
    def _():
        K0[pl.ds(LO, 12)] = zeros3
        B0[pl.ds(LO, 12)] = zeros3

    @pl.when(r == NR - 1)
    def _():
        K0[pl.ds(HI, 12)] = zeros3
        B0[pl.ds(HI, 12)] = zeros3

    RC_LO[...] = jnp.zeros_like(RC_LO)
    RC_HI[...] = jnp.zeros_like(RC_HI)
    RN[...] = jnp.ones_like(RN)
    RX[...] = jnp.ones_like(RX)
    RB[...] = jnp.zeros_like(RB)

    barrier = pltpu.get_barrier_semaphore()
    sgn = 1 - 2 * side
    inner = near & jnp.logical_not(is_if)
    greet, heard = [], []

    def meet(cond, dt, dr):
        greet.append((cond, dt, dr))
        heard.append(cond)

    for dr in (1, 2, 3):
        far_dr = dr * sgn
        to_inner = is_if & (dr > 1)
        from_if = inner & ((r + far_dr == HALF - 1) | (r + far_dr == HALF)) & ((r + far_dr) // HALF != side)
        for o in range(7, 11):
            if dr > 1:
                greet.append((to_inner, sgn * o, far_dr))
            heard.append(from_if)
    for o in range(7, 11):
        meet(is_if, sgn * o, sgn)
        meet((r == HALF - 2) | (r == HALF + 1), sgn * o, 3 * sgn)
    for o in range(6, 11):
        meet(is_if, o, 0)
    for dr in (-3, 3, -2, 2, -1, 1, 0):
        inside = (r + dr >= 0) & (r + dr < NR)
        for dt in (-1, 1, 0) if abs(dr) < 2 else (0,):
            if dr or dt:
                meet(inside, dt, dr)
    for o in (-2, 2):
        meet(near, o, 0)
    for cond, dt, dr in greet:
        peer = (theta(dt), r + dr)

        @pl.when(cond)
        def _(peer=peer):
            pl.semaphore_signal(barrier, inc=1, device_id=peer, device_id_type=MESH)

    for arr, (src, dst) in enumerate(((k_ref, K0), (b_ref, B0))):
        loads[arr].wait()

        def move(j, src=src, dst=dst):
            for half in range(2):
                dst[OWN + j, :, pl.ds(128 * half, 128)] = src[pl.ds(tile_row(j, half), 8, stride=2 * ROWS), :]

        loop_rows(0, ROWS, move, ROWS)
        for m in range(4):
            left = right = None
            for q in range(8):
                row = OWN + 8 * m + q
                low = roll(dst[row, :, pl.ds(0, 128)], 16 * q, 1)
                high = roll(dst[row, :, pl.ds(128, 128)], 16 * q + 16, 1)
                here = lane // 16 == q
                left = low if q == 0 else jnp.where(here, low, left)
                right = high if q == 0 else jnp.where(here, high, right)
            EP[0, m, arr] = left
            EP[1, m, arr] = right

    pl.semaphore_wait(barrier, sum(cond.astype(jnp.int32) for cond in heard))

    messages = []

    def message(index, send, recv, src, dst, target, start=True):
        copy = pltpu.make_async_remote_copy(
            src_ref=src,
            dst_ref=dst,
            send_sem=sem_s.at[index],
            recv_sem=sem_r.at[index],
            device_id=target,
            device_id_type=MESH,
        )
        if start:
            pl.when(send)(copy.start)
        messages.append((send, copy))
        return lambda: pl.when(recv)(copy.wait_recv)

    always = r >= 0
    down_s, down_r = (r >= 1) & (r != HALF), (r < NR - 1) & (r != HALF - 1)
    up_s, up_r = down_r, down_s
    wide = pl.ds(0, 256)
    w_th = [
        message(0, always, always, EP.at[0], RT.at[0], (theta(-1), r)),
        message(1, always, always, EP.at[1], RT.at[1], (theta(1), r)),
    ]
    w_k = [
        message(2, down_s, down_r, K0.at[pl.ds(OWN, 12), :, wide], K0.at[pl.ds(HI, 12), :, wide], (t, r - 1)),
        message(3, up_s, up_r, K0.at[pl.ds(OWN + 20, 12), :, wide], K0.at[pl.ds(LO, 12), :, wide], (t, r + 1)),
        message(4, down_s, down_r, EP.at[0, pl.ds(0, 2)], RC_HI.at[0], (theta(-1), r - 1)),
        message(5, down_s, down_r, EP.at[1, pl.ds(0, 2)], RC_HI.at[1], (theta(1), r - 1)),
        message(6, up_s, up_r, EP.at[0, pl.ds(2, 2)], RC_LO.at[0], (theta(-1), r + 1)),
        message(7, up_s, up_r, EP.at[1, pl.ds(2, 2)], RC_LO.at[1], (theta(1), r + 1)),
    ]
    w_b = [
        message(8, down_s, down_r, B0.at[pl.ds(OWN, 12), :, wide], B0.at[pl.ds(HI, 12), :, wide], (t, r - 1)),
        message(9, up_s, up_r, B0.at[pl.ds(OWN + 20, 12), :, wide], B0.at[pl.ds(LO, 12), :, wide], (t, r + 1)),
    ]
    w_i = []

    th = {o: theta(o) for o in (-1, 1, 8)}
    th_far = {"g2": theta(-9 * sgn), "ge": theta(-10 + 17 * side), "gw": theta(-7 + 17 * side), "c2": theta(9 * sgn)}

    facing = OWN + 20 * (1 - side)
    facing4 = OWN + 28 * (1 - side)
    group4 = 3 * (1 - side)
    other = NR - 1 - r
    ghost = GOD + (GOU - GOD) * side
    own4 = K0.at[pl.ds(facing4, 4), :, wide]
    items = [
        (own4, K0.at[pl.ds(ghost, 4), :, wide], (t, other)),
        (EP.at[0, group4, 0], RG.at[0], (th[-1], other)),
        (EP.at[1, group4, 0], RG.at[1], (th[1], other)),
        (own4, WC1.at[pl.ds(24, 4)], (th[8], r)),
        (own4, WC2.at[pl.ds(24, 4)], (th_far["g2"], r)),
        (EP.at[0, group4, 0], RGH.at[0], (th_far["ge"], r)),
        (EP.at[1, group4, 0], RGH.at[1], (th_far["gw"], r)),
        (K0.at[pl.ds(facing, 12), :, wide], WC1.at[pl.ds(0, 12)], (th[8], other)),
        (K0.at[pl.ds(facing, 12), :, wide], WC2.at[pl.ds(0, 12)], (th_far["c2"], other)),
        (B0.at[pl.ds(facing, 12), :, wide], WC1.at[pl.ds(12, 12)], (th[8], other)),
        (B0.at[pl.ds(facing, 12), :, wide], WC2.at[pl.ds(12, 12)], (th_far["c2"], other)),
    ]
    for n, (src, dst, target) in enumerate(items):
        w_i.append(message(10 + n, is_if, is_if, src, dst, target))

    cross_corners = []
    for part, (cond, dst, first) in enumerate(((is_sta, RC_HI, 0), (is_rot, RC_LO, 2))):
        other = r - 1 if part == 0 else r + 1
        offs = (-10, -7) if part == 0 else (7, 10)
        got = is_rot if part == 0 else is_sta
        for e in range(2):
            cross_corners.append(
                message(
                    (4 if part == 0 else 6) + e,
                    cond,
                    got,
                    EP.at[e, pl.ds(first, 2)],
                    dst.at[e],
                    (theta(offs[e]), other),
                )
            )

    slide = slide_ref[0]
    frac = frac_ref[0]
    gain = gain_ref[0]

    def pairs(x, cell):
        width = x.shape[-1]
        pick = (lax.broadcasted_iota(jnp.int32, x.shape, x.ndim - 1) // cell) % 2 == 1
        return x + jnp.where(pick, roll(x, cell, x.ndim - 1), roll(x, width - cell, x.ndim - 1))

    gather_index = (lane % 16) * 8

    def pack(rows):
        out = None
        for q, x in enumerate(rows):
            for half in range(2):
                part = jnp.take_along_axis(x[:, 128 * half : 128 * half + 128], gather_index, axis=1)
                out = part if out is None else jnp.where(lane // 16 == 2 * q + half, part, out)
        return out

    own3 = []
    for j in range(4):
        k2 = []
        for i in range(2):
            k1 = []
            for h in range(2):
                row = OWN + 8 * j + 4 * i + 2 * h
                k1.append(0.25 * pairs(K0[row, :, wide] + K0[row + 1, :, wide], 1))
            k2.append(0.25 * pairs(k1[0] + k1[1], 2))
        own3.append(0.25 * pairs(k2[0] + k2[1], 4))
    PK[...] = pack(own3)

    RN[REACH, 0] = PK[...]
    base_t, base_n, base_x, base_b = 21, 24, 24 + SEGS, 24 + 2 * SEGS
    w_t = [
        message(base_t, always, always, PK, RN.at[REACH, 1], (theta(-1), r)),
        message(base_t + 1, always, always, PK, RN.at[REACH, 3], (theta(1), r)),
        message(base_t + 2, near, near, PK, RN.at[REACH, 2], (theta(-2), r)),
    ]

    w_n, w_x = {}, {}

    def send_plain():
        for dr in (-3, 3, -2, 2, -1, 1):
            inside_s = (r + dr >= 0) & (r + dr < NR)
            inside_r = (r - dr >= 0) & (r - dr < NR)
            seg = REACH - dr
            w_n[seg] = message(base_n + seg, inside_s, inside_r, RN.at[REACH], RN.at[seg], (t, r + dr))

    def send_across(which):
        for dr in range(-REACH, REACH + 1):
            seg = REACH - dr
            to, fro = r + dr, r - dr
            to_rot = (to < HALF) & (to >= HALF - REACH) & (r >= HALF - 1)
            to_sta = (to >= HALF) & (to < HALF + REACH) & (r <= HALF)
            got = ((r < HALF) & (r >= HALF - REACH) & (fro >= HALF - 1)) | (
                (r >= HALF) & (r < HALF + REACH) & (fro <= HALF)
            )
            off = -FROM_STATOR[0] + ((r + dr) // HALF) * (FROM_STATOR[0] - FROM_ROTOR[0])
            w_x[seg] = message(
                base_x + seg, (to_rot | to_sta) & which, got, RN.at[REACH], RX.at[seg], (theta(off), r + dr)
            )

    def third(left_pack, right_pack, q):
        return jnp.where(lane < 64, roll(left_pack, -16 * q, 1), roll(right_pack, 112 - 16 * q, 1))

    halo = pl.ds(256, 128)
    for w in w_th:
        w()
    for m in range(4):
        for arr, ref in enumerate((K0, B0)):
            for q in range(8):
                ref[OWN + 8 * m + q, :, halo] = third(RT[0, m, arr], RT[1, m, arr], q)
    for w in w_t:
        w()
    send_plain()
    send_across(inner)
    def down_k(level, low, high):
        fine_k, coarse_k = levels[level - 1]["K"], levels[level]["K"]

        def body(j):
            coarse_k[j] = 0.25 * pairs(fine_k[2 * j] + fine_k[2 * j + 1], 1 << (level - 1))

        loop_rows(low, high, body, 8)

    top = axial < 7
    low_ok, high_ok = r > 0, r < NR - 1

    def coefficients(level, seg, low, high, unroll=8):
        A = levels[level]
        rows_level = GLOBAL_ROWS >> level
        inv = 1.0 / rows_level
        cell = 1 << level
        start = {"lo": LO + 12, "own": OWN, "hi": HI - 32}[seg] >> level
        ok = {"lo": low_ok, "own": None, "hi": high_ok}[seg]

        def body(j):
            pos = r * (ROWS >> level) + j - start
            posf = pos.astype(F32)
            hu = 0.5 * (1.0 + (posf + 1.0) * inv) * jnp.where(pos == rows_level // 2 - 1, gain, 1.0)
            hl = 0.5 * (1.0 + posf * inv) * jnp.where(pos == rows_level // 2, gain, 1.0)
            rc = 1.0 + (posf + 0.5) * inv
            hc1 = 0.5 / jnp.full((8, 128), rc, F32)
            hz1 = jnp.where(top, 0.5 * rc, 0.0)
            hc = jnp.concatenate([hc1] * 3, axis=1)
            hz = jnp.concatenate([hz1] * 3, axis=1)
            k = A["K"][j]
            ce = (k + roll(k, -cell, 1)) * hc
            cw = roll(ce, cell, 1)
            cu = (k + A["K"][j + 1]) * hu
            cl = (k + A["K"][j - 1]) * hl
            cz = (k + roll(k, -1, 0)) * hz
            cd = roll(cz, 1, 0)
            diag = cu + cl + ce + cw + cz + cd
            wd = 0.8 / diag
            if ok is not None:
                wd = jnp.where(ok, wd, 0.0)
            A["CU"][j], A["CL"][j], A["CE"][j], A["CW"][j], A["CZ"][j], A["CD"][j] = cu, cl, ce, cw, cz, cd
            A["WD"][j] = wd
            if level == 0:
                A["U"][j] = wd * A["B"][j]
                if seg == "own":
                    DG[j - OWN] = diag

        loop_rows(low, high, body, unroll)

    fine = slide - NT * 256 // 2

    def weights(active, shift, count):
        out = []
        for i in range(count):
            w = jnp.where(shift == i, 1.0 - frac, 0.0) + jnp.where(shift == i - 1, frac, 0.0)
            out.append(jnp.where(active, w, 1.0 if i == 0 else 0.0))
        return out

    shifts = (fine % 4, (fine // 2) % 2, 0 * fine)
    up_w = [weights(is_rot, shifts[level], (5, 3, 2)[level]) for level in range(3)]
    low_w = [weights(is_sta, shifts[level], (5, 3, 2)[level]) for level in range(3)]

    def mix(x, w, step):
        out = w[0] * x
        for i in range(1, len(w)):
            out = out + w[i] * roll(x, i * step, x.ndim - 1)
        return out

    def ghosts(field, level):
        cell = 1 << level
        lo_end, own, own_end, hi = LO + 12 >> level, OWN >> level, GOU >> level, HI >> level
        field[own_end] = mix(field[hi], up_w[level], -cell)
        field[hi - 1] = mix(field[own_end - 1], up_w[level], cell)
        field[lo_end] = mix(field[own], low_w[level], -cell)
        field[own - 1] = mix(field[lo_end - 1], low_w[level], cell)

    def neighbours(level, field, j):
        A = levels[level]
        cell = 1 << level
        v = field[j]
        return (
            A["CU"][j] * field[j + 1]
            + A["CL"][j] * field[j - 1]
            + A["CE"][j] * roll(v, -cell, 1)
            + A["CW"][j] * roll(v, cell, 1)
            + A["CZ"][j] * roll(v, -1, 0)
            + A["CD"][j] * roll(v, 1, 0)
        )

    def first(level, low, high):
        A = levels[level]

        def body(j):
            A["U"][j] = A["WD"][j] * A["B"][j]

        loop_rows(low, high, body, 8)

    def restrict(level, low, high):
        A = levels[level]

        def body(j):
            x = 0.2 * (A["B"][2 * j] + A["B"][2 * j + 1])
            x = x + (neighbours(level, A["U"], 2 * j) + neighbours(level, A["U"], 2 * j + 1))
            levels[level + 1]["B"][j] = pairs(x, 1 << level)

        loop_rows(low, high, body, 7)

    def restrict3(rows):
        A = levels[2]
        for j in rows:
            x = None
            for i in range(2):
                row = (OWN >> 2) + 2 * j + i
                y = 0.2 * A["B"][row] + neighbours(2, A["U"], row)
                x = y if x is None else x + y
            B3S[j] = pairs(x, 4)

    own0, own1, own2 = OWN, OWN >> 1, OWN >> 2
    lo0, lo1, lo2 = LO + 12, LO + 12 >> 1, LO + 12 >> 2
    hi0, hi1, hi2 = HI, HI >> 1, HI >> 2

    down_k(1, own1, own1 + 16)
    down_k(2, own2, own2 + 8)
    coefficients(0, "own", own0 + 1, own0 + 31)
    coefficients(1, "own", own1 + 1, own1 + 15)
    coefficients(2, "own", own2 + 1, own2 + 7)
    restrict(0, own1 + 1, own1 + 15)
    first(1, own1 + 1, own1 + 15)
    restrict(1, own2 + 1, own2 + 7)
    first(2, own2 + 1, own2 + 7)
    restrict3((1, 2))

    for w in w_k:
        w()
    for w in cross_corners:
        w()
    for w in w_b:
        w()
    for j in range(12):
        for arr, ref in enumerate((K0, B0)):
            m, q = divmod(j, 8)
            ref[HI + j, :, halo] = third(RC_HI[0, m, arr], RC_HI[1, m, arr], q)
            m, q = divmod(4 + j, 8)
            ref[LO + j, :, halo] = third(RC_LO[0, m, arr], RC_LO[1, m, arr], q)

    d4 = (fine // 4) * 4
    q4 = d4 % 128
    far = d4 >= 128
    back4 = lax.rem(128 - q4, 128)

    for w in w_i:
        w()
    send_across(is_if)

    def window(tiles, sign):
        if sign > 0:
            tiles = [jnp.where(far, tiles[(i + 1) % 5], tiles[i]) for i in range(5)]
            turned = [pltpu.roll(x, back4, 1) for x in tiles]
            keep = lane < 128 - q4
            out = [jnp.where(keep, turned[i], turned[(i + 1) % 5]) for i in (0, 1, 2, 4)]
        else:
            tiles = [jnp.where(far, tiles[(i + 4) % 5], tiles[i]) for i in range(5)]
            turned = [pltpu.roll(x, q4, 1) for x in tiles]
            keep = lane >= q4
            out = [jnp.where(keep, turned[i], turned[(i + 4) % 5]) for i in (0, 1, 2, 4)]
        return out[0], out[1], jnp.where(lane < 64, out[2], out[3])

    def fill(sign, dst_k, dst_ghost):
        for j in range(28):
            if j < 24:
                ref, row = ((K0, B0)[j // 12], dst_k + j % 12)
                edge = ref[row, :, halo]
            else:
                ref, row = (K0, dst_ghost + j - 24)
                edge = third(RGH[0], RGH[1], j - 24 + (4 if sign > 0 else 0))
            a = [WC1[j, :, pl.ds(0, 128)], WC1[j, :, pl.ds(128, 128)]]
            b = [WC2[j, :, pl.ds(0, 128)], WC2[j, :, pl.ds(128, 128)]]
            tiles = a + b + [edge] if sign > 0 else a + [edge] + b
            for i, x in enumerate(window(tiles, sign)):
                ref[row, :, pl.ds(128 * i, 128)] = x

    @pl.when(is_rot)
    def _():
        fill(1, HI, GHD)
        for j in range(4):
            K0[GOU + j, :, halo] = third(RG[0], RG[1], j)

    @pl.when(is_sta)
    def _():
        fill(-1, LO, GLU)
        for j in range(4):
            K0[GOD + j, :, halo] = third(RG[0], RG[1], 4 + j)

    @pl.when(jnp.logical_not(is_rot))
    def _():
        K0[pl.ds(GOU, 4)] = K0[pl.ds(HI, 4)]
        K0[pl.ds(GHD, 4)] = K0[pl.ds(OWN + 28, 4)]

    @pl.when(jnp.logical_not(is_sta))
    def _():
        K0[pl.ds(GLU, 4)] = K0[pl.ds(OWN, 4)]
        K0[pl.ds(GOD, 4)] = K0[pl.ds(LO + 8, 4)]

    for level, low, high, end in ((1, own1, own1 + 16, PHYS >> 1), (2, own2, own2 + 8, PHYS >> 2)):
        down_k(level, 0, low)
        down_k(level, high, end)
    coefficients(0, "own", own0, own0 + 1)
    coefficients(0, "own", own0 + 31, own0 + 32)
    coefficients(0, "lo", lo0 - 11, lo0)
    coefficients(0, "hi", hi0, hi0 + 11)
    coefficients(1, "own", own1, own1 + 1)
    coefficients(1, "own", own1 + 15, own1 + 16)
    coefficients(1, "lo", lo1 - 5, lo1)
    coefficients(1, "hi", hi1, hi1 + 5)
    coefficients(2, "own", own2, own2 + 1)
    coefficients(2, "own", own2 + 7, own2 + 8)
    coefficients(2, "lo", lo2 - 2, lo2)
    coefficients(2, "hi", hi2, hi2 + 2)
    ghosts(levels[0]["U"], 0)
    for low, high in ((lo1 - 5, lo1), (own1, own1 + 1), (own1 + 15, own1 + 16), (hi1, hi1 + 5)):
        restrict(0, low, high)
    for low, high in ((lo1 - 5, lo1), (own1, own1 + 1), (own1 + 15, own1 + 16), (hi1, hi1 + 5)):
        first(1, low, high)
    ghosts(levels[1]["U"], 1)
    for low, high in ((lo2 - 2, lo2), (own2, own2 + 1), (own2 + 7, own2 + 8), (hi2, hi2 + 2)):
        restrict(1, low, high)
    for low, high in ((lo2 - 2, lo2), (own2, own2 + 1), (own2 + 7, own2 + 8), (hi2, hi2 + 2)):
        first(2, low, high)
    ghosts(levels[2]["U"], 2)
    restrict3((0, 3))

    PB[...] = pack([B3S[j, :, wide] for j in range(4)])
    RB[REACH, 0] = PB[...]
    w_p, sent = [], []
    for dr in (-3, 3, -2, 2, -1, 1, 0):
        inside_s = (r + dr >= 0) & (r + dr < NR)
        inside_r = (r - dr >= 0) & (r - dr < NR)
        seg = REACH - dr
        same_s = (r + dr) // HALF == side
        same_r = (r - dr) // HALF == side
        to_side = (r + dr) // HALF
        near_ways = [(slot, off) for slot, off in NORMAL.items() if dr or off]
        ways = [(inside_s & same_s, inside_r & same_r, [(slot, theta(-off)) for slot, off in near_ways])]
        if dr:
            across = [
                (slot, theta(-FROM_STATOR[slot] + to_side * (FROM_STATOR[slot] - FROM_ROTOR[slot])))
                for slot in range(SLOTS)
            ]
            ways.append((inside_s & jnp.logical_not(same_s), inside_r & jnp.logical_not(same_r), across))
        for send, recv, targets in ways:

            def copy_of(src, dst, target, seg=seg, dr=dr):
                return pltpu.make_async_remote_copy(
                    src_ref=src,
                    dst_ref=dst,
                    send_sem=sem_s.at[base_b + seg],
                    recv_sem=sem_r.at[base_b + seg],
                    device_id=(target, r + dr),
                    device_id_type=MESH,
                )

            copies = [copy_of(PB, RB.at[seg, slot], target) for slot, target in targets]

            @pl.when(send)
            def _(copies=copies):
                for copy in copies:
                    copy.start()

            whole = RB.at[seg, pl.ds(0, len(targets))]
            both = copy_of(whole, whole, targets[0][1])
            w_p.append((recv, both))
            sent.append((send, both))
    for send, copy in messages:
        pl.when(send)(copy.wait_send)

    count3 = 4 * SEGS
    d3 = (fine // 16) * 2
    sgn_x = jnp.where(side == 0, lax.rem(128 - d3, 128), lax.rem(d3 + 96, 128))

    def unpack(ref):
        tiles = [ref[:, o] for o in range(SLOTS)]
        lane7 = lax.broadcasted_iota(jnp.int32, (SEGS, 8, 128), 2) // 32
        rows = []
        for q in range(4):
            out = roll(tiles[0], -32 * q, 2)
            for o in range(1, SLOTS):
                out = jnp.where(lane7 == o, roll(tiles[o], 32 * (o - q), 2), out)
            rows.append(out)
        return jnp.stack(rows, axis=1).reshape(count3, 8, 128)

    def turn(x):
        return pltpu.roll(x, sgn_x, 2)

    for w in list(w_x.values()) + list(w_n.values()):
        w()
    kn = unpack(RN)
    kx = turn(unpack(RX))

    far_off = jnp.where(near, side, 1 << 20)

    def coefficients_patch(kn, kx, rows, level, cell):
        rows_level = GLOBAL_ROWS >> level
        inv = 1.0 / rows_level
        pos = (r - REACH) * (ROWS >> level) + lax.broadcasted_iota(jnp.int32, (rows, 8, 128), 0)
        ok = (pos >= 0) & (pos < rows_level)
        beyond = (pos - rows_level // 2) * (1 - 2 * side) >= far_off
        posf = pos.astype(F32)
        hu = 0.5 * (1.0 + (posf + 1.0) * inv) * jnp.where(pos == rows_level // 2 - 1, gain, 1.0)
        hl = 0.5 * (1.0 + posf * inv) * jnp.where(pos == rows_level // 2, gain, 1.0)
        rc = 1.0 + (posf + 0.5) * inv
        hc = 0.5 / rc
        hz = jnp.where(lax.broadcasted_iota(jnp.int32, (rows, 8, 128), 1) < 7, 0.5 * rc, 0.0)
        k = jnp.where(beyond, kx, kn)
        ku = jnp.where(beyond, jnp.concatenate([kx[1:], kx[:1]], 0), jnp.concatenate([kn[1:], kn[:1]], 0))
        kd = jnp.where(beyond, jnp.concatenate([kx[-1:], kx[:-1]], 0), jnp.concatenate([kn[-1:], kn[:-1]], 0))
        ku = jnp.where(pos == rows_level - 1, 0.0, ku)
        kd = jnp.where(pos == 0, 0.0, kd)
        ce = (k + roll(k, -cell, 2)) * hc
        cw = roll(ce, cell, 2)
        cu = (k + ku) * hu
        cl = (k + kd) * hl
        cz = (k + roll(k, -1, 1)) * hz
        cd = roll(cz, 1, 1)
        wd = jnp.where(ok, 0.8 / (cu + cl + ce + cw + cz + cd), 0.0)
        return (cu, cl, ce, cw, cz, cd, wd, beyond)

    def coarse_k(x):
        y = x.reshape(x.shape[0] // 2, 2, 8, 128)
        return 0.25 * pairs(y[:, 0] + y[:, 1], 1)

    C3 = coefficients_patch(kn, kx, count3, 3, 1)
    C4 = coefficients_patch(coarse_k(kn), coarse_k(kx), count3 // 2, 4, 2)

    odd = (fine // 8) % 2
    w3 = weights(r >= 0, odd, 3)
    w4 = weights(r >= 0, 0 * odd, 2)

    def neighbours_patch(C, v, step, w, cell):
        n = v.shape[0]
        edge = lax.rem(HALF - r + REACH + 4 * SEGS, SEGS) * step
        VP[pl.ds(0, n)] = v
        over = mix(VP[edge], w, -cell)
        under = mix(VP[lax.rem(edge + n - 1, n)], w, cell)
        row = lax.broadcasted_iota(jnp.int32, v.shape, 0)
        vu = jnp.concatenate([v[1:], v[:1]], 0)
        vd = jnp.concatenate([v[-1:], v[:-1]], 0)
        mark = jnp.where(near, edge, -8)
        vu = jnp.where(row == mark - 1, over[None], vu)
        vd = jnp.where(row == mark, under[None], vd)
        return (
            C[0] * vu
            + C[1] * vd
            + C[2] * roll(v, -cell, 2)
            + C[3] * roll(v, cell, 2)
            + C[4] * roll(v, -1, 1)
            + C[5] * roll(v, 1, 1)
        )

    for recv, both in w_p:
        pl.when(recv)(both.wait_recv)
    b3 = unpack(RB)
    b3 = jnp.where(C3[7], turn(b3), b3)
    u3 = C3[6] * b3
    x = 0.2 * b3 + neighbours_patch(C3, u3, 4, w3, 1)
    x = x.reshape(count3 // 2, 2, 8, 128)
    b4 = pairs(x[:, 0] + x[:, 1], 1)
    v4 = C4[6] * b4
    for _ in range(3):
        v4 = 0.2 * v4 + C4[6] * (b4 + neighbours_patch(C4, v4, 2, w4, 2))
    up4 = jnp.broadcast_to(v4[:, None], (count3 // 2, 2, 8, 128)).reshape(count3, 8, 128)
    v3 = u3 + up4
    e3 = 0.2 * v3 + C3[6] * (b3 + neighbours_patch(C3, v3, 4, w3, 1))

    delta = (fine // 4) % 4 * 4
    first_row = 4 * REACH - 1
    for j in range(6):
        if j == 0:
            shift = jnp.where(is_sta, -delta, 0)
        elif j == 5:
            shift = jnp.where(is_rot, delta, 0)
        else:
            shift = 0
        for i in range(3):
            signed = lane + 128 * i
            if i == 2:
                signed = jnp.where(lane < 64, signed, signed - LANES)
            index = ((signed + shift + 1024) // 8) % 128
            E3S[j, :, pl.ds(128 * i, 128)] = jnp.take_along_axis(e3[first_row + j], index, axis=1)

    for level in (2, 1, 0):
        A = levels[level]
        low, own, hi = LO + 12 >> level, OWN >> level, HI >> level
        rows = ROWS >> level
        if level == 2:
            A["U"][low - 2] = A["U"][low - 2] + E3S[0]
            A["U"][low - 1] = A["U"][low - 1] + E3S[0]
            for j in range(rows):
                A["U"][own + j] = A["U"][own + j] + E3S[1 + j // 2]
            A["U"][hi] = A["U"][hi] + E3S[5]
            A["U"][hi + 1] = A["U"][hi + 1] + E3S[5]
        else:
            E = levels[level + 1]["E"]

            def add(j, A=A, E=E):
                e = E[j]
                A["U"][2 * j] = A["U"][2 * j] + e
                A["U"][2 * j + 1] = A["U"][2 * j + 1] + e

            add((low >> 1) - 1)
            loop_rows(own >> 1, (own + rows) >> 1, add, 4)
            add(hi >> 1)
        ghosts(A["U"], level)

        def smooth(j, A=A, level=level):
            A["E"][j] = 0.2 * A["U"][j] + A["WD"][j] * (A["B"][j] + neighbours(level, A["U"], j))

        smooth(low - 1)
        loop_rows(own, own + rows, smooth, 16)
        smooth(hi)

    ghosts(levels[0]["E"], 0)

    def finish(j):
        E = levels[0]["E"]
        p = E[OWN + j]
        A = levels[0]
        o = OWN + j
        east, west = roll(p, -1, 1)[:, :256], roll(p, 1, 1)[:, :256]
        v = p[:, :256]
        out = (
            B0[o, :, wide]
            - DG[j, :, wide] * v
            + A["CU"][o, :, wide] * E[o + 1, :, wide]
            + A["CL"][o, :, wide] * E[o - 1, :, wide]
            + A["CE"][o, :, wide] * east
            + A["CW"][o, :, wide] * west
            + A["CZ"][o, :, wide] * roll(v, -1, 0)
            + A["CD"][o, :, wide] * roll(v, 1, 0)
        )
        for half in range(2):
            place = pl.ds(tile_row(j, half), 8, stride=2 * ROWS)
            p_ref[place, :] = p[:, 128 * half : 128 * half + 128]
            res_ref[place, :] = out[:, 128 * half : 128 * half + 128]

    loop_rows(0, ROWS, finish, 32)

    for send, both in sent:
        pl.when(send)(both.wait_send)


def on_device(source, conductance, slide, fraction, gain):
    nz, rows, columns = source.shape
    scratch = []
    for level in range(3):
        scratch += [pltpu.VMEM((PHYS >> level, nz, LANES), F32)] * len(PER_LEVEL)
    tile = (8, 128)
    scratch += [
        pltpu.VMEM((ROWS, nz, LANES), F32),
        pltpu.VMEM((4, nz, LANES), F32),
        pltpu.VMEM((2, 4, 2) + tile, F32),
        pltpu.VMEM((2, 4, 2) + tile, F32),
        pltpu.VMEM((2, 2, 2) + tile, F32),
        pltpu.VMEM((2, 2, 2) + tile, F32),
        pltpu.VMEM((2,) + tile, F32),
        pltpu.VMEM((2,) + tile, F32),
        pltpu.VMEM((28, nz, 256), F32),
        pltpu.VMEM((28, nz, 256), F32),
        pltpu.VMEM(tile, F32),
        pltpu.VMEM(tile, F32),
        pltpu.VMEM((SEGS, SLOTS) + tile, F32),
        pltpu.VMEM((SEGS, SLOTS) + tile, F32),
        pltpu.VMEM((SEGS, SLOTS) + tile, F32),
        pltpu.VMEM((4 * SEGS,) + tile, F32),
        pltpu.VMEM((6, nz, LANES), F32),
        pltpu.VMEM((nz * rows * columns // 128, 128), F32),
        pltpu.VMEM((nz * rows * columns // 128, 128), F32),
    ]
    sems = 24 + 3 * SEGS
    scratch += [pltpu.SemaphoreType.DMA((n,)) for n in (sems, sems, 2)]
    vmem = pl.BlockSpec(memory_space=pltpu.VMEM)
    smem = pl.BlockSpec(memory_space=pltpu.SMEM)
    hbm = pl.BlockSpec(memory_space=pltpu.HBM)
    flat = jax.ShapeDtypeStruct((nz * rows * columns // 128, 128), F32)
    large = [pltpu.with_memory_space_constraint(to_tiles(x), pltpu.HBM) for x in (source, conductance)]
    operands = (slide, fraction, gain, *large)
    pressure, residual = pl.pallas_call(
        kernel,
        out_shape=(flat, flat),
        in_specs=[smem] * 3 + [hbm] * 2,
        out_specs=(vmem, vmem),
        scratch_shapes=scratch,
        compiler_params=pltpu.CompilerParams(
            collective_id=0, has_side_effects=True, vmem_limit_bytes=48 * 1024 * 1024
        ),
    )(*operands)
    return from_tiles(pressure, source.shape), from_tiles(residual, source.shape)


def solution(mesh):
    spec = P(None, "rad", "theta")
    return jax.shard_map(
        on_device, mesh=mesh, in_specs=(spec, spec, P(), P(), P()), out_specs=(spec, spec), check_vma=False
    )
```
